32 devices in a mesh: dp: 8 (over y, x, core), ctx: 4 (over z).
Axes of the slice: x: 2, y: 2, z: 4, core: 2. Of those that a mesh axis runs over, the one named last changes fastest.
Arguments:
- hidden: bfloat16 [8, 512, 3584], P('dp', 'ctx'), may hold values from -6 to 6
- norm_gain: bfloat16 [3584], replicated, may hold values from 0.099609375 to 1.8984375
- w_query: bfloat16 [3584, 2048], P('dp'), may hold values from -0.09375 to 0.09375
- w_key: bfloat16 [3584, 512], P('dp'), may hold values from -0.09375 to 0.09375
- w_value: bfloat16 [3584, 512], P('dp'), may hold values from -0.09375 to 0.09375
- bias_query: bfloat16 [2048], replicated, may hold values from -4 to 4
- bias_key: bfloat16 [512], replicated, may hold values from -4 to 4
- bias_value: bfloat16 [512], replicated, may hold values from -4 to 4
- kv_blocks: int32 [16, 4, 4], P('ctx'), may hold values from 0 to 3, as said below
- block_counts: int32 [16, 4], P('ctx'), may hold values from 1 to 4, as said below
Outputs:
- attended: bfloat16 [8, 512, 2048], P('dp', 'ctx')
The draws below stay inside these ranges and needn't reach their ends.
Inputs may be any that keep to these rules, and one draw needn't show every extreme that they name: Entry 0 of kv_blocks[h, b] is b itself; entries 1 to block_counts[h, b] - 1 are distinct blocks below b; later entries are valid block numbers that are not used. block_counts[h, b] is at most b + 1, and the last query block of every head has 4.
All inputs are finite; a program needn't handle non-finite values.
Results may differ from the reference program's by a relative error of at most 0.0053.
Values may be sent and summed in bfloat16 or wider, within the bound.
A program may use at most 64 MiB of HBM per device.

```python
import jax
import jax.numpy as jnp
from jax import lax

D = 3584
KVH = 4
HEAD = 128
QHEADS = 16
BLOCK = 128
MAXB = 4
SEQ = 512
QBLOCKS = 4
DOCS = 8


def mask_tables(key):
    level_key, slot_key, count_key = jax.random.split(jax.random.fold_in(key, 7), 3)
    levels = jax.random.randint(level_key, (QHEADS, 1), 0, MAXB)
    raw_counts = jax.random.randint(count_key, (QHEADS, QBLOCKS), 0, MAXB)
    rows_idx = jnp.arange(QBLOCKS)
    counts = jnp.minimum(1 + jnp.minimum(raw_counts, levels), rows_idx[None, :] + 1)
    counts = jnp.where(rows_idx[None, :] == QBLOCKS - 1, MAXB, counts)
    noise = jax.random.randint(slot_key, (QHEADS, QBLOCKS, QBLOCKS), 0, 1 << 20)
    cols_idx = jnp.arange(QBLOCKS)
    below = cols_idx[None, None, :] < rows_idx[None, :, None]
    scored = jnp.where(below, noise * QBLOCKS + cols_idx[None, None, :], (1 << 20) * QBLOCKS + cols_idx[None, None, :])
    order = jnp.argsort(scored, axis=-1, stable=True)[..., :MAXB - 1]
    usable = jnp.arange(MAXB - 1)[None, :] < rows_idx[:, None]
    others = jnp.where(usable[None, :, :], order, rows_idx[None, :, None])
    diagonal = jnp.broadcast_to(rows_idx[None, :, None], (QHEADS, QBLOCKS, 1))
    blocks = jnp.concatenate([diagonal, others], axis=-1)
    return (blocks.astype(jnp.int32), counts.astype(jnp.int32))


def draw_kv_blocks(key, part):
    return mask_tables(key)[0]


def draw_block_counts(key, part):
    return mask_tables(key)[1]


def level_of(own_key, dims, cuts, smallest, top_value):
    loudness = 1.0
    for dim, shards_of in cuts:
        steps = jax.random.uniform(jax.random.fold_in(jax.random.fold_in(own_key, 6), dim), (shards_of,), jnp.float32, smallest / len(cuts), top_value / len(cuts))
        loudness = loudness * jnp.repeat(jnp.exp(steps), dims[dim] // shards_of).reshape((-1,) + (1,) * (len(dims) - 1 - dim))
    return loudness


def bell_draw(stream_key, dims, deviation, reach, cuts=(), kind=jnp.bfloat16):
    gain = level_of(stream_key, dims, cuts, -0.22, 0.18) if cuts else 1.0
    result = jax.random.normal(stream_key, dims, jnp.float32) * deviation * gain
    return jnp.minimum(jnp.maximum(result, -reach), reach).astype(kind)


def setup_inputs(seed: int = 0) -> dict:
    key_of = jax.random.split(jax.random.key(seed), 11)
    hidden = bell_draw(key_of[0], (DOCS, SEQ, D), 1.0, 6.0, ((0, 8), (1, 4)))
    norm_gain = jnp.clip(1.0 + 0.18 * jax.random.normal(key_of[1], (D,), jnp.float32), 0.099609375, 1.8984375).astype(jnp.bfloat16)
    w_query = bell_draw(key_of[2], (D, QHEADS * HEAD), D ** -0.5, 0.09375, ((0, 8),))
    w_key = bell_draw(key_of[3], (D, KVH * HEAD), D ** -0.5, 0.09375, ((0, 8),))
    w_value = bell_draw(key_of[4], (D, KVH * HEAD), D ** -0.5, 0.09375, ((0, 8),))
    bias_query = bell_draw(key_of[5], (QHEADS * HEAD,), 1.0, 4.0)
    bias_key = bell_draw(key_of[6], (KVH * HEAD,), 1.0, 4.0)
    bias_value = bell_draw(key_of[7], (KVH * HEAD,), 1.0, 4.0)
    kv_blocks = draw_kv_blocks(jax.random.fold_in(key_of[10], 71), 0)
    block_counts = draw_block_counts(jax.random.fold_in(key_of[10], 71), 0)
    return {"hidden": hidden, "norm_gain": norm_gain, "w_query": w_query, "w_key": w_key, "w_value": w_value, "bias_query": bias_query, "bias_key": bias_key, "bias_value": bias_value, "kv_blocks": kv_blocks, "block_counts": block_counts}


EPSILON = 1e-06
THETA = 1000000.0

def rms_norm(tokens, norm_gain):
    floats = tokens.astype(jnp.float32)
    meansq = lax.optimization_barrier(jnp.mean(floats * floats, axis=-1, keepdims=True))
    return (floats * lax.rsqrt(meansq + EPSILON) * norm_gain.astype(jnp.float32)).astype(jnp.bfloat16)

def rotary(heads_in, position):
    half_size = heads_in.shape[-1] // 2
    exponent = jnp.arange(half_size, dtype=jnp.float32) * (2.0 / heads_in.shape[-1])
    inverse = jnp.power(jnp.float32(THETA), -exponent)
    angles = position[:, None] * inverse[None, :]
    cosine = jnp.cos(angles)[:, None, :]
    sine = jnp.sin(angles)[:, None, :]
    first = heads_in[..., :half_size]
    second = heads_in[..., half_size:]
    return jnp.concatenate([first * cosine - second * sine, second * cosine + first * sine], axis=-1)

def head_projection(normed, weight, bias, heads, position, rotate_it):
    summed = jnp.dot(normed, weight, preferred_element_type=jnp.float32) + bias.astype(jnp.float32)
    shaped = summed.reshape(summed.shape[0], heads, HEAD)
    if rotate_it:
        shaped = rotary(shaped, position)
    return shaped.astype(jnp.bfloat16)

def sparse_head(queries, key_rows, value_rows, blocks, counts):
    nblocks = queries.shape[0] // BLOCK
    query_tiles = queries.reshape(nblocks, BLOCK, HEAD)
    key_tiles = key_rows.reshape(nblocks, BLOCK, HEAD)[blocks].reshape(nblocks, MAXB * BLOCK, HEAD)
    value_tiles = value_rows.reshape(nblocks, BLOCK, HEAD)[blocks].reshape(nblocks, MAXB * BLOCK, HEAD)
    scores = jnp.einsum('qih,qjh->qij', query_tiles.astype(jnp.float32), key_tiles.astype(jnp.float32)) * HEAD ** (-0.5)
    column = jnp.arange(MAXB * BLOCK)
    slot_of = column // BLOCK
    inside = column % BLOCK
    row_pos = jnp.arange(BLOCK)
    allowed = (slot_of[None, None, :] < counts[:, None, None]) & ((slot_of[None, None, :] > 0) | (inside[None, None, :] <= row_pos[None, :, None]))
    expo = jnp.where(allowed, jnp.exp(scores), jnp.float32(0.0))
    totals = lax.optimization_barrier(jnp.sum(expo, axis=-1))
    probs = expo.astype(jnp.bfloat16)
    mixed = jnp.einsum('qij,qjh->qih', probs.astype(jnp.float32), value_tiles.astype(jnp.float32)) / totals[..., None]
    return mixed.astype(jnp.bfloat16).reshape(nblocks * BLOCK, HEAD)

def reference(hidden, norm_gain, w_query, w_key, w_value, bias_query, bias_key, bias_value, kv_blocks, block_counts):
    group = QHEADS // KVH
    position = jnp.arange(SEQ, dtype=jnp.float32)

    def one_head(packed):
        return sparse_head(packed[0], packed[1], packed[2], packed[3], packed[4])

    def one_document(tokens):
        normed = rms_norm(tokens, norm_gain)
        queries = head_projection(normed, w_query, bias_query, QHEADS, position, True)
        key_rows = jnp.repeat(head_projection(normed, w_key, bias_key, KVH, position, True), group, axis=1)
        value_rows = jnp.repeat(head_projection(normed, w_value, bias_value, KVH, position, False), group, axis=1)
        mixed = lax.map(one_head, (queries.transpose(1, 0, 2), key_rows.transpose(1, 0, 2), value_rows.transpose(1, 0, 2), kv_blocks, block_counts))
        return mixed.transpose(1, 0, 2).reshape(SEQ, QHEADS * HEAD)
    return lax.map(one_document, hidden)
```

```python
import jax
import jax.numpy as jnp
from jax import lax
from jax.sharding import PartitionSpec as P

KVH = 4
HEAD = 128
QHEADS = 16
BLOCK = 128
MAXB = 4


EPSILON = 1e-06
THETA = 1000000.0


def rms_norm(tokens, norm_gain):
    floats = tokens.astype(jnp.float32)
    meansq = jnp.mean(floats * floats, axis=-1, keepdims=True)
    return (floats * lax.rsqrt(meansq + EPSILON) * norm_gain.astype(jnp.float32)).astype(
        jnp.bfloat16
    )


def rotary(heads_in, position):
    half_size = heads_in.shape[-1] // 2
    exponent = jnp.arange(half_size, dtype=jnp.float32) * (2.0 / heads_in.shape[-1])
    inverse = jnp.power(jnp.float32(THETA), -exponent)
    angles = position[:, None] * inverse[None, :]
    cosine = jnp.cos(angles)[:, None, :]
    sine = jnp.sin(angles)[:, None, :]
    first = heads_in[..., :half_size]
    second = heads_in[..., half_size:]
    return jnp.concatenate(
        [first * cosine - second * sine, second * cosine + first * sine], axis=-1
    )


def finish_heads(summed, bias, heads, position, rotate_it):
    shaped = (summed + bias.astype(jnp.float32)).reshape(summed.shape[0], heads, HEAD)
    if rotate_it:
        shaped = rotary(shaped, position)
    return shaped.astype(jnp.bfloat16)


def fold_rows(source, pieces):
    return tuple((jnp.dot(source, piece, preferred_element_type=jnp.float32) for piece in pieces))


def sparse_head(queries, key_rows, value_rows, blocks, counts):
    nblocks = queries.shape[0] // BLOCK
    query_tiles = queries.reshape(nblocks, BLOCK, HEAD)
    key_tiles = key_rows.reshape(nblocks, BLOCK, HEAD)[blocks].reshape(nblocks, MAXB * BLOCK, HEAD)
    value_tiles = value_rows.reshape(nblocks, BLOCK, HEAD)[blocks].reshape(
        nblocks, MAXB * BLOCK, HEAD
    )
    scores = jnp.einsum(
        "qih,qjh->qij", query_tiles, key_tiles, preferred_element_type=jnp.float32
    ) * HEAD ** (-0.5)
    column = jnp.arange(MAXB * BLOCK)
    slot_of = column // BLOCK
    inside = column % BLOCK
    row_pos = jnp.arange(BLOCK)
    allowed = (slot_of[None, None, :] < counts[:, None, None]) & (
        (slot_of[None, None, :] > 0) | (inside[None, None, :] <= row_pos[None, :, None])
    )
    expo = jnp.where(allowed, jnp.exp(scores), jnp.float32(0.0))
    totals = jnp.sum(expo, axis=-1)
    probs = expo.astype(jnp.bfloat16)
    mixed = (
        jnp.einsum("qij,qjh->qih", probs, value_tiles, preferred_element_type=jnp.float32)
        / totals[..., None]
    )
    return mixed.astype(jnp.bfloat16).reshape(nblocks * BLOCK, HEAD)


def one_head(packed):
    return sparse_head(packed[0], packed[1], packed[2], packed[3], packed[4])


def body(
    hidden,
    norm_gain,
    w_query,
    w_key,
    w_value,
    bias_query,
    bias_key,
    bias_value,
    kv_blocks,
    block_counts,
):
    groups = lax.axis_size("ctx")
    device = lax.axis_index("ctx")
    tokens = hidden[0]
    local_rows = tokens.shape[0]
    seq_len = local_rows * groups
    heads_here = QHEADS // groups
    kv_here = KVH // groups
    width_query = heads_here * HEAD
    width_pair = kv_here * HEAD
    normed = rms_norm(tokens, norm_gain)
    parts = lax.axis_size("dp")
    depth = w_query.shape[0]
    gathered = lax.all_to_all(
        normed.reshape(local_rows, parts, depth), "dp", split_axis=1, concat_axis=0, tiled=True
    ).reshape(parts * local_rows, depth)
    weights = jnp.concatenate([w_key, w_value, w_query], axis=1)
    partial = jnp.dot(gathered, weights, preferred_element_type=jnp.float32).astype(jnp.bfloat16)
    summed = lax.psum_scatter(partial, "dp", scatter_dimension=0, tiled=True).astype(jnp.float32)
    width = KVH * HEAD
    sum_key, sum_value, sum_query = (
        summed[:, :width],
        summed[:, width : 2 * width],
        summed[:, 2 * width :],
    )
    position = (device * local_rows + jnp.arange(local_rows, dtype=jnp.int32)).astype(jnp.float32)
    queries = finish_heads(sum_query, bias_query, QHEADS, position, True)
    key_rows = finish_heads(sum_key, bias_key, KVH, position, True)
    value_rows = finish_heads(sum_value, bias_value, KVH, position, False)
    query_send = queries.reshape(local_rows, groups, width_query)
    pair_send = jnp.concatenate([key_rows, value_rows], axis=2)
    query_got, pair_got = (
        lax.all_to_all(query_send, "ctx", split_axis=1, concat_axis=0, tiled=True),
        lax.all_to_all(pair_send, "ctx", split_axis=1, concat_axis=0, tiled=True),
    )
    queries = query_got.reshape(seq_len, heads_here, HEAD)
    key_rows = pair_got[:, 0, :width_pair].reshape(seq_len, kv_here, HEAD)
    value_rows = pair_got[:, 0, width_pair:].reshape(seq_len, kv_here, HEAD)
    group = heads_here // kv_here
    key_rows = jnp.repeat(key_rows, group, axis=1)
    value_rows = jnp.repeat(value_rows, group, axis=1)
    mixed = lax.map(
        one_head,
        (
            queries.transpose(1, 0, 2),
            key_rows.transpose(1, 0, 2),
            value_rows.transpose(1, 0, 2),
            kv_blocks,
            block_counts,
        ),
    )
    result = mixed.transpose(1, 0, 2).reshape(seq_len, 1, width_query)
    returned = lax.all_to_all(result, "ctx", split_axis=0, concat_axis=1, tiled=True)
    return returned.reshape(1, local_rows, QHEADS * HEAD)


def solution(mesh):
    placed = (
        P("dp", "ctx", None),
        P(),
        P("dp", None),
        P("dp", None),
        P("dp", None),
        P(),
        P(),
        P(),
        P("ctx", None, None),
        P("ctx", None),
    )
    return jax.shard_map(
        body, mesh=mesh, in_specs=placed, out_specs=P("dp", "ctx", None), check_vma=False
    )
```

```python
import jax
import jax.numpy as jnp
from jax import lax
from jax.experimental import pallas as pl
from jax.experimental.pallas import tpu as pltpu
from jax.sharding import PartitionSpec as P

KVH = 4
HEAD = 128
QHEADS = 16
BLOCK = 128
MAXB = 4


EPSILON = 1e-06
THETA = 1000000.0


def rms_norm(tokens, norm_gain):
    floats = tokens.astype(jnp.float32)
    meansq = jnp.mean(floats * floats, axis=-1, keepdims=True)
    return (floats * lax.rsqrt(meansq + EPSILON) * norm_gain.astype(jnp.float32)).astype(
        jnp.bfloat16
    )


def rotary(heads_in, position):
    half_size = heads_in.shape[-1] // 2
    exponent = jnp.arange(half_size, dtype=jnp.float32) * (2.0 / heads_in.shape[-1])
    inverse = jnp.power(jnp.float32(THETA), -exponent)
    angles = position[:, None] * inverse[None, :]
    cosine = jnp.cos(angles)[:, None, :]
    sine = jnp.sin(angles)[:, None, :]
    first = heads_in[..., :half_size]
    second = heads_in[..., half_size:]
    return jnp.concatenate(
        [first * cosine - second * sine, second * cosine + first * sine], axis=-1
    )


def finish_heads(summed, bias, heads, position, rotate_it):
    shaped = (summed + bias.astype(jnp.float32)).reshape(summed.shape[0], heads, HEAD)
    if rotate_it:
        shaped = rotary(shaped, position)
    return shaped.astype(jnp.bfloat16)


def fold_rows(source, pieces):
    return tuple((jnp.dot(source, piece, preferred_element_type=jnp.float32) for piece in pieces))


def sparse_head(queries, key_rows, value_rows, blocks, counts):
    nblocks = queries.shape[0] // BLOCK
    query_tiles = queries.reshape(nblocks, BLOCK, HEAD)
    key_tiles = key_rows.reshape(nblocks, BLOCK, HEAD)[blocks].reshape(nblocks, MAXB * BLOCK, HEAD)
    value_tiles = value_rows.reshape(nblocks, BLOCK, HEAD)[blocks].reshape(
        nblocks, MAXB * BLOCK, HEAD
    )
    scores = jnp.einsum(
        "qih,qjh->qij", query_tiles, key_tiles, preferred_element_type=jnp.float32
    ) * HEAD ** (-0.5)
    column = jnp.arange(MAXB * BLOCK)
    slot_of = column // BLOCK
    inside = column % BLOCK
    row_pos = jnp.arange(BLOCK)
    allowed = (slot_of[None, None, :] < counts[:, None, None]) & (
        (slot_of[None, None, :] > 0) | (inside[None, None, :] <= row_pos[None, :, None])
    )
    expo = jnp.where(allowed, jnp.exp(scores), jnp.float32(0.0))
    totals = jnp.sum(expo, axis=-1)
    probs = expo.astype(jnp.bfloat16)
    mixed = (
        jnp.einsum("qij,qjh->qih", probs, value_tiles, preferred_element_type=jnp.float32)
        / totals[..., None]
    )
    return mixed.astype(jnp.bfloat16).reshape(nblocks * BLOCK, HEAD)


def one_head(packed):
    return sparse_head(packed[0], packed[1], packed[2], packed[3], packed[4])


def body(
    hidden,
    norm_gain,
    w_query,
    w_key,
    w_value,
    bias_query,
    bias_key,
    bias_value,
    kv_blocks,
    block_counts,
):
    groups = lax.axis_size("ctx")
    device = lax.axis_index("ctx")
    tokens = hidden[0]
    local_rows = tokens.shape[0]
    seq_len = local_rows * groups
    heads_here = QHEADS // groups
    kv_here = KVH // groups
    width_query = heads_here * HEAD
    width_pair = kv_here * HEAD
    normed = rms_norm(tokens, norm_gain)
    parts = lax.axis_size("dp")
    depth = w_query.shape[0]
    gathered = lax.all_to_all(
        normed.reshape(local_rows, parts, depth), "dp", split_axis=1, concat_axis=0, tiled=True
    ).reshape(parts * local_rows, depth)
    weights = jnp.concatenate([w_key, w_value, w_query], axis=1)
    partial = jnp.dot(gathered, weights, preferred_element_type=jnp.float32).astype(jnp.bfloat16)
    summed = lax.psum_scatter(partial, "dp", scatter_dimension=0, tiled=True).astype(jnp.float32)
    width = KVH * HEAD
    sum_key, sum_value, sum_query = (
        summed[:, :width],
        summed[:, width : 2 * width],
        summed[:, 2 * width :],
    )
    position = (device * local_rows + jnp.arange(local_rows, dtype=jnp.int32)).astype(jnp.float32)
    queries = finish_heads(sum_query, bias_query, QHEADS, position, True)
    key_rows = finish_heads(sum_key, bias_key, KVH, position, True)
    value_rows = finish_heads(sum_value, bias_value, KVH, position, False)
    query_send = queries.reshape(local_rows, groups, width_query)
    pair_send = jnp.concatenate([key_rows, value_rows], axis=2)
    query_got, pair_got = (
        lax.all_to_all(query_send, "ctx", split_axis=1, concat_axis=0, tiled=True),
        lax.all_to_all(pair_send, "ctx", split_axis=1, concat_axis=0, tiled=True),
    )
    queries = query_got.reshape(seq_len, heads_here, HEAD)
    key_rows = pair_got[:, 0, :width_pair].reshape(seq_len, kv_here, HEAD)
    value_rows = pair_got[:, 0, width_pair:].reshape(seq_len, kv_here, HEAD)
    group = heads_here // kv_here
    key_rows = jnp.repeat(key_rows, group, axis=1)
    value_rows = jnp.repeat(value_rows, group, axis=1)
    mixed = lax.map(
        one_head,
        (
            queries.transpose(1, 0, 2),
            key_rows.transpose(1, 0, 2),
            value_rows.transpose(1, 0, 2),
            kv_blocks,
            block_counts,
        ),
    )
    result = mixed.transpose(1, 0, 2).reshape(seq_len, 1, width_query)
    returned = lax.all_to_all(result, "ctx", split_axis=0, concat_axis=1, tiled=True)
    return returned.reshape(1, local_rows, QHEADS * HEAD)


MESH = pl.DeviceIdType.MESH
CHUNK = 2 * HEAD
GROUP = QHEADS // KVH
PAIRS = KVH // 2


def chunk_sources(half, chunk):
    if chunk < PAIRS:
        first = pl.multiple_of((PAIRS * half + chunk) * HEAD, HEAD)
        return ((1, first, HEAD, 0), (2, first, HEAD, HEAD))
    first = half * (QHEADS // 2 * HEAD) + (chunk - PAIRS) * CHUNK
    return ((0, pl.multiple_of(first, CHUNK), CHUNK, 0),)


def fused_kernel(
    hidden,
    gain,
    w_query,
    w_key,
    w_value,
    bias,
    cosine,
    sine,
    allowed,
    out,
    normed,
    x_buf,
    w_buf,
    a1_out,
    a1_in,
    b1_out,
    b1_in,
    a2_out,
    a2_in,
    b2_out,
    b2_in,
    keep,
    own,
    kv_buf,
    q_buf,
    mask_buf,
    acc,
    tot,
    o_buf,
    o_in,
    w_loc,
    w_snd,
    w_rcv,
    x_snd,
    x_rcv,
    f_snd,
    f_rcv,
    m_snd,
    m_rcv,
    s1_snd,
    s1_rcv,
    s2_snd,
    s2_rcv,
    kv_snd,
    kv_rcv,
    o_snd,
    o_rcv,
):
    me = lax.axis_index("dp")
    z = lax.axis_index("ctx")
    tops = lax.axis_size("ctx")
    core = lax.rem(me, 2)
    xpos = lax.rem(me // 2, 2)
    ypos = me // 4
    sibling = me + 1 - 2 * core
    xn = me + 2 - 4 * xpos
    yn = me + 4 - 8 * ypos
    dn = xn + 4 - 8 * ypos
    chunks = w_buf.shape[0]
    depth = w_query.shape[0]
    width = 2 * depth
    weights = (w_query, w_key, w_value)
    sends = []

    def remote(src, dst, snd, rcv, dp, ctx):
        return pltpu.make_async_remote_copy(
            src_ref=src, dst_ref=dst, send_sem=snd, recv_sem=rcv, device_id=(dp, ctx), device_id_type=MESH
        )

    def launch(*args):
        copy = remote(*args)
        copy.start()
        sends.append(copy)

    locals_ = []
    rows = pl.ds(pl.multiple_of(core * depth, 64), depth)
    number = 0
    for chunk in range(chunks):
        for which, first, cols, place in chunk_sources(core, chunk):
            copy = pltpu.make_async_copy(
                weights[which].at[:, pl.ds(first, cols)],
                w_buf.at[chunk, rows, pl.ds(place, cols)],
                w_loc.at[number],
            )
            copy.start()
            locals_.append((chunk, copy))
            number += 1

    barrier = pltpu.get_barrier_semaphore()
    for peer in (sibling, xn, yn, dn):
        pl.semaphore_signal(barrier, inc=1, device_id=(peer, z), device_id_type=MESH)
    for step in range(1, tops):
        pl.semaphore_signal(barrier, inc=1, device_id=(me, lax.rem(z + step, tops)), device_id_type=MESH)

    floats = hidden[0].astype(jnp.float32)
    scale = lax.rsqrt(jnp.mean(floats * floats, axis=-1, keepdims=True) + EPSILON)
    pl.semaphore_wait(barrier, 4 + tops - 1)

    def norm_block(chip):
        cols = pl.ds(pl.multiple_of(chip * width, HEAD), width)
        block = hidden[0, :, cols].astype(jnp.float32)
        return (block * scale * gain[:, cols].astype(jnp.float32)).astype(jnp.bfloat16)

    relations = (dn, xn, yn)
    for index, peer in enumerate(relations):
        normed[index] = norm_block(peer // 2)
        launch(normed.at[index], x_buf.at[me], x_snd.at[index], x_rcv.at[index], peer, z)
    x_buf[me] = norm_block(me // 2)
    launch(x_buf.at[me], x_buf.at[me], f_snd.at[3], f_rcv.at[3], sibling, z)

    number = 0
    for chunk in range(chunks):
        for which, first, cols, place in chunk_sources(1 - core, chunk):
            launch(
                weights[which].at[:, pl.ds(first, cols)],
                w_buf.at[chunk, rows, pl.ds(place, cols)],
                w_snd.at[number],
                w_rcv.at[number],
                sibling,
                z,
            )
            number += 1
    for step in range(1, tops):
        peer = lax.rem(z + step, tops)
        launch(allowed.at[peer], mask_buf.at[z], m_snd.at[step - 1], m_rcv.at[step - 1], me, peer)
    mask_buf[z] = allowed[z]

    def sibling_of(device):
        return device + 1 - 2 * core

    def docs_of(index):
        peer = relations[index]
        remote(x_buf.at[peer], x_buf.at[peer], x_snd.at[index], x_rcv.at[index], peer, z).wait_recv()
        launch(x_buf.at[peer], x_buf.at[peer], f_snd.at[index], f_rcv.at[index], sibling, z)

    def forwarded(index, device):
        there = x_buf.at[sibling_of(device)]
        remote(there, there, f_snd.at[index], f_rcv.at[index], sibling, z).wait_recv()

    def wait_weights(chunk):
        other = pl.ds(pl.multiple_of((1 - core) * depth, 64), depth)
        for number, (owner, copy) in enumerate(locals_):
            if owner == chunk:
                copy.wait()
        number = 0
        for at in range(chunks):
            for _, _, cols, place in chunk_sources(core, at):
                if at == chunk:
                    there = w_buf.at[chunk, other, pl.ds(place, cols)]
                    remote(there, there, w_snd.at[number], w_rcv.at[number], sibling, z).wait_recv()
                number += 1

    def product(chunk, device):
        pair = x_buf[pl.ds(device // 2 * 2, 2)].reshape(2 * BLOCK, width)
        return jnp.dot(pair, w_buf[chunk], preferred_element_type=jnp.float32)

    def multiply(chunk):
        wait_weights(chunk)
        if chunk == 0:
            forwarded(3, me)
            docs_of(1)
            docs_of(2)
            docs_of(0)
            forwarded(1, xn)
        to_x = product(chunk, xn)
        a1_out[chunk, 0] = to_x[:BLOCK].astype(jnp.bfloat16)
        keep[chunk, 1] = to_x[BLOCK:]
        if chunk == 0:
            forwarded(2, yn)
        to_y = product(chunk, yn)
        b1_out[chunk, 0] = to_y[BLOCK:].astype(jnp.bfloat16)
        keep[chunk, 0] = to_y[:BLOCK]
        if chunk == 0:
            forwarded(0, dn)
        to_d = product(chunk, dn).astype(jnp.bfloat16)
        a1_out[chunk, 1] = to_d[:BLOCK]
        b1_out[chunk, 1] = to_d[BLOCK:]
        launch(a1_out.at[chunk], a1_in.at[chunk], s1_snd.at[0, chunk], s1_rcv.at[0, chunk], xn, z)
        launch(b1_out.at[chunk], b1_in.at[chunk], s1_snd.at[1, chunk], s1_rcv.at[1, chunk], yn, z)
        mine = product(chunk, me)
        own[chunk, 0] = mine[:BLOCK]
        own[chunk, 1] = mine[BLOCK:]

    def second(chunk):
        remote(a1_out.at[chunk], a1_in.at[chunk], s1_snd.at[0, chunk], s1_rcv.at[0, chunk], xn, z).wait_recv()
        a2_out[chunk] = (keep[chunk, 0] + a1_in[chunk, 1].astype(jnp.float32)).astype(jnp.bfloat16)
        launch(a2_out.at[chunk], a2_in.at[chunk], s2_snd.at[0, chunk], s2_rcv.at[0, chunk], yn, z)
        remote(b1_out.at[chunk], b1_in.at[chunk], s1_snd.at[1, chunk], s1_rcv.at[1, chunk], yn, z).wait_recv()
        b2_out[chunk] = (keep[chunk, 1] + b1_in[chunk, 1].astype(jnp.float32)).astype(jnp.bfloat16)
        launch(b2_out.at[chunk], b2_in.at[chunk], s2_snd.at[1, chunk], s2_rcv.at[1, chunk], xn, z)

    def rotate(head):
        return (head * cosine[...] + pltpu.roll(head, HEAD // 2, 1) * sine[...]).astype(jnp.bfloat16)

    def kv_copy(pair, origin):
        place = kv_buf.at[origin, pair]
        return remote(place, place, kv_snd.at[pair, origin], kv_rcv.at[pair, origin], me, lax.rem(z + 1, tops))

    def finish(chunk):
        both = ((a1_in, a2_in, a2_out, yn), (b1_in, b2_in, b2_out, xn))
        for doc, (first_in, second_in, second_out, peer) in enumerate(both):
            remote(
                second_out.at[chunk], second_in.at[chunk], s2_snd.at[doc, chunk], s2_rcv.at[doc, chunk], peer, z
            ).wait_recv()
            total = (
                own[chunk, doc]
                + first_in[chunk, 0].astype(jnp.float32)
                + second_in[chunk].astype(jnp.float32)
                + bias[core * chunks + chunk]
            )
            if chunk < PAIRS:
                kv_buf[z, chunk, doc, :, :HEAD] = rotate(total[:, :HEAD])
                kv_buf[z, chunk, doc, :, HEAD:] = total[:, HEAD:].astype(jnp.bfloat16)
            else:
                head = (chunk - PAIRS) * 2
                q_buf[doc, head] = rotate(total[:, :HEAD])
                q_buf[doc, head + 1] = rotate(total[:, HEAD:])
        if chunk < PAIRS:

            @pl.when(z < tops - 1)
            def _():
                kv_copy(chunk, z).start()

    def pass_on(pair, step):
        @pl.when(z >= step)
        def _():
            kv_copy(pair, z - step).wait_recv()

            @pl.when(z < tops - 1)
            def _():
                kv_copy(pair, z - step).start()

    def scores_of(queries, keys):
        return lax.dot_general(
            queries, keys, (((1,), (1,)), ((), ())), preferred_element_type=jnp.float32
        ) * HEAD ** (-0.5)

    def attend(pair):
        row = lax.broadcasted_iota(jnp.int32, (BLOCK, BLOCK), 0)
        column = lax.broadcasted_iota(jnp.int32, (BLOCK, BLOCK), 1)
        causal = jnp.concatenate([column <= row] * GROUP, axis=0)
        for doc in range(2):
            queries = q_buf[doc, pair * GROUP : (pair + 1) * GROUP].reshape(GROUP * BLOCK, HEAD)
            block = kv_buf[z, pair, doc]
            expo = jnp.where(causal, jnp.exp(scores_of(queries, block[:, :HEAD])), 0.0)
            tot[...] = expo
            acc[...] = jnp.dot(
                expo.astype(jnp.bfloat16), block[:, HEAD:], preferred_element_type=jnp.float32
            )
            for origin in range(tops - 1):

                @pl.when(origin < z)
                def _():
                    block = kv_buf[origin, pair, doc]
                    flags = mask_buf[PAIRS * core + pair]
                    seen = jnp.concatenate(
                        [
                            jnp.broadcast_to(flags[h * tops + origin : h * tops + origin + 1], (BLOCK, BLOCK))
                            for h in range(GROUP)
                        ],
                        axis=0,
                    )
                    expo = jnp.where(seen > 0.5, jnp.exp(scores_of(queries, block[:, :HEAD])), 0.0)
                    tot[...] += expo
                    acc[...] += jnp.dot(
                        expo.astype(jnp.bfloat16), block[:, HEAD:], preferred_element_type=jnp.float32
                    )

            mixed = (acc[...] / jnp.sum(tot[...], axis=-1, keepdims=True)).astype(jnp.bfloat16)
            for h in range(GROUP):
                first = h * HEAD
                o_buf[doc, pair, :, first : first + HEAD] = mixed[h * BLOCK : (h + 1) * BLOCK]
        launch(o_buf.at[1 - core, pair], o_in.at[pair], o_snd.at[pair], o_rcv.at[pair], sibling, z)

    multiply(0)
    multiply(1)
    for chunk in range(chunks):
        second(chunk)
        if chunk + 2 < chunks:
            multiply(chunk + 2)
        if chunk >= 1:
            finish(chunk - 1)
        if chunk == 2:
            pass_on(0, 1)
        if chunk == 3:
            pass_on(1, 1)
            pass_on(0, 2)
        if chunk == 4:
            pass_on(1, 2)
            pass_on(0, 3)
            for step in range(1, tops):
                here = mask_buf.at[lax.rem(z - step + tops, tops)]
                remote(here, here, m_snd.at[step - 1], m_rcv.at[step - 1], me, z).wait_recv()
    pass_on(1, 3)
    attend(0)
    finish(chunks - 1)
    attend(1)

    half = QHEADS // 2 * HEAD
    part = half // PAIRS
    for pair in range(PAIRS):
        first = pl.multiple_of(core * half + pair * part, HEAD)
        out[0, :, pl.ds(first, part)] = o_buf[core, pair]
    for pair in range(PAIRS):
        first = pl.multiple_of((1 - core) * half + pair * part, HEAD)
        remote(o_buf.at[core, pair], o_in.at[pair], o_snd.at[pair], o_rcv.at[pair], sibling, z).wait_recv()
        out[0, :, pl.ds(first, part)] = o_in[pair]
    for copy in sends:
        copy.wait_send()
    for pair in range(PAIRS):
        for step in range(tops):

            @pl.when((z >= step) & (z < tops - 1))
            def _():
                kv_copy(pair, z - step).wait_send()


def fused_body(
    hidden,
    norm_gain,
    w_query,
    w_key,
    w_value,
    bias_query,
    bias_key,
    bias_value,
    kv_blocks,
    block_counts,
):
    tops = lax.axis_size("ctx")
    rows = hidden.shape[1]
    depth = w_query.shape[0]
    chunks = PAIRS + QHEADS // 4
    halves = []
    for half in range(2):
        for pair in range(PAIRS):
            first = (PAIRS * half + pair) * HEAD
            halves += [bias_key[first : first + HEAD], bias_value[first : first + HEAD]]
        first = half * (QHEADS // 2 * HEAD)
        halves.append(bias_query[first : first + QHEADS // 2 * HEAD])
    bias = jnp.concatenate(halves).astype(jnp.float32).reshape(2 * chunks, 1, CHUNK)
    position = (lax.axis_index("ctx") * rows + jnp.arange(rows, dtype=jnp.int32)).astype(jnp.float32)
    exponent = (jnp.arange(HEAD) % (HEAD // 2)).astype(jnp.float32) * (2.0 / HEAD)
    angles = position[:, None] * jnp.power(jnp.float32(THETA), -exponent)[None, :]
    cosine = jnp.cos(angles)
    sine = jnp.sin(angles) * jnp.where(jnp.arange(HEAD) < HEAD // 2, -1.0, 1.0)
    slots = jnp.arange(MAXB)
    active = (slots > 0) & (slots < block_counts[:, :, None])
    seen = jnp.any(active[..., None] & (kv_blocks[..., None] == jnp.arange(tops)), axis=2)
    seen = seen.transpose(1, 0, 2).reshape(tops, GROUP * tops, 1).astype(jnp.float32)
    allowed = jnp.broadcast_to(seen, (tops, GROUP * tops, HEAD))
    bf16, f32 = jnp.bfloat16, jnp.float32
    vmem = pl.BlockSpec(memory_space=pltpu.VMEM)
    hbm = pl.BlockSpec(memory_space=pl.ANY)
    dma = pltpu.SemaphoreType.DMA
    copies = 2 * PAIRS + chunks - PAIRS
    part = QHEADS // 2 * HEAD // PAIRS
    return pl.pallas_call(
        fused_kernel,
        out_shape=jax.ShapeDtypeStruct((1, rows, QHEADS * HEAD), bf16),
        in_specs=[vmem, vmem, hbm, hbm, hbm, vmem, vmem, vmem, vmem],
        out_specs=vmem,
        scratch_shapes=[
            pltpu.VMEM((3, rows, 2 * depth), bf16),
            pltpu.VMEM((8, rows, 2 * depth), bf16),
            pltpu.VMEM((chunks, 2 * depth, CHUNK), bf16),
            pltpu.VMEM((chunks, 2, rows, CHUNK), bf16),
            pltpu.VMEM((chunks, 2, rows, CHUNK), bf16),
            pltpu.VMEM((chunks, 2, rows, CHUNK), bf16),
            pltpu.VMEM((chunks, 2, rows, CHUNK), bf16),
            pltpu.VMEM((chunks, rows, CHUNK), bf16),
            pltpu.VMEM((chunks, rows, CHUNK), bf16),
            pltpu.VMEM((chunks, rows, CHUNK), bf16),
            pltpu.VMEM((chunks, rows, CHUNK), bf16),
            pltpu.VMEM((chunks, 2, rows, CHUNK), f32),
            pltpu.VMEM((chunks, 2, rows, CHUNK), f32),
            pltpu.VMEM((tops, PAIRS, 2, rows, CHUNK), bf16),
            pltpu.VMEM((2, QHEADS // 2, rows, HEAD), bf16),
            pltpu.VMEM((tops, GROUP * tops, HEAD), f32),
            pltpu.VMEM((GROUP * rows, HEAD), f32),
            pltpu.VMEM((GROUP * rows, HEAD), f32),
            pltpu.VMEM((2, PAIRS, rows, part), bf16),
            pltpu.VMEM((PAIRS, rows, part), bf16),
            dma((copies,)),
            dma((copies,)),
            dma((copies,)),
            dma((3,)),
            dma((3,)),
            dma((4,)),
            dma((4,)),
            dma((tops - 1,)),
            dma((tops - 1,)),
            dma((2, chunks)),
            dma((2, chunks)),
            dma((2, chunks)),
            dma((2, chunks)),
            dma((PAIRS, tops)),
            dma((PAIRS, tops)),
            dma((PAIRS,)),
            dma((PAIRS,)),
        ],
        compiler_params=pltpu.CompilerParams(
            collective_id=0, has_side_effects=True, vmem_limit_bytes=40 * 1024 * 1024
        ),
    )(
        hidden,
        norm_gain.reshape(1, -1),
        w_query,
        w_key,
        w_value,
        bias,
        cosine,
        sine,
        allowed,
    )


def solution(mesh):
    placed = (
        P("dp", "ctx", None),
        P(),
        P("dp", None),
        P("dp", None),
        P("dp", None),
        P(),
        P(),
        P(),
        P("ctx", None, None),
        P("ctx", None),
    )
    plane = mesh.shape["dp"] == 8 and mesh.shape["ctx"] == MAXB
    return jax.shard_map(
        fused_body if plane else body, mesh=mesh, in_specs=placed, out_specs=P("dp", "ctx", None), check_vma=False
    )
```

```python
import math

import jax
import jax.numpy as jnp
from jax import lax
from jax.experimental import pallas as pl
from jax.experimental.pallas import tpu as pltpu
from jax.sharding import PartitionSpec as P

KVH = 4
HEAD = 128
QHEADS = 16
BLOCK = 128
MAXB = 4


EPSILON = 1e-06
THETA = 1000000.0


def rms_norm(tokens, norm_gain):
    floats = tokens.astype(jnp.float32)
    meansq = jnp.mean(floats * floats, axis=-1, keepdims=True)
    return (floats * lax.rsqrt(meansq + EPSILON) * norm_gain.astype(jnp.float32)).astype(
        jnp.bfloat16
    )


def rotary(heads_in, position):
    half_size = heads_in.shape[-1] // 2
    exponent = jnp.arange(half_size, dtype=jnp.float32) * (2.0 / heads_in.shape[-1])
    inverse = jnp.power(jnp.float32(THETA), -exponent)
    angles = position[:, None] * inverse[None, :]
    cosine = jnp.cos(angles)[:, None, :]
    sine = jnp.sin(angles)[:, None, :]
    first = heads_in[..., :half_size]
    second = heads_in[..., half_size:]
    return jnp.concatenate(
        [first * cosine - second * sine, second * cosine + first * sine], axis=-1
    )


def finish_heads(summed, bias, heads, position, rotate_it):
    shaped = (summed + bias.astype(jnp.float32)).reshape(summed.shape[0], heads, HEAD)
    if rotate_it:
        shaped = rotary(shaped, position)
    return shaped.astype(jnp.bfloat16)


def fold_rows(source, pieces):
    return tuple((jnp.dot(source, piece, preferred_element_type=jnp.float32) for piece in pieces))


def sparse_head(queries, key_rows, value_rows, blocks, counts):
    nblocks = queries.shape[0] // BLOCK
    query_tiles = queries.reshape(nblocks, BLOCK, HEAD)
    key_tiles = key_rows.reshape(nblocks, BLOCK, HEAD)[blocks].reshape(nblocks, MAXB * BLOCK, HEAD)
    value_tiles = value_rows.reshape(nblocks, BLOCK, HEAD)[blocks].reshape(
        nblocks, MAXB * BLOCK, HEAD
    )
    scores = jnp.einsum(
        "qih,qjh->qij", query_tiles, key_tiles, preferred_element_type=jnp.float32
    ) * HEAD ** (-0.5)
    column = jnp.arange(MAXB * BLOCK)
    slot_of = column // BLOCK
    inside = column % BLOCK
    row_pos = jnp.arange(BLOCK)
    allowed = (slot_of[None, None, :] < counts[:, None, None]) & (
        (slot_of[None, None, :] > 0) | (inside[None, None, :] <= row_pos[None, :, None])
    )
    expo = jnp.where(allowed, jnp.exp(scores), jnp.float32(0.0))
    totals = jnp.sum(expo, axis=-1)
    probs = expo.astype(jnp.bfloat16)
    mixed = (
        jnp.einsum("qij,qjh->qih", probs, value_tiles, preferred_element_type=jnp.float32)
        / totals[..., None]
    )
    return mixed.astype(jnp.bfloat16).reshape(nblocks * BLOCK, HEAD)


def one_head(packed):
    return sparse_head(packed[0], packed[1], packed[2], packed[3], packed[4])


def body(
    hidden,
    norm_gain,
    w_query,
    w_key,
    w_value,
    bias_query,
    bias_key,
    bias_value,
    kv_blocks,
    block_counts,
):
    groups = lax.axis_size("ctx")
    device = lax.axis_index("ctx")
    tokens = hidden[0]
    local_rows = tokens.shape[0]
    seq_len = local_rows * groups
    heads_here = QHEADS // groups
    kv_here = KVH // groups
    width_query = heads_here * HEAD
    width_pair = kv_here * HEAD
    normed = rms_norm(tokens, norm_gain)
    parts = lax.axis_size("dp")
    depth = w_query.shape[0]
    gathered = lax.all_to_all(
        normed.reshape(local_rows, parts, depth), "dp", split_axis=1, concat_axis=0, tiled=True
    ).reshape(parts * local_rows, depth)
    weights = jnp.concatenate([w_key, w_value, w_query], axis=1)
    partial = jnp.dot(gathered, weights, preferred_element_type=jnp.float32).astype(jnp.bfloat16)
    summed = lax.psum_scatter(partial, "dp", scatter_dimension=0, tiled=True).astype(jnp.float32)
    width = KVH * HEAD
    sum_key, sum_value, sum_query = (
        summed[:, :width],
        summed[:, width : 2 * width],
        summed[:, 2 * width :],
    )
    position = (device * local_rows + jnp.arange(local_rows, dtype=jnp.int32)).astype(jnp.float32)
    queries = finish_heads(sum_query, bias_query, QHEADS, position, True)
    key_rows = finish_heads(sum_key, bias_key, KVH, position, True)
    value_rows = finish_heads(sum_value, bias_value, KVH, position, False)
    query_send = queries.reshape(local_rows, groups, width_query)
    pair_send = jnp.concatenate([key_rows, value_rows], axis=2)
    query_got, pair_got = (
        lax.all_to_all(query_send, "ctx", split_axis=1, concat_axis=0, tiled=True),
        lax.all_to_all(pair_send, "ctx", split_axis=1, concat_axis=0, tiled=True),
    )
    queries = query_got.reshape(seq_len, heads_here, HEAD)
    key_rows = pair_got[:, 0, :width_pair].reshape(seq_len, kv_here, HEAD)
    value_rows = pair_got[:, 0, width_pair:].reshape(seq_len, kv_here, HEAD)
    group = heads_here // kv_here
    key_rows = jnp.repeat(key_rows, group, axis=1)
    value_rows = jnp.repeat(value_rows, group, axis=1)
    mixed = lax.map(
        one_head,
        (
            queries.transpose(1, 0, 2),
            key_rows.transpose(1, 0, 2),
            value_rows.transpose(1, 0, 2),
            kv_blocks,
            block_counts,
        ),
    )
    result = mixed.transpose(1, 0, 2).reshape(seq_len, 1, width_query)
    returned = lax.all_to_all(result, "ctx", split_axis=0, concat_axis=1, tiled=True)
    return returned.reshape(1, local_rows, QHEADS * HEAD)


MESH = pl.DeviceIdType.MESH
CHUNK = 2 * HEAD
GROUP = QHEADS // KVH
PAIRS = KVH // 2


def chunk_sources(half, chunk):
    if chunk < PAIRS:
        first = pl.multiple_of((PAIRS * half + chunk) * HEAD, HEAD)
        return ((1, first, HEAD, 0), (2, first, HEAD, HEAD))
    first = half * (QHEADS // 2 * HEAD) + (chunk - PAIRS) * CHUNK
    return ((0, pl.multiple_of(first, CHUNK), CHUNK, 0),)


def fused_kernel(
    hidden,
    gain,
    w_query,
    w_key,
    w_value,
    bias_query,
    bias_key,
    bias_value,
    kv_blocks,
    block_counts,
    out,
    raw,
    gains,
    biases,
    cosine,
    sine,
    allowed,
    normed,
    x_buf,
    w_buf,
    a1_out,
    a1_in,
    b1_out,
    b1_in,
    a2_out,
    a2_in,
    b2_out,
    b2_in,
    keep,
    own,
    kv_buf,
    q_buf,
    mask_buf,
    acc,
    tot,
    o_buf,
    o_in,
    h_sem,
    w_loc,
    w_snd,
    w_rcv,
    x_snd,
    x_rcv,
    f_snd,
    f_rcv,
    m_snd,
    m_rcv,
    s1_snd,
    s1_rcv,
    s2_snd,
    s2_rcv,
    kv_snd,
    kv_rcv,
    o_snd,
    o_rcv,
):
    me = lax.axis_index("dp")
    z = lax.axis_index("ctx")
    tops = lax.axis_size("ctx")
    core = lax.rem(me, 2)
    xpos = lax.rem(me // 2, 2)
    ypos = me // 4
    sibling = me + 1 - 2 * core
    xn = me + 2 - 4 * xpos
    yn = me + 4 - 8 * ypos
    dn = xn + 4 - 8 * ypos
    chunks = w_buf.shape[0]
    depth = w_query.shape[0]
    width = 2 * depth
    weights = (w_query, w_key, w_value)
    sends = []

    read = pltpu.make_async_copy(hidden.at[0], raw, h_sem)
    read.start()
    barrier = pltpu.get_barrier_semaphore()
    for peer in (sibling, xn, yn, dn):
        pl.semaphore_signal(barrier, inc=1, device_id=(peer, z), device_id_type=MESH)
    for step in range(1, tops):
        pl.semaphore_signal(barrier, inc=1, device_id=(me, lax.rem(z + step, tops)), device_id_type=MESH)

    def remote(src, dst, snd, rcv, dp, ctx):
        return pltpu.make_async_remote_copy(
            src_ref=src, dst_ref=dst, send_sem=snd, recv_sem=rcv, device_id=(dp, ctx), device_id_type=MESH
        )

    def launch(*args):
        copy = remote(*args)
        copy.start()
        sends.append(copy)

    locals_ = []
    rows = pl.ds(pl.multiple_of(core * depth, 64), depth)
    number = 0
    for chunk in range(chunks):
        for which, first, cols, place in chunk_sources(core, chunk):
            copy = pltpu.make_async_copy(
                weights[which].at[:, pl.ds(first, cols)],
                w_buf.at[chunk, rows, pl.ds(place, cols)],
                w_loc.at[number],
            )
            copy.start()
            locals_.append((chunk, copy))
            number += 1

    gains[...] = gain[...].astype(jnp.float32).reshape(1, -1)
    read.wait()
    floats = raw[...].astype(jnp.float32)
    scale = lax.rsqrt(jnp.mean(floats * floats, axis=-1, keepdims=True) + EPSILON)

    def norm_block(chip):
        cols = pl.ds(pl.multiple_of(chip * width, HEAD), width)
        return (raw[:, cols].astype(jnp.float32) * scale * gains[:, cols]).astype(jnp.bfloat16)

    normed[1] = norm_block(xn // 2)
    pl.semaphore_wait(barrier, 4 + tops - 1)
    relations = (dn, xn, yn)
    for index in (1, 2, 0):
        peer = relations[index]
        if index != 1:
            normed[index] = norm_block(peer // 2)
        launch(normed.at[index], x_buf.at[me], x_snd.at[index], x_rcv.at[index], peer, z)
    x_buf[me] = norm_block(me // 2)
    launch(x_buf.at[me], x_buf.at[me], f_snd.at[3], f_rcv.at[3], sibling, z)

    number = 0
    for chunk in range(chunks):
        for which, first, cols, place in chunk_sources(1 - core, chunk):
            launch(
                weights[which].at[:, pl.ds(first, cols)],
                w_buf.at[chunk, rows, pl.ds(place, cols)],
                w_snd.at[number],
                w_rcv.at[number],
                sibling,
                z,
            )
            number += 1
    for h in range(GROUP):
        for b in range(tops):
            blocks = kv_blocks[h, b : b + 1, :]
            count = block_counts[h : h + 1, b : b + 1]
            origin = lax.broadcasted_iota(jnp.int32, (tops, HEAD), 0)
            seen = jnp.zeros((tops, HEAD), jnp.float32)
            for slot in range(1, MAXB):
                hit = (blocks[:, slot : slot + 1] == origin) & (count > slot)
                seen = jnp.where(hit, 1.0, seen)
            allowed[b, h * tops : (h + 1) * tops, :] = seen
    for step in range(1, tops):
        peer = lax.rem(z + step, tops)
        launch(allowed.at[peer], mask_buf.at[z], m_snd.at[step - 1], m_rcv.at[step - 1], me, peer)
    mask_buf[z] = allowed[z]

    lane = lax.broadcasted_iota(jnp.int32, (BLOCK, HEAD), 1)
    token = lax.broadcasted_iota(jnp.int32, (BLOCK, HEAD), 0) + z * BLOCK
    exponent = lax.rem(lane, HEAD // 2).astype(jnp.float32) * (2.0 / HEAD)
    angles = token.astype(jnp.float32) * jnp.exp(exponent * (-math.log(THETA)))
    cosine[...] = jnp.cos(angles)
    sine[...] = jnp.where(lane < HEAD // 2, -jnp.sin(angles), jnp.sin(angles))
    starts = []
    for vector in (bias_query, bias_key, bias_value):
        first = starts[-1][1] if starts else 0
        starts.append((first, first + vector.shape[0]))
        biases[:, first : first + vector.shape[0]] = vector[...].astype(jnp.float32).reshape(1, -1)

    def bias_of(chunk):
        return jnp.concatenate(
            [
                biases[:, pl.ds(pl.multiple_of(starts[which][0] + first, HEAD), cols)]
                for which, first, cols, _ in chunk_sources(core, chunk)
            ],
            axis=1,
        )

    def sibling_of(device):
        return device + 1 - 2 * core

    def docs_of(index):
        peer = relations[index]
        remote(x_buf.at[peer], x_buf.at[peer], x_snd.at[index], x_rcv.at[index], peer, z).wait_recv()
        launch(x_buf.at[peer], x_buf.at[peer], f_snd.at[index], f_rcv.at[index], sibling, z)

    def forwarded(index, device):
        there = x_buf.at[sibling_of(device)]
        remote(there, there, f_snd.at[index], f_rcv.at[index], sibling, z).wait_recv()

    def wait_weights(chunk):
        other = pl.ds(pl.multiple_of((1 - core) * depth, 64), depth)
        for number, (owner, copy) in enumerate(locals_):
            if owner == chunk:
                copy.wait()
        number = 0
        for at in range(chunks):
            for _, _, cols, place in chunk_sources(core, at):
                if at == chunk:
                    there = w_buf.at[chunk, other, pl.ds(place, cols)]
                    remote(there, there, w_snd.at[number], w_rcv.at[number], sibling, z).wait_recv()
                number += 1

    def product(chunk, device):
        pair = x_buf[pl.ds(device // 2 * 2, 2)].reshape(2 * BLOCK, width)
        return jnp.dot(pair, w_buf[chunk], preferred_element_type=jnp.float32)

    def first_x(chunk):
        to_x = product(chunk, xn)
        a1_out[chunk, 0] = to_x[:BLOCK].astype(jnp.bfloat16)
        keep[chunk, 1] = to_x[BLOCK:]
        first_copy(0, 0, chunk).start()

    def first_y(chunk):
        to_y = product(chunk, yn)
        b1_out[chunk, 0] = to_y[BLOCK:].astype(jnp.bfloat16)
        keep[chunk, 0] = to_y[:BLOCK]
        first_copy(1, 0, chunk).start()

    def first_d(chunk):
        to_d = product(chunk, dn).astype(jnp.bfloat16)
        a1_out[chunk, 1] = to_d[:BLOCK]
        b1_out[chunk, 1] = to_d[BLOCK:]
        first_copy(0, 1, chunk).start()
        first_copy(1, 1, chunk).start()

    def first_own(chunk):
        mine = product(chunk, me)
        own[chunk, 0] = mine[:BLOCK]
        own[chunk, 1] = mine[BLOCK:]

    def first_copy(doc, piece, chunk):
        there, back = ((a1_out, a1_in), (b1_out, b1_in))[doc]
        return remote(
            there.at[chunk, piece],
            back.at[chunk, piece],
            s1_snd.at[doc, piece, chunk],
            s1_rcv.at[doc, piece, chunk],
            (xn, yn)[doc],
            z,
        )

    def multiply(chunk):
        wait_weights(chunk)
        first_d(chunk)
        first_x(chunk)
        first_y(chunk)
        first_own(chunk)

    def second(chunk):
        first_copy(0, 1, chunk).wait_recv()
        a2_out[chunk] = (keep[chunk, 0] + a1_in[chunk, 1].astype(jnp.float32)).astype(jnp.bfloat16)
        launch(a2_out.at[chunk], a2_in.at[chunk], s2_snd.at[0, chunk], s2_rcv.at[0, chunk], yn, z)
        first_copy(1, 1, chunk).wait_recv()
        b2_out[chunk] = (keep[chunk, 1] + b1_in[chunk, 1].astype(jnp.float32)).astype(jnp.bfloat16)
        launch(b2_out.at[chunk], b2_in.at[chunk], s2_snd.at[1, chunk], s2_rcv.at[1, chunk], xn, z)

    def rotate(head):
        return (head * cosine[...] + pltpu.roll(head, HEAD // 2, 1) * sine[...]).astype(jnp.bfloat16)

    def kv_copy(pair, origin):
        place = kv_buf.at[origin, pair]
        return remote(place, place, kv_snd.at[pair, origin], kv_rcv.at[pair, origin], me, lax.rem(z + 1, tops))

    def finish(chunk):
        both = ((a1_in, a2_in, a2_out, yn), (b1_in, b2_in, b2_out, xn))
        bias = bias_of(chunk)
        for doc, (first_in, second_in, second_out, peer) in enumerate(both):
            first_copy(doc, 0, chunk).wait_recv()
            remote(
                second_out.at[chunk], second_in.at[chunk], s2_snd.at[doc, chunk], s2_rcv.at[doc, chunk], peer, z
            ).wait_recv()
            total = (
                own[chunk, doc]
                + first_in[chunk, 0].astype(jnp.float32)
                + second_in[chunk].astype(jnp.float32)
                + bias
            )
            if chunk < PAIRS:
                kv_buf[z, chunk, doc, :, :HEAD] = rotate(total[:, :HEAD])
                kv_buf[z, chunk, doc, :, HEAD:] = total[:, HEAD:].astype(jnp.bfloat16)
            else:
                head = (chunk - PAIRS) * 2
                q_buf[doc, head] = rotate(total[:, :HEAD])
                q_buf[doc, head + 1] = rotate(total[:, HEAD:])
        if chunk < PAIRS:

            @pl.when(z < tops - 1)
            def _():
                kv_copy(chunk, z).start()

    def pass_on(pair, step):
        @pl.when(z >= step)
        def _():
            kv_copy(pair, z - step).wait_recv()

            @pl.when(z < tops - 1)
            def _():
                kv_copy(pair, z - step).start()

    def scores_of(queries, keys):
        return lax.dot_general(
            queries, keys, (((1,), (1,)), ((), ())), preferred_element_type=jnp.float32
        ) * HEAD ** (-0.5)

    row = lax.broadcasted_iota(jnp.int32, (BLOCK, BLOCK), 0)
    column = lax.broadcasted_iota(jnp.int32, (BLOCK, BLOCK), 1)
    causal = jnp.concatenate([column <= row] * 2, axis=0)

    def attend_own(chunk):
        at = chunk - PAIRS
        for doc in range(2):
            queries = q_buf[doc, 2 * at : 2 * at + 2].reshape(2 * BLOCK, HEAD)
            block = kv_buf[z, at // 2, doc]
            expo = jnp.where(causal, jnp.exp(scores_of(queries, block[:, :HEAD])), 0.0)
            tot[at, doc] = expo
            acc[at, doc] = jnp.dot(
                expo.astype(jnp.bfloat16), block[:, HEAD:], preferred_element_type=jnp.float32
            )

    def attend_below(chunk, step):
        at = chunk - PAIRS

        @pl.when(z >= step)
        def _():
            origin = z - step
            rows_of = [
                mask_buf[PAIRS * core + at // 2, pl.ds((at % 2 * 2 + h) * tops + origin, 1)]
                for h in range(2)
            ]
            seen = jnp.concatenate([jnp.broadcast_to(r, (BLOCK, BLOCK)) for r in rows_of], axis=0)
            for doc in range(2):
                queries = q_buf[doc, 2 * at : 2 * at + 2].reshape(2 * BLOCK, HEAD)
                block = kv_buf[origin, at // 2, doc]
                expo = jnp.where(seen > 0.5, jnp.exp(scores_of(queries, block[:, :HEAD])), 0.0)
                tot[at, doc] += expo
                acc[at, doc] += jnp.dot(
                    expo.astype(jnp.bfloat16), block[:, HEAD:], preferred_element_type=jnp.float32
                )

    def attend_end(chunk):
        at = chunk - PAIRS
        for doc in range(2):
            mixed = (acc[at, doc] / jnp.sum(tot[at, doc], axis=-1, keepdims=True)).astype(jnp.bfloat16)
            o_buf[doc, at, :, :HEAD] = mixed[:BLOCK]
            o_buf[doc, at, :, HEAD:] = mixed[BLOCK:]
        launch(o_buf.at[1 - core, at], o_in.at[at], o_snd.at[at], o_rcv.at[at], sibling, z)

    wait_weights(0)
    wait_weights(1)
    forwarded(3, me)
    docs_of(1)
    docs_of(2)
    forwarded(1, xn)
    first_x(0)
    first_x(1)
    forwarded(2, yn)
    first_y(0)
    first_y(1)
    docs_of(0)
    first_own(0)
    forwarded(0, dn)
    first_d(0)
    first_d(1)
    first_own(1)
    second(0)
    second(1)
    multiply(2)
    finish(0)
    multiply(3)
    finish(1)
    second(2)
    pass_on(0, 1)
    multiply(4)
    for step in range(1, tops):
        here = mask_buf.at[lax.rem(z - step + tops, tops)]
        remote(here, here, m_snd.at[step - 1], m_rcv.at[step - 1], me, z).wait_recv()
    second(3)
    multiply(5)
    pass_on(1, 1)
    finish(2)
    attend_own(2)
    attend_below(2, 1)
    pass_on(0, 2)
    attend_below(2, 2)
    second(4)
    finish(3)
    attend_own(3)
    attend_below(3, 1)
    pass_on(1, 2)
    attend_below(3, 2)
    second(5)
    pass_on(0, 3)
    attend_below(2, 3)
    attend_end(2)
    attend_below(3, 3)
    attend_end(3)
    finish(4)
    attend_own(4)
    attend_below(4, 1)
    attend_below(4, 2)
    finish(5)
    attend_own(5)
    attend_below(5, 1)
    attend_below(5, 2)
    pass_on(1, 3)
    attend_below(4, 3)
    attend_end(4)
    attend_below(5, 3)
    attend_end(5)

    half = QHEADS // 2 * HEAD
    for at in range(chunks - PAIRS):
        first = pl.multiple_of(core * half + at * CHUNK, CHUNK)
        out[0, :, pl.ds(first, CHUNK)] = o_buf[core, at]
    for at in range(chunks - PAIRS):
        first = pl.multiple_of((1 - core) * half + at * CHUNK, CHUNK)
        remote(o_buf.at[core, at], o_in.at[at], o_snd.at[at], o_rcv.at[at], sibling, z).wait_recv()
        out[0, :, pl.ds(first, CHUNK)] = o_in[at]
    for doc in range(2):
        for piece in range(2):
            for chunk in range(chunks):
                first_copy(doc, piece, chunk).wait_send()
    for copy in sends:
        copy.wait_send()
    for pair in range(PAIRS):
        for step in range(tops):

            @pl.when((z >= step) & (z < tops - 1))
            def _():
                kv_copy(pair, z - step).wait_send()


def fused_body(
    hidden,
    norm_gain,
    w_query,
    w_key,
    w_value,
    bias_query,
    bias_key,
    bias_value,
    kv_blocks,
    block_counts,
):
    tops = lax.axis_size("ctx")
    rows = hidden.shape[1]
    depth = w_query.shape[0]
    chunks = PAIRS + QHEADS // 4
    bf16, f32 = jnp.bfloat16, jnp.float32
    vmem = pl.BlockSpec(memory_space=pltpu.VMEM)
    hbm = pl.BlockSpec(memory_space=pl.ANY)
    dma = pltpu.SemaphoreType.DMA
    copies = 2 * PAIRS + chunks - PAIRS
    return pl.pallas_call(
        fused_kernel,
        out_shape=jax.ShapeDtypeStruct((1, rows, QHEADS * HEAD), bf16),
        in_specs=[hbm, vmem, hbm, hbm, hbm, vmem, vmem, vmem, vmem, vmem],
        out_specs=vmem,
        scratch_shapes=[
            pltpu.VMEM((rows, hidden.shape[2]), bf16),
            pltpu.VMEM((1, hidden.shape[2]), f32),
            pltpu.VMEM((1, (QHEADS + 2 * KVH) * HEAD), f32),
            pltpu.VMEM((rows, HEAD), f32),
            pltpu.VMEM((rows, HEAD), f32),
            pltpu.VMEM((tops, GROUP * tops, HEAD), f32),
            pltpu.VMEM((3, rows, 2 * depth), bf16),
            pltpu.VMEM((8, rows, 2 * depth), bf16),
            pltpu.VMEM((chunks, 2 * depth, CHUNK), bf16),
            pltpu.VMEM((chunks, 2, rows, CHUNK), bf16),
            pltpu.VMEM((chunks, 2, rows, CHUNK), bf16),
            pltpu.VMEM((chunks, 2, rows, CHUNK), bf16),
            pltpu.VMEM((chunks, 2, rows, CHUNK), bf16),
            pltpu.VMEM((chunks, rows, CHUNK), bf16),
            pltpu.VMEM((chunks, rows, CHUNK), bf16),
            pltpu.VMEM((chunks, rows, CHUNK), bf16),
            pltpu.VMEM((chunks, rows, CHUNK), bf16),
            pltpu.VMEM((chunks, 2, rows, CHUNK), f32),
            pltpu.VMEM((chunks, 2, rows, CHUNK), f32),
            pltpu.VMEM((tops, PAIRS, 2, rows, CHUNK), bf16),
            pltpu.VMEM((2, QHEADS // 2, rows, HEAD), bf16),
            pltpu.VMEM((tops, GROUP * tops, HEAD), f32),
            pltpu.VMEM((chunks - PAIRS, 2, 2 * rows, HEAD), f32),
            pltpu.VMEM((chunks - PAIRS, 2, 2 * rows, HEAD), f32),
            pltpu.VMEM((2, chunks - PAIRS, rows, CHUNK), bf16),
            pltpu.VMEM((chunks - PAIRS, rows, CHUNK), bf16),
            dma,
            dma((copies,)),
            dma((copies,)),
            dma((copies,)),
            dma((3,)),
            dma((3,)),
            dma((4,)),
            dma((4,)),
            dma((tops - 1,)),
            dma((tops - 1,)),
            dma((2, 2, chunks)),
            dma((2, 2, chunks)),
            dma((2, chunks)),
            dma((2, chunks)),
            dma((PAIRS, tops)),
            dma((PAIRS, tops)),
            dma((chunks - PAIRS,)),
            dma((chunks - PAIRS,)),
        ],
        compiler_params=pltpu.CompilerParams(
            collective_id=0, has_side_effects=True, vmem_limit_bytes=60 * 1024 * 1024
        ),
    )(
        hidden,
        norm_gain,
        w_query,
        w_key,
        w_value,
        bias_query,
        bias_key,
        bias_value,
        kv_blocks,
        block_counts,
    )


def solution(mesh):
    placed = (
        P("dp", "ctx", None),
        P(),
        P("dp", None),
        P("dp", None),
        P("dp", None),
        P(),
        P(),
        P(),
        P("ctx", None, None),
        P("ctx", None),
    )
    plane = mesh.shape["dp"] == 8 and mesh.shape["ctx"] == MAXB
    return jax.shard_map(
        fused_body if plane else body, mesh=mesh, in_specs=placed, out_specs=P("dp", "ctx", None), check_vma=False
    )
```

```python
import math

import jax
import jax.numpy as jnp
from jax import lax
from jax.experimental import pallas as pl
from jax.experimental.pallas import tpu as pltpu
from jax.sharding import PartitionSpec as P

KVH = 4
HEAD = 128
QHEADS = 16
BLOCK = 128
MAXB = 4


EPSILON = 1e-06
THETA = 1000000.0


def rms_norm(tokens, norm_gain):
    floats = tokens.astype(jnp.float32)
    meansq = jnp.mean(floats * floats, axis=-1, keepdims=True)
    return (floats * lax.rsqrt(meansq + EPSILON) * norm_gain.astype(jnp.float32)).astype(
        jnp.bfloat16
    )


def rotary(heads_in, position):
    half_size = heads_in.shape[-1] // 2
    exponent = jnp.arange(half_size, dtype=jnp.float32) * (2.0 / heads_in.shape[-1])
    inverse = jnp.power(jnp.float32(THETA), -exponent)
    angles = position[:, None] * inverse[None, :]
    cosine = jnp.cos(angles)[:, None, :]
    sine = jnp.sin(angles)[:, None, :]
    first = heads_in[..., :half_size]
    second = heads_in[..., half_size:]
    return jnp.concatenate(
        [first * cosine - second * sine, second * cosine + first * sine], axis=-1
    )


def finish_heads(summed, bias, heads, position, rotate_it):
    shaped = (summed + bias.astype(jnp.float32)).reshape(summed.shape[0], heads, HEAD)
    if rotate_it:
        shaped = rotary(shaped, position)
    return shaped.astype(jnp.bfloat16)


def fold_rows(source, pieces):
    return tuple((jnp.dot(source, piece, preferred_element_type=jnp.float32) for piece in pieces))


def sparse_head(queries, key_rows, value_rows, blocks, counts):
    nblocks = queries.shape[0] // BLOCK
    query_tiles = queries.reshape(nblocks, BLOCK, HEAD)
    key_tiles = key_rows.reshape(nblocks, BLOCK, HEAD)[blocks].reshape(nblocks, MAXB * BLOCK, HEAD)
    value_tiles = value_rows.reshape(nblocks, BLOCK, HEAD)[blocks].reshape(
        nblocks, MAXB * BLOCK, HEAD
    )
    scores = jnp.einsum(
        "qih,qjh->qij", query_tiles, key_tiles, preferred_element_type=jnp.float32
    ) * HEAD ** (-0.5)
    column = jnp.arange(MAXB * BLOCK)
    slot_of = column // BLOCK
    inside = column % BLOCK
    row_pos = jnp.arange(BLOCK)
    allowed = (slot_of[None, None, :] < counts[:, None, None]) & (
        (slot_of[None, None, :] > 0) | (inside[None, None, :] <= row_pos[None, :, None])
    )
    expo = jnp.where(allowed, jnp.exp(scores), jnp.float32(0.0))
    totals = jnp.sum(expo, axis=-1)
    probs = expo.astype(jnp.bfloat16)
    mixed = (
        jnp.einsum("qij,qjh->qih", probs, value_tiles, preferred_element_type=jnp.float32)
        / totals[..., None]
    )
    return mixed.astype(jnp.bfloat16).reshape(nblocks * BLOCK, HEAD)


def one_head(packed):
    return sparse_head(packed[0], packed[1], packed[2], packed[3], packed[4])


def body(
    hidden,
    norm_gain,
    w_query,
    w_key,
    w_value,
    bias_query,
    bias_key,
    bias_value,
    kv_blocks,
    block_counts,
):
    groups = lax.axis_size("ctx")
    device = lax.axis_index("ctx")
    tokens = hidden[0]
    local_rows = tokens.shape[0]
    seq_len = local_rows * groups
    heads_here = QHEADS // groups
    kv_here = KVH // groups
    width_query = heads_here * HEAD
    width_pair = kv_here * HEAD
    normed = rms_norm(tokens, norm_gain)
    parts = lax.axis_size("dp")
    depth = w_query.shape[0]
    gathered = lax.all_to_all(
        normed.reshape(local_rows, parts, depth), "dp", split_axis=1, concat_axis=0, tiled=True
    ).reshape(parts * local_rows, depth)
    weights = jnp.concatenate([w_key, w_value, w_query], axis=1)
    partial = jnp.dot(gathered, weights, preferred_element_type=jnp.float32).astype(jnp.bfloat16)
    summed = lax.psum_scatter(partial, "dp", scatter_dimension=0, tiled=True).astype(jnp.float32)
    width = KVH * HEAD
    sum_key, sum_value, sum_query = (
        summed[:, :width],
        summed[:, width : 2 * width],
        summed[:, 2 * width :],
    )
    position = (device * local_rows + jnp.arange(local_rows, dtype=jnp.int32)).astype(jnp.float32)
    queries = finish_heads(sum_query, bias_query, QHEADS, position, True)
    key_rows = finish_heads(sum_key, bias_key, KVH, position, True)
    value_rows = finish_heads(sum_value, bias_value, KVH, position, False)
    query_send = queries.reshape(local_rows, groups, width_query)
    pair_send = jnp.concatenate([key_rows, value_rows], axis=2)
    query_got, pair_got = (
        lax.all_to_all(query_send, "ctx", split_axis=1, concat_axis=0, tiled=True),
        lax.all_to_all(pair_send, "ctx", split_axis=1, concat_axis=0, tiled=True),
    )
    queries = query_got.reshape(seq_len, heads_here, HEAD)
    key_rows = pair_got[:, 0, :width_pair].reshape(seq_len, kv_here, HEAD)
    value_rows = pair_got[:, 0, width_pair:].reshape(seq_len, kv_here, HEAD)
    group = heads_here // kv_here
    key_rows = jnp.repeat(key_rows, group, axis=1)
    value_rows = jnp.repeat(value_rows, group, axis=1)
    mixed = lax.map(
        one_head,
        (
            queries.transpose(1, 0, 2),
            key_rows.transpose(1, 0, 2),
            value_rows.transpose(1, 0, 2),
            kv_blocks,
            block_counts,
        ),
    )
    result = mixed.transpose(1, 0, 2).reshape(seq_len, 1, width_query)
    returned = lax.all_to_all(result, "ctx", split_axis=0, concat_axis=1, tiled=True)
    return returned.reshape(1, local_rows, QHEADS * HEAD)


MESH = pl.DeviceIdType.MESH
CHUNK = 2 * HEAD
GROUP = QHEADS // KVH
PAIRS = KVH // 2


def chunk_sources(half, chunk):
    if chunk < PAIRS:
        first = pl.multiple_of((PAIRS * half + chunk) * HEAD, HEAD)
        return ((1, first, HEAD, 0), (2, first, HEAD, HEAD))
    first = half * (QHEADS // 2 * HEAD) + (chunk - PAIRS) * CHUNK
    return ((0, pl.multiple_of(first, CHUNK), CHUNK, 0),)


def fused_kernel(
    hidden,
    gain_hbm,
    w_query,
    w_key,
    w_value,
    bias_query_hbm,
    bias_key_hbm,
    bias_value_hbm,
    kv_blocks_hbm,
    block_counts_hbm,
    out,
    gain,
    bias_query,
    bias_key,
    bias_value,
    kv_blocks,
    block_counts,
    raw,
    x_raw,
    scale_out,
    scale_in,
    gains,
    biases,
    cosine,
    sine,
    allowed,
    x_buf,
    w_buf,
    a1_out,
    a1_in,
    b1_out,
    b1_in,
    a2_out,
    a2_in,
    b2_out,
    b2_in,
    keep,
    own,
    kv_buf,
    q_buf,
    mask_buf,
    acc,
    tot,
    o_buf,
    o_in,
    h_sem,
    v_sem,
    c_snd,
    c_rcv,
    w_loc,
    w_snd,
    w_rcv,
    x_snd,
    x_rcv,
    f_snd,
    f_rcv,
    m_snd,
    m_rcv,
    s1_snd,
    s1_rcv,
    s2_snd,
    s2_rcv,
    kv_snd,
    kv_rcv,
    o_snd,
    o_rcv,
):
    me = lax.axis_index("dp")
    z = lax.axis_index("ctx")
    tops = lax.axis_size("ctx")
    core = lax.rem(me, 2)
    xpos = lax.rem(me // 2, 2)
    ypos = me // 4
    sibling = me + 1 - 2 * core
    xn = me + 2 - 4 * xpos
    yn = me + 4 - 8 * ypos
    dn = xn + 4 - 8 * ypos
    chunks = w_buf.shape[0]
    depth = w_query.shape[0]
    width = 2 * depth
    weights = (w_query, w_key, w_value)
    sends = []

    read = pltpu.make_async_copy(hidden.at[0], raw, h_sem)
    read.start()
    smalls = []
    for number, (source, place) in enumerate(
        (
            (gain_hbm, gain),
            (kv_blocks_hbm, kv_blocks),
            (block_counts_hbm, block_counts),
            (bias_query_hbm, bias_query),
            (bias_key_hbm, bias_key),
            (bias_value_hbm, bias_value),
        )
    ):
        smalls.append(pltpu.make_async_copy(source, place, v_sem.at[number]))
        smalls[-1].start()
    barrier = pltpu.get_barrier_semaphore()
    for peer in (sibling, xn, yn, dn):
        pl.semaphore_signal(barrier, inc=1, device_id=(peer, z), device_id_type=MESH)
    for step in range(1, tops):
        pl.semaphore_signal(barrier, inc=1, device_id=(me, lax.rem(z + step, tops)), device_id_type=MESH)

    def remote(src, dst, snd, rcv, dp, ctx):
        return pltpu.make_async_remote_copy(
            src_ref=src, dst_ref=dst, send_sem=snd, recv_sem=rcv, device_id=(dp, ctx), device_id_type=MESH
        )

    def launch(*args):
        copy = remote(*args)
        copy.start()
        sends.append(copy)

    locals_ = []
    rows = pl.ds(pl.multiple_of(core * depth, 64), depth)
    number = 0
    for chunk in range(chunks):
        for which, first, cols, place in chunk_sources(core, chunk):
            copy = pltpu.make_async_copy(
                weights[which].at[:, pl.ds(first, cols)],
                w_buf.at[chunk, rows, pl.ds(place, cols)],
                w_loc.at[number],
            )
            copy.start()
            locals_.append((chunk, copy))
            number += 1

    def columns_of(chip):
        return pl.ds(pl.multiple_of(chip * width, HEAD), width)

    relations = (dn, xn, yn)
    pl.semaphore_wait(barrier, 4 + tops - 1)
    for index in (1, 2, 0):
        peer = relations[index]
        source = hidden.at[0, :, columns_of(peer // 2)]
        launch(source, x_raw.at[index], x_snd.at[index], x_rcv.at[index], peer, z)

    number = 0
    for chunk in range(chunks):
        for which, first, cols, place in chunk_sources(1 - core, chunk):
            launch(
                weights[which].at[:, pl.ds(first, cols)],
                w_buf.at[chunk, rows, pl.ds(place, cols)],
                w_snd.at[number],
                w_rcv.at[number],
                sibling,
                z,
            )
            number += 1
    row = lax.broadcasted_iota(jnp.int32, (BLOCK, BLOCK), 0)
    column = lax.broadcasted_iota(jnp.int32, (BLOCK, BLOCK), 1)
    read.wait()
    floats = raw[...].astype(jnp.float32)
    scale = lax.rsqrt(jnp.mean(floats * floats, axis=-1, keepdims=True) + EPSILON)
    across = jnp.sum(jnp.where(row == column, scale, 0.0), axis=0, keepdims=True)
    scale_out[...] = jnp.broadcast_to(across, scale_out.shape)
    for index in (1, 2, 0):
        launch(scale_out, scale_in.at[index], c_snd.at[index], c_rcv.at[index], relations[index], z)
    smalls[0].wait()
    gains[...] = gain[...].astype(jnp.float32).reshape(1, -1)
    here = columns_of(me // 2)
    x_buf[me] = (raw[:, here].astype(jnp.float32) * scale * gains[:, here]).astype(jnp.bfloat16)
    launch(x_buf.at[me], x_buf.at[me], f_snd.at[3], f_rcv.at[3], sibling, z)

    for copy in smalls[1:]:
        copy.wait()
    for h in range(GROUP):
        for b in range(tops):
            blocks = kv_blocks[h, b : b + 1, :]
            count = block_counts[h : h + 1, b : b + 1]
            origin = lax.broadcasted_iota(jnp.int32, (tops, HEAD), 0)
            seen = jnp.zeros((tops, HEAD), jnp.float32)
            for slot in range(1, MAXB):
                hit = (blocks[:, slot : slot + 1] == origin) & (count > slot)
                seen = jnp.where(hit, 1.0, seen)
            allowed[b, h * tops : (h + 1) * tops, :] = seen
    for step in range(1, tops):
        peer = lax.rem(z + step, tops)
        launch(allowed.at[peer], mask_buf.at[z], m_snd.at[step - 1], m_rcv.at[step - 1], me, peer)
    mask_buf[z] = allowed[z]

    lane = lax.broadcasted_iota(jnp.int32, (BLOCK, HEAD), 1)
    token = lax.broadcasted_iota(jnp.int32, (BLOCK, HEAD), 0) + z * BLOCK
    exponent = lax.rem(lane, HEAD // 2).astype(jnp.float32) * (2.0 / HEAD)
    angles = token.astype(jnp.float32) * jnp.exp(exponent * (-math.log(THETA)))
    cosine[...] = jnp.cos(angles)
    sine[...] = jnp.where(lane < HEAD // 2, -jnp.sin(angles), jnp.sin(angles))
    starts = []
    for vector in (bias_query, bias_key, bias_value):
        first = starts[-1][1] if starts else 0
        starts.append((first, first + vector.shape[0]))
        biases[:, first : first + vector.shape[0]] = vector[...].astype(jnp.float32).reshape(1, -1)

    def bias_of(chunk):
        return jnp.concatenate(
            [
                biases[:, pl.ds(pl.multiple_of(starts[which][0] + first, HEAD), cols)]
                for which, first, cols, _ in chunk_sources(core, chunk)
            ],
            axis=1,
        )

    def sibling_of(device):
        return device + 1 - 2 * core

    def docs_of(index):
        peer = relations[index]
        remote(scale_out, scale_in.at[index], c_snd.at[index], c_rcv.at[index], peer, z).wait_recv()
        across = jnp.broadcast_to(scale_in[index, 0:1], (BLOCK, BLOCK))
        scale = jnp.sum(jnp.where(row == column, across, 0.0), axis=1, keepdims=True)
        remote(x_raw.at[index], x_raw.at[index], x_snd.at[index], x_rcv.at[index], peer, z).wait_recv()
        x_buf[peer] = (
            x_raw[index].astype(jnp.float32) * scale * gains[:, columns_of(me // 2)]
        ).astype(jnp.bfloat16)
        launch(x_buf.at[peer], x_buf.at[peer], f_snd.at[index], f_rcv.at[index], sibling, z)

    def forwarded(index, device):
        there = x_buf.at[sibling_of(device)]
        remote(there, there, f_snd.at[index], f_rcv.at[index], sibling, z).wait_recv()

    def wait_weights(chunk):
        other = pl.ds(pl.multiple_of((1 - core) * depth, 64), depth)
        for number, (owner, copy) in enumerate(locals_):
            if owner == chunk:
                copy.wait()
        number = 0
        for at in range(chunks):
            for _, _, cols, place in chunk_sources(core, at):
                if at == chunk:
                    there = w_buf.at[chunk, other, pl.ds(place, cols)]
                    remote(there, there, w_snd.at[number], w_rcv.at[number], sibling, z).wait_recv()
                number += 1

    def product(chunk, device):
        pair = x_buf[pl.ds(device // 2 * 2, 2)].reshape(2 * BLOCK, width)
        return jnp.dot(pair, w_buf[chunk], preferred_element_type=jnp.float32)

    def first_x(chunk):
        to_x = product(chunk, xn)
        a1_out[chunk, 0] = to_x[:BLOCK].astype(jnp.bfloat16)
        keep[chunk, 1] = to_x[BLOCK:]
        first_copy(0, 0, chunk).start()

    def first_y(chunk):
        to_y = product(chunk, yn)
        b1_out[chunk, 0] = to_y[BLOCK:].astype(jnp.bfloat16)
        keep[chunk, 0] = to_y[:BLOCK]
        first_copy(1, 0, chunk).start()

    def first_d(chunk):
        to_d = product(chunk, dn).astype(jnp.bfloat16)
        a1_out[chunk, 1] = to_d[:BLOCK]
        b1_out[chunk, 1] = to_d[BLOCK:]
        first_copy(0, 1, chunk).start()
        first_copy(1, 1, chunk).start()

    def first_own(chunk):
        mine = product(chunk, me)
        own[chunk, 0] = mine[:BLOCK]
        own[chunk, 1] = mine[BLOCK:]

    def first_copy(doc, piece, chunk):
        there, back = ((a1_out, a1_in), (b1_out, b1_in))[doc]
        return remote(
            there.at[chunk, piece],
            back.at[chunk, piece],
            s1_snd.at[doc, piece, chunk],
            s1_rcv.at[doc, piece, chunk],
            (xn, yn)[doc],
            z,
        )

    def multiply(chunk):
        wait_weights(chunk)
        first_d(chunk)
        first_x(chunk)
        first_y(chunk)
        first_own(chunk)

    def second(chunk):
        first_copy(0, 1, chunk).wait_recv()
        a2_out[chunk] = (keep[chunk, 0] + a1_in[chunk, 1].astype(jnp.float32)).astype(jnp.bfloat16)
        launch(a2_out.at[chunk], a2_in.at[chunk], s2_snd.at[0, chunk], s2_rcv.at[0, chunk], yn, z)
        first_copy(1, 1, chunk).wait_recv()
        b2_out[chunk] = (keep[chunk, 1] + b1_in[chunk, 1].astype(jnp.float32)).astype(jnp.bfloat16)
        launch(b2_out.at[chunk], b2_in.at[chunk], s2_snd.at[1, chunk], s2_rcv.at[1, chunk], xn, z)

    def rotate(head):
        return (head * cosine[...] + pltpu.roll(head, HEAD // 2, 1) * sine[...]).astype(jnp.bfloat16)

    def kv_copy(pair, origin):
        place = kv_buf.at[origin, pair]
        return remote(place, place, kv_snd.at[pair, origin], kv_rcv.at[pair, origin], me, lax.rem(z + 1, tops))

    def finish(chunk):
        both = ((a1_in, a2_in, a2_out, yn), (b1_in, b2_in, b2_out, xn))
        bias = bias_of(chunk)
        for doc, (first_in, second_in, second_out, peer) in enumerate(both):
            first_copy(doc, 0, chunk).wait_recv()
            remote(
                second_out.at[chunk], second_in.at[chunk], s2_snd.at[doc, chunk], s2_rcv.at[doc, chunk], peer, z
            ).wait_recv()
            total = (
                own[chunk, doc]
                + first_in[chunk, 0].astype(jnp.float32)
                + second_in[chunk].astype(jnp.float32)
                + bias
            )
            if chunk < PAIRS:
                kv_buf[z, chunk, doc, :, :HEAD] = rotate(total[:, :HEAD])
                kv_buf[z, chunk, doc, :, HEAD:] = total[:, HEAD:].astype(jnp.bfloat16)
            else:
                head = (chunk - PAIRS) * 2
                q_buf[doc, head] = rotate(total[:, :HEAD])
                q_buf[doc, head + 1] = rotate(total[:, HEAD:])
        if chunk < PAIRS:

            @pl.when(z < tops - 1)
            def _():
                kv_copy(chunk, z).start()

    def pass_on(pair, step):
        @pl.when(z >= step)
        def _():
            kv_copy(pair, z - step).wait_recv()

            @pl.when(z < tops - 1)
            def _():
                kv_copy(pair, z - step).start()

    def scores_of(queries, keys):
        return lax.dot_general(
            queries, keys, (((1,), (1,)), ((), ())), preferred_element_type=jnp.float32
        ) * HEAD ** (-0.5)

    causal = jnp.concatenate([column <= row] * 2, axis=0)

    def attend_own(chunk):
        at = chunk - PAIRS
        for doc in range(2):
            queries = q_buf[doc, 2 * at : 2 * at + 2].reshape(2 * BLOCK, HEAD)
            block = kv_buf[z, at // 2, doc]
            expo = jnp.where(causal, jnp.exp(scores_of(queries, block[:, :HEAD])), 0.0)
            tot[at, doc] = expo
            acc[at, doc] = jnp.dot(
                expo.astype(jnp.bfloat16), block[:, HEAD:], preferred_element_type=jnp.float32
            )

    def attend_below(chunk, step):
        at = chunk - PAIRS

        @pl.when(z >= step)
        def _():
            origin = z - step
            rows_of = [
                mask_buf[PAIRS * core + at // 2, pl.ds((at % 2 * 2 + h) * tops + origin, 1)]
                for h in range(2)
            ]
            seen = jnp.concatenate([jnp.broadcast_to(r, (BLOCK, BLOCK)) for r in rows_of], axis=0)
            for doc in range(2):
                queries = q_buf[doc, 2 * at : 2 * at + 2].reshape(2 * BLOCK, HEAD)
                block = kv_buf[origin, at // 2, doc]
                expo = jnp.where(seen > 0.5, jnp.exp(scores_of(queries, block[:, :HEAD])), 0.0)
                tot[at, doc] += expo
                acc[at, doc] += jnp.dot(
                    expo.astype(jnp.bfloat16), block[:, HEAD:], preferred_element_type=jnp.float32
                )

    def attend_end(chunk):
        at = chunk - PAIRS
        for doc in range(2):
            mixed = (acc[at, doc] / jnp.sum(tot[at, doc], axis=-1, keepdims=True)).astype(jnp.bfloat16)
            o_buf[doc, at, :, :HEAD] = mixed[:BLOCK]
            o_buf[doc, at, :, HEAD:] = mixed[BLOCK:]
        launch(o_buf.at[1 - core, at], o_in.at[at], o_snd.at[at], o_rcv.at[at], sibling, z)

    for chunk in range(3):
        wait_weights(chunk)
    forwarded(3, me)
    docs_of(1)
    docs_of(2)
    forwarded(1, xn)
    for chunk in range(3):
        first_x(chunk)
    forwarded(2, yn)
    for chunk in range(3):
        first_y(chunk)
    docs_of(0)
    first_own(0)
    forwarded(0, dn)
    first_d(0)
    first_d(1)
    first_own(1)
    second(0)
    second(1)
    first_d(2)
    finish(0)
    first_own(2)
    multiply(3)
    finish(1)
    second(2)
    pass_on(0, 1)
    multiply(4)
    for step in range(1, tops):
        here = mask_buf.at[lax.rem(z - step + tops, tops)]
        remote(here, here, m_snd.at[step - 1], m_rcv.at[step - 1], me, z).wait_recv()
    second(3)
    multiply(5)
    pass_on(1, 1)
    finish(2)
    attend_own(2)
    attend_below(2, 1)
    pass_on(0, 2)
    attend_below(2, 2)
    second(4)
    finish(3)
    attend_own(3)
    attend_below(3, 1)
    pass_on(1, 2)
    attend_below(3, 2)
    second(5)
    pass_on(0, 3)
    attend_below(2, 3)
    attend_end(2)
    attend_below(3, 3)
    attend_end(3)
    finish(4)
    attend_own(4)
    attend_below(4, 1)
    attend_below(4, 2)
    finish(5)
    attend_own(5)
    attend_below(5, 1)
    attend_below(5, 2)
    pass_on(1, 3)
    attend_below(4, 3)
    attend_end(4)
    attend_below(5, 3)
    attend_end(5)

    half = QHEADS // 2 * HEAD
    for at in range(chunks - PAIRS):
        first = pl.multiple_of(core * half + at * CHUNK, CHUNK)
        out[0, :, pl.ds(first, CHUNK)] = o_buf[core, at]
    for at in range(chunks - PAIRS):
        first = pl.multiple_of((1 - core) * half + at * CHUNK, CHUNK)
        remote(o_buf.at[core, at], o_in.at[at], o_snd.at[at], o_rcv.at[at], sibling, z).wait_recv()
        out[0, :, pl.ds(first, CHUNK)] = o_in[at]
    for doc in range(2):
        for piece in range(2):
            for chunk in range(chunks):
                first_copy(doc, piece, chunk).wait_send()
    for copy in sends:
        copy.wait_send()
    for pair in range(PAIRS):
        for step in range(tops):

            @pl.when((z >= step) & (z < tops - 1))
            def _():
                kv_copy(pair, z - step).wait_send()


def fused_body(
    hidden,
    norm_gain,
    w_query,
    w_key,
    w_value,
    bias_query,
    bias_key,
    bias_value,
    kv_blocks,
    block_counts,
):
    tops = lax.axis_size("ctx")
    rows = hidden.shape[1]
    depth = w_query.shape[0]
    chunks = PAIRS + QHEADS // 4
    bf16, f32 = jnp.bfloat16, jnp.float32
    vmem = pl.BlockSpec(memory_space=pltpu.VMEM)
    hbm = pl.BlockSpec(memory_space=pl.ANY)
    dma = pltpu.SemaphoreType.DMA
    copies = 2 * PAIRS + chunks - PAIRS
    return pl.pallas_call(
        fused_kernel,
        out_shape=pltpu.VMEM((1, rows, QHEADS * HEAD), bf16),
        in_specs=[hbm] * 10,
        out_specs=vmem,
        scratch_shapes=[
            pltpu.VMEM(norm_gain.shape, bf16),
            pltpu.VMEM(bias_query.shape, bf16),
            pltpu.VMEM(bias_key.shape, bf16),
            pltpu.VMEM(bias_value.shape, bf16),
            pltpu.VMEM(kv_blocks.shape, jnp.int32),
            pltpu.VMEM(block_counts.shape, jnp.int32),
            pltpu.VMEM((rows, hidden.shape[2]), bf16),
            pltpu.VMEM((3, rows, 2 * depth), bf16),
            pltpu.VMEM((8, rows), f32),
            pltpu.VMEM((3, 8, rows), f32),
            pltpu.VMEM((1, hidden.shape[2]), f32),
            pltpu.VMEM((1, (QHEADS + 2 * KVH) * HEAD), f32),
            pltpu.VMEM((rows, HEAD), f32),
            pltpu.VMEM((rows, HEAD), f32),
            pltpu.VMEM((tops, GROUP * tops, HEAD), f32),
            pltpu.VMEM((8, rows, 2 * depth), bf16),
            pltpu.VMEM((chunks, 2 * depth, CHUNK), bf16),
            pltpu.VMEM((chunks, 2, rows, CHUNK), bf16),
            pltpu.VMEM((chunks, 2, rows, CHUNK), bf16),
            pltpu.VMEM((chunks, 2, rows, CHUNK), bf16),
            pltpu.VMEM((chunks, 2, rows, CHUNK), bf16),
            pltpu.VMEM((chunks, rows, CHUNK), bf16),
            pltpu.VMEM((chunks, rows, CHUNK), bf16),
            pltpu.VMEM((chunks, rows, CHUNK), bf16),
            pltpu.VMEM((chunks, rows, CHUNK), bf16),
            pltpu.VMEM((chunks, 2, rows, CHUNK), f32),
            pltpu.VMEM((chunks, 2, rows, CHUNK), f32),
            pltpu.VMEM((tops, PAIRS, 2, rows, CHUNK), bf16),
            pltpu.VMEM((2, QHEADS // 2, rows, HEAD), bf16),
            pltpu.VMEM((tops, GROUP * tops, HEAD), f32),
            pltpu.VMEM((chunks - PAIRS, 2, 2 * rows, HEAD), f32),
            pltpu.VMEM((chunks - PAIRS, 2, 2 * rows, HEAD), f32),
            pltpu.VMEM((2, chunks - PAIRS, rows, CHUNK), bf16),
            pltpu.VMEM((chunks - PAIRS, rows, CHUNK), bf16),
            dma,
            dma((6,)),
            dma((3,)),
            dma((3,)),
            dma((copies,)),
            dma((copies,)),
            dma((copies,)),
            dma((3,)),
            dma((3,)),
            dma((4,)),
            dma((4,)),
            dma((tops - 1,)),
            dma((tops - 1,)),
            dma((2, 2, chunks)),
            dma((2, 2, chunks)),
            dma((2, chunks)),
            dma((2, chunks)),
            dma((PAIRS, tops)),
            dma((PAIRS, tops)),
            dma((chunks - PAIRS,)),
            dma((chunks - PAIRS,)),
        ],
        compiler_params=pltpu.CompilerParams(
            collective_id=0, has_side_effects=True, vmem_limit_bytes=56 * 1024 * 1024
        ),
    )(
        hidden,
        norm_gain,
        w_query,
        w_key,
        w_value,
        bias_query,
        bias_key,
        bias_value,
        kv_blocks,
        block_counts,
    )


def solution(mesh):
    placed = (
        P("dp", "ctx", None),
        P(),
        P("dp", None),
        P("dp", None),
        P("dp", None),
        P(),
        P(),
        P(),
        P("ctx", None, None),
        P("ctx", None),
    )
    plane = mesh.shape["dp"] == 8 and mesh.shape["ctx"] == MAXB
    return jax.shard_map(
        fused_body if plane else body, mesh=mesh, in_specs=placed, out_specs=P("dp", "ctx", None), check_vma=False
    )
```

```python
import math

import jax
import jax.numpy as jnp
from jax import lax
from jax.experimental import pallas as pl
from jax.experimental.pallas import tpu as pltpu
from jax.sharding import PartitionSpec as P

KVH = 4
HEAD = 128
QHEADS = 16
BLOCK = 128
MAXB = 4


EPSILON = 1e-06
THETA = 1000000.0


def rms_norm(tokens, norm_gain):
    floats = tokens.astype(jnp.float32)
    meansq = jnp.mean(floats * floats, axis=-1, keepdims=True)
    return (floats * lax.rsqrt(meansq + EPSILON) * norm_gain.astype(jnp.float32)).astype(
        jnp.bfloat16
    )


def rotary(heads_in, position):
    half_size = heads_in.shape[-1] // 2
    exponent = jnp.arange(half_size, dtype=jnp.float32) * (2.0 / heads_in.shape[-1])
    inverse = jnp.power(jnp.float32(THETA), -exponent)
    angles = position[:, None] * inverse[None, :]
    cosine = jnp.cos(angles)[:, None, :]
    sine = jnp.sin(angles)[:, None, :]
    first = heads_in[..., :half_size]
    second = heads_in[..., half_size:]
    return jnp.concatenate(
        [first * cosine - second * sine, second * cosine + first * sine], axis=-1
    )


def finish_heads(summed, bias, heads, position, rotate_it):
    shaped = (summed + bias.astype(jnp.float32)).reshape(summed.shape[0], heads, HEAD)
    if rotate_it:
        shaped = rotary(shaped, position)
    return shaped.astype(jnp.bfloat16)


def fold_rows(source, pieces):
    return tuple((jnp.dot(source, piece, preferred_element_type=jnp.float32) for piece in pieces))


def sparse_head(queries, key_rows, value_rows, blocks, counts):
    nblocks = queries.shape[0] // BLOCK
    query_tiles = queries.reshape(nblocks, BLOCK, HEAD)
    key_tiles = key_rows.reshape(nblocks, BLOCK, HEAD)[blocks].reshape(nblocks, MAXB * BLOCK, HEAD)
    value_tiles = value_rows.reshape(nblocks, BLOCK, HEAD)[blocks].reshape(
        nblocks, MAXB * BLOCK, HEAD
    )
    scores = jnp.einsum(
        "qih,qjh->qij", query_tiles, key_tiles, preferred_element_type=jnp.float32
    ) * HEAD ** (-0.5)
    column = jnp.arange(MAXB * BLOCK)
    slot_of = column // BLOCK
    inside = column % BLOCK
    row_pos = jnp.arange(BLOCK)
    allowed = (slot_of[None, None, :] < counts[:, None, None]) & (
        (slot_of[None, None, :] > 0) | (inside[None, None, :] <= row_pos[None, :, None])
    )
    expo = jnp.where(allowed, jnp.exp(scores), jnp.float32(0.0))
    totals = jnp.sum(expo, axis=-1)
    probs = expo.astype(jnp.bfloat16)
    mixed = (
        jnp.einsum("qij,qjh->qih", probs, value_tiles, preferred_element_type=jnp.float32)
        / totals[..., None]
    )
    return mixed.astype(jnp.bfloat16).reshape(nblocks * BLOCK, HEAD)


def one_head(packed):
    return sparse_head(packed[0], packed[1], packed[2], packed[3], packed[4])


def body(
    hidden,
    norm_gain,
    w_query,
    w_key,
    w_value,
    bias_query,
    bias_key,
    bias_value,
    kv_blocks,
    block_counts,
):
    groups = lax.axis_size("ctx")
    device = lax.axis_index("ctx")
    tokens = hidden[0]
    local_rows = tokens.shape[0]
    seq_len = local_rows * groups
    heads_here = QHEADS // groups
    kv_here = KVH // groups
    width_query = heads_here * HEAD
    width_pair = kv_here * HEAD
    normed = rms_norm(tokens, norm_gain)
    parts = lax.axis_size("dp")
    depth = w_query.shape[0]
    gathered = lax.all_to_all(
        normed.reshape(local_rows, parts, depth), "dp", split_axis=1, concat_axis=0, tiled=True
    ).reshape(parts * local_rows, depth)
    weights = jnp.concatenate([w_key, w_value, w_query], axis=1)
    partial = jnp.dot(gathered, weights, preferred_element_type=jnp.float32).astype(jnp.bfloat16)
    summed = lax.psum_scatter(partial, "dp", scatter_dimension=0, tiled=True).astype(jnp.float32)
    width = KVH * HEAD
    sum_key, sum_value, sum_query = (
        summed[:, :width],
        summed[:, width : 2 * width],
        summed[:, 2 * width :],
    )
    position = (device * local_rows + jnp.arange(local_rows, dtype=jnp.int32)).astype(jnp.float32)
    queries = finish_heads(sum_query, bias_query, QHEADS, position, True)
    key_rows = finish_heads(sum_key, bias_key, KVH, position, True)
    value_rows = finish_heads(sum_value, bias_value, KVH, position, False)
    query_send = queries.reshape(local_rows, groups, width_query)
    pair_send = jnp.concatenate([key_rows, value_rows], axis=2)
    query_got, pair_got = (
        lax.all_to_all(query_send, "ctx", split_axis=1, concat_axis=0, tiled=True),
        lax.all_to_all(pair_send, "ctx", split_axis=1, concat_axis=0, tiled=True),
    )
    queries = query_got.reshape(seq_len, heads_here, HEAD)
    key_rows = pair_got[:, 0, :width_pair].reshape(seq_len, kv_here, HEAD)
    value_rows = pair_got[:, 0, width_pair:].reshape(seq_len, kv_here, HEAD)
    group = heads_here // kv_here
    key_rows = jnp.repeat(key_rows, group, axis=1)
    value_rows = jnp.repeat(value_rows, group, axis=1)
    mixed = lax.map(
        one_head,
        (
            queries.transpose(1, 0, 2),
            key_rows.transpose(1, 0, 2),
            value_rows.transpose(1, 0, 2),
            kv_blocks,
            block_counts,
        ),
    )
    result = mixed.transpose(1, 0, 2).reshape(seq_len, 1, width_query)
    returned = lax.all_to_all(result, "ctx", split_axis=0, concat_axis=1, tiled=True)
    return returned.reshape(1, local_rows, QHEADS * HEAD)


MESH = pl.DeviceIdType.MESH
CHUNK = 2 * HEAD
GROUP = QHEADS // KVH
PAIRS = KVH // 2


def chunk_sources(half, chunk):
    if chunk < PAIRS:
        first = pl.multiple_of((PAIRS * half + chunk) * HEAD, HEAD)
        return ((1, first, HEAD, 0), (2, first, HEAD, HEAD))
    first = half * (QHEADS // 2 * HEAD) + (chunk - PAIRS) * CHUNK
    return ((0, pl.multiple_of(first, CHUNK), CHUNK, 0),)


def fused_kernel(
    hidden,
    gain_hbm,
    w_query,
    w_key,
    w_value,
    bias_query_hbm,
    bias_key_hbm,
    bias_value_hbm,
    kv_blocks_hbm,
    block_counts_hbm,
    out,
    gain,
    bias_query,
    bias_key,
    bias_value,
    kv_blocks,
    block_counts,
    raw,
    x_raw,
    scale_out,
    scale_in,
    gains,
    biases,
    cosine,
    sine,
    allowed,
    x_buf,
    w_buf,
    a1_out,
    a1_in,
    b1_out,
    b1_in,
    a2_out,
    a2_in,
    b2_out,
    b2_in,
    keep,
    own,
    kv_buf,
    q_buf,
    mask_buf,
    acc,
    tot,
    o_buf,
    o_in,
    h_sem,
    v_sem,
    c_snd,
    c_rcv,
    w_loc,
    w_snd,
    w_rcv,
    x_snd,
    x_rcv,
    f_snd,
    f_rcv,
    m_snd,
    m_rcv,
    s1_snd,
    s1_rcv,
    s2_snd,
    s2_rcv,
    kv_snd,
    kv_rcv,
    o_snd,
    o_rcv,
):
    me = lax.axis_index("dp")
    z = lax.axis_index("ctx")
    tops = lax.axis_size("ctx")
    core = lax.rem(me, 2)
    xpos = lax.rem(me // 2, 2)
    ypos = me // 4
    sibling = me + 1 - 2 * core
    xn = me + 2 - 4 * xpos
    yn = me + 4 - 8 * ypos
    dn = xn + 4 - 8 * ypos
    chunks = w_buf.shape[0]
    depth = w_query.shape[0]
    width = 2 * depth
    weights = (w_query, w_key, w_value)
    sends = []

    read = pltpu.make_async_copy(hidden.at[0], raw, h_sem)
    read.start()
    smalls = []
    for number, (source, place) in enumerate(
        (
            (gain_hbm, gain),
            (kv_blocks_hbm, kv_blocks),
            (block_counts_hbm, block_counts),
            (bias_query_hbm, bias_query),
            (bias_key_hbm, bias_key),
            (bias_value_hbm, bias_value),
        )
    ):
        smalls.append(pltpu.make_async_copy(source, place, v_sem.at[number]))
        smalls[-1].start()
    barrier = pltpu.get_barrier_semaphore()
    for peer in (sibling, xn, yn, dn):
        pl.semaphore_signal(barrier, inc=1, device_id=(peer, z), device_id_type=MESH)
    for step in range(1, tops):
        pl.semaphore_signal(barrier, inc=1, device_id=(me, lax.rem(z + step, tops)), device_id_type=MESH)

    def remote(src, dst, snd, rcv, dp, ctx):
        return pltpu.make_async_remote_copy(
            src_ref=src, dst_ref=dst, send_sem=snd, recv_sem=rcv, device_id=(dp, ctx), device_id_type=MESH
        )

    def launch(*args):
        copy = remote(*args)
        copy.start()
        sends.append(copy)

    locals_ = []
    rows = pl.ds(pl.multiple_of(core * depth, 64), depth)
    number = 0
    for chunk in range(chunks):
        for which, first, cols, place in chunk_sources(core, chunk):
            copy = pltpu.make_async_copy(
                weights[which].at[:, pl.ds(first, cols)],
                w_buf.at[chunk, rows, pl.ds(place, cols)],
                w_loc.at[number],
            )
            copy.start()
            locals_.append((chunk, copy))
            number += 1

    def columns_of(chip):
        return pl.ds(pl.multiple_of(chip * width, HEAD), width)

    relations = (dn, xn, yn)
    pl.semaphore_wait(barrier, 4 + tops - 1)

    def send_raw(index):
        peer = relations[index]
        source = hidden.at[0, :, columns_of(peer // 2)]
        launch(source, x_raw.at[index], x_snd.at[index], x_rcv.at[index], peer, z)

    send_raw(1)
    send_raw(2)

    def send_weights(wanted):
        number = 0
        for chunk in range(chunks):
            for which, first, cols, place in chunk_sources(1 - core, chunk):
                if chunk in wanted:
                    launch(
                        weights[which].at[:, pl.ds(first, cols)],
                        w_buf.at[chunk, rows, pl.ds(place, cols)],
                        w_snd.at[number],
                        w_rcv.at[number],
                        sibling,
                        z,
                    )
                number += 1

    row = lax.broadcasted_iota(jnp.int32, (BLOCK, BLOCK), 0)
    column = lax.broadcasted_iota(jnp.int32, (BLOCK, BLOCK), 1)
    read.wait()
    floats = raw[...].astype(jnp.float32)
    scale = lax.rsqrt(jnp.mean(floats * floats, axis=-1, keepdims=True) + EPSILON)
    across = jnp.sum(jnp.where(row == column, scale, 0.0), axis=0, keepdims=True)
    scale_out[...] = jnp.broadcast_to(across, scale_out.shape)
    for index in (1, 2, 0):
        launch(scale_out, scale_in.at[index], c_snd.at[index], c_rcv.at[index], relations[index], z)
    send_raw(0)
    smalls[0].wait()
    gains[...] = gain[...].astype(jnp.float32).reshape(1, -1)
    here = columns_of(me // 2)
    x_buf[me] = (raw[:, here].astype(jnp.float32) * scale * gains[:, here]).astype(jnp.bfloat16)
    launch(x_buf.at[me], x_buf.at[me], f_snd.at[3], f_rcv.at[3], sibling, z)

    send_weights((0, 1, 2))
    for copy in smalls[1:]:
        copy.wait()
    for h in range(GROUP):
        for b in range(tops):
            blocks = kv_blocks[h, b : b + 1, :]
            count = block_counts[h : h + 1, b : b + 1]
            origin = lax.broadcasted_iota(jnp.int32, (tops, HEAD), 0)
            seen = jnp.zeros((tops, HEAD), jnp.float32)
            for slot in range(1, MAXB):
                hit = (blocks[:, slot : slot + 1] == origin) & (count > slot)
                seen = jnp.where(hit, 1.0, seen)
            allowed[b, h * tops : (h + 1) * tops, :] = seen
    for step in range(1, tops):
        peer = lax.rem(z + step, tops)
        launch(allowed.at[peer], mask_buf.at[z], m_snd.at[step - 1], m_rcv.at[step - 1], me, peer)
    mask_buf[z] = allowed[z]

    lane = lax.broadcasted_iota(jnp.int32, (BLOCK, HEAD), 1)
    token = lax.broadcasted_iota(jnp.int32, (BLOCK, HEAD), 0) + z * BLOCK
    exponent = lax.rem(lane, HEAD // 2).astype(jnp.float32) * (2.0 / HEAD)
    angles = token.astype(jnp.float32) * jnp.exp(exponent * (-math.log(THETA)))
    cosine[...] = jnp.cos(angles)
    sine[...] = jnp.where(lane < HEAD // 2, -jnp.sin(angles), jnp.sin(angles))
    starts = []
    for vector in (bias_query, bias_key, bias_value):
        first = starts[-1][1] if starts else 0
        starts.append((first, first + vector.shape[0]))
        biases[:, first : first + vector.shape[0]] = vector[...].astype(jnp.float32).reshape(1, -1)

    def bias_of(chunk):
        return jnp.concatenate(
            [
                biases[:, pl.ds(pl.multiple_of(starts[which][0] + first, HEAD), cols)]
                for which, first, cols, _ in chunk_sources(core, chunk)
            ],
            axis=1,
        )

    def sibling_of(device):
        return device + 1 - 2 * core

    def docs_of(index):
        peer = relations[index]
        remote(scale_out, scale_in.at[index], c_snd.at[index], c_rcv.at[index], peer, z).wait_recv()
        across = jnp.broadcast_to(scale_in[index, 0:1], (BLOCK, BLOCK))
        scale = jnp.sum(jnp.where(row == column, across, 0.0), axis=1, keepdims=True)
        remote(x_raw.at[index], x_raw.at[index], x_snd.at[index], x_rcv.at[index], peer, z).wait_recv()
        x_buf[peer] = (
            x_raw[index].astype(jnp.float32) * scale * gains[:, columns_of(me // 2)]
        ).astype(jnp.bfloat16)
        launch(x_buf.at[peer], x_buf.at[peer], f_snd.at[index], f_rcv.at[index], sibling, z)

    def forwarded(index, device):
        there = x_buf.at[sibling_of(device)]
        remote(there, there, f_snd.at[index], f_rcv.at[index], sibling, z).wait_recv()

    def wait_weights(chunk):
        other = pl.ds(pl.multiple_of((1 - core) * depth, 64), depth)
        for number, (owner, copy) in enumerate(locals_):
            if owner == chunk:
                copy.wait()
        number = 0
        for at in range(chunks):
            for _, _, cols, place in chunk_sources(core, at):
                if at == chunk:
                    there = w_buf.at[chunk, other, pl.ds(place, cols)]
                    remote(there, there, w_snd.at[number], w_rcv.at[number], sibling, z).wait_recv()
                number += 1

    def product(chunk, device):
        pair = x_buf[pl.ds(device // 2 * 2, 2)].reshape(2 * BLOCK, width)
        return jnp.dot(pair, w_buf[chunk], preferred_element_type=jnp.float32)

    def first_x(chunk):
        to_x = product(chunk, xn)
        a1_out[chunk, 0] = to_x[:BLOCK].astype(jnp.bfloat16)
        keep[chunk, 1] = to_x[BLOCK:]

    def first_y(chunk):
        to_y = product(chunk, yn)
        b1_out[chunk, 0] = to_y[BLOCK:].astype(jnp.bfloat16)
        keep[chunk, 0] = to_y[:BLOCK]

    def first_d(chunk):
        to_d = product(chunk, dn).astype(jnp.bfloat16)
        a1_out[chunk, 1] = to_d[:BLOCK]
        b1_out[chunk, 1] = to_d[BLOCK:]

    def first_own(chunk):
        mine = product(chunk, me)
        own[chunk, 0] = mine[:BLOCK]
        own[chunk, 1] = mine[BLOCK:]

    def send_first(chunk, piece):
        first_copy(0, piece, chunk).start()
        first_copy(1, piece, chunk).start()

    def first_copy(doc, piece, chunk):
        there, back = ((a1_out, a1_in), (b1_out, b1_in))[doc]
        return remote(
            there.at[chunk, piece],
            back.at[chunk, piece],
            s1_snd.at[doc, piece, chunk],
            s1_rcv.at[doc, piece, chunk],
            (xn, yn)[doc],
            z,
        )

    def multiply(chunk):
        first_d(chunk)
        first_x(chunk)
        first_y(chunk)
        first_own(chunk)

    def second(chunk):
        first_copy(0, 1, chunk).wait_recv()
        a2_out[chunk] = (keep[chunk, 0] + a1_in[chunk, 1].astype(jnp.float32)).astype(jnp.bfloat16)
        launch(a2_out.at[chunk], a2_in.at[chunk], s2_snd.at[0, chunk], s2_rcv.at[0, chunk], yn, z)
        first_copy(1, 1, chunk).wait_recv()
        b2_out[chunk] = (keep[chunk, 1] + b1_in[chunk, 1].astype(jnp.float32)).astype(jnp.bfloat16)
        launch(b2_out.at[chunk], b2_in.at[chunk], s2_snd.at[1, chunk], s2_rcv.at[1, chunk], xn, z)

    def rotate(head):
        return (head * cosine[...] + pltpu.roll(head, HEAD // 2, 1) * sine[...]).astype(jnp.bfloat16)

    def kv_copy(pair, origin):
        place = kv_buf.at[origin, pair]
        return remote(place, place, kv_snd.at[pair, origin], kv_rcv.at[pair, origin], me, lax.rem(z + 1, tops))

    def finish(chunk):
        both = ((a1_in, a2_in, a2_out, yn), (b1_in, b2_in, b2_out, xn))
        bias = bias_of(chunk)
        for doc, (first_in, second_in, second_out, peer) in enumerate(both):
            first_copy(doc, 0, chunk).wait_recv()
            remote(
                second_out.at[chunk], second_in.at[chunk], s2_snd.at[doc, chunk], s2_rcv.at[doc, chunk], peer, z
            ).wait_recv()
            total = (
                own[chunk, doc]
                + first_in[chunk, 0].astype(jnp.float32)
                + second_in[chunk].astype(jnp.float32)
                + bias
            )
            if chunk < PAIRS:
                kv_buf[z, chunk, doc, :, :HEAD] = rotate(total[:, :HEAD])
                kv_buf[z, chunk, doc, :, HEAD:] = total[:, HEAD:].astype(jnp.bfloat16)
            else:
                head = (chunk - PAIRS) * 2
                q_buf[doc, head] = rotate(total[:, :HEAD])
                q_buf[doc, head + 1] = rotate(total[:, HEAD:])
        if chunk < PAIRS:

            @pl.when(z < tops - 1)
            def _():
                kv_copy(chunk, z).start()

    def pass_on(pair, step):
        @pl.when(z >= step)
        def _():
            kv_copy(pair, z - step).wait_recv()

            @pl.when(z < tops - 1)
            def _():
                kv_copy(pair, z - step).start()

    def scores_of(queries, keys):
        return lax.dot_general(
            queries, keys, (((1,), (1,)), ((), ())), preferred_element_type=jnp.float32
        ) * HEAD ** (-0.5)

    causal = jnp.concatenate([column <= row] * 2, axis=0)

    def attend_own(chunk):
        at = chunk - PAIRS
        for doc in range(2):
            queries = q_buf[doc, 2 * at : 2 * at + 2].reshape(2 * BLOCK, HEAD)
            block = kv_buf[z, at // 2, doc]
            expo = jnp.where(causal, jnp.exp(scores_of(queries, block[:, :HEAD])), 0.0)
            tot[at, doc] = expo
            acc[at, doc] = jnp.dot(
                expo.astype(jnp.bfloat16), block[:, HEAD:], preferred_element_type=jnp.float32
            )

    def attend_below(chunk, step):
        at = chunk - PAIRS

        @pl.when(z >= step)
        def _():
            origin = z - step
            rows_of = [
                mask_buf[PAIRS * core + at // 2, pl.ds((at % 2 * 2 + h) * tops + origin, 1)]
                for h in range(2)
            ]
            seen = jnp.concatenate([jnp.broadcast_to(r, (BLOCK, BLOCK)) for r in rows_of], axis=0)
            for doc in range(2):
                queries = q_buf[doc, 2 * at : 2 * at + 2].reshape(2 * BLOCK, HEAD)
                block = kv_buf[origin, at // 2, doc]
                expo = jnp.where(seen > 0.5, jnp.exp(scores_of(queries, block[:, :HEAD])), 0.0)
                tot[at, doc] += expo
                acc[at, doc] += jnp.dot(
                    expo.astype(jnp.bfloat16), block[:, HEAD:], preferred_element_type=jnp.float32
                )

    def attend_end(chunk):
        at = chunk - PAIRS
        for doc in range(2):
            mixed = (acc[at, doc] / jnp.sum(tot[at, doc], axis=-1, keepdims=True)).astype(jnp.bfloat16)
            o_buf[doc, at, :, :HEAD] = mixed[:BLOCK]
            o_buf[doc, at, :, HEAD:] = mixed[BLOCK:]
        launch(o_buf.at[1 - core, at], o_in.at[at], o_snd.at[at], o_rcv.at[at], sibling, z)

    for chunk in range(3):
        wait_weights(chunk)
    forwarded(3, me)
    docs_of(1)
    docs_of(2)
    forwarded(1, xn)
    for chunk in range(3):
        first_x(chunk)
        first_copy(0, 0, chunk).start()
    forwarded(2, yn)
    for chunk in range(3):
        first_y(chunk)
        first_copy(1, 0, chunk).start()
    first_own(0)
    docs_of(0)
    send_weights(range(3, chunks))
    first_own(1)
    forwarded(0, dn)
    for chunk in range(2):
        first_d(chunk)
        send_first(chunk, 1)
    first_d(2)
    first_own(2)
    second(0)
    for chunk in range(3, chunks):
        wait_weights(chunk)
    second(1)
    send_first(2, 1)
    finish(0)
    multiply(3)
    send_first(3, 1)
    send_first(3, 0)
    finish(1)
    multiply(4)
    second(2)
    send_first(4, 1)
    send_first(4, 0)
    pass_on(0, 1)
    multiply(5)
    for step in range(1, tops):
        here = mask_buf.at[lax.rem(z - step + tops, tops)]
        remote(here, here, m_snd.at[step - 1], m_rcv.at[step - 1], me, z).wait_recv()
    second(3)
    send_first(5, 1)
    send_first(5, 0)
    pass_on(1, 1)
    finish(2)
    attend_own(2)
    attend_below(2, 1)
    pass_on(0, 2)
    attend_below(2, 2)
    second(4)
    finish(3)
    attend_own(3)
    attend_below(3, 1)
    pass_on(1, 2)
    attend_below(3, 2)
    second(5)
    pass_on(0, 3)
    attend_below(2, 3)
    attend_end(2)
    attend_below(3, 3)
    attend_end(3)
    finish(4)
    attend_own(4)
    attend_below(4, 1)
    attend_below(4, 2)
    pass_on(1, 3)
    attend_below(4, 3)
    attend_end(4)
    finish(5)
    attend_own(5)
    attend_below(5, 1)
    attend_below(5, 2)
    attend_below(5, 3)
    attend_end(5)

    half = QHEADS // 2 * HEAD
    for at in range(chunks - PAIRS):
        first = pl.multiple_of(core * half + at * CHUNK, CHUNK)
        out[0, :, pl.ds(first, CHUNK)] = o_buf[core, at]
    for at in range(chunks - PAIRS):
        first = pl.multiple_of((1 - core) * half + at * CHUNK, CHUNK)
        remote(o_buf.at[core, at], o_in.at[at], o_snd.at[at], o_rcv.at[at], sibling, z).wait_recv()
        out[0, :, pl.ds(first, CHUNK)] = o_in[at]
    for doc in range(2):
        for piece in range(2):
            for chunk in range(chunks):
                first_copy(doc, piece, chunk).wait_send()
    for copy in sends:
        copy.wait_send()
    for pair in range(PAIRS):
        for step in range(tops):

            @pl.when((z >= step) & (z < tops - 1))
            def _():
                kv_copy(pair, z - step).wait_send()


def fused_body(
    hidden,
    norm_gain,
    w_query,
    w_key,
    w_value,
    bias_query,
    bias_key,
    bias_value,
    kv_blocks,
    block_counts,
):
    tops = lax.axis_size("ctx")
    rows = hidden.shape[1]
    depth = w_query.shape[0]
    chunks = PAIRS + QHEADS // 4
    bf16, f32 = jnp.bfloat16, jnp.float32
    vmem = pl.BlockSpec(memory_space=pltpu.VMEM)
    hbm = pl.BlockSpec(memory_space=pl.ANY)
    dma = pltpu.SemaphoreType.DMA
    copies = 2 * PAIRS + chunks - PAIRS
    return pl.pallas_call(
        fused_kernel,
        out_shape=pltpu.VMEM((1, rows, QHEADS * HEAD), bf16),
        in_specs=[hbm] * 10,
        out_specs=vmem,
        scratch_shapes=[
            pltpu.VMEM(norm_gain.shape, bf16),
            pltpu.VMEM(bias_query.shape, bf16),
            pltpu.VMEM(bias_key.shape, bf16),
            pltpu.VMEM(bias_value.shape, bf16),
            pltpu.VMEM(kv_blocks.shape, jnp.int32),
            pltpu.VMEM(block_counts.shape, jnp.int32),
            pltpu.VMEM((rows, hidden.shape[2]), bf16),
            pltpu.VMEM((3, rows, 2 * depth), bf16),
            pltpu.VMEM((8, rows), f32),
            pltpu.VMEM((3, 8, rows), f32),
            pltpu.VMEM((1, hidden.shape[2]), f32),
            pltpu.VMEM((1, (QHEADS + 2 * KVH) * HEAD), f32),
            pltpu.VMEM((rows, HEAD), f32),
            pltpu.VMEM((rows, HEAD), f32),
            pltpu.VMEM((tops, GROUP * tops, HEAD), f32),
            pltpu.VMEM((8, rows, 2 * depth), bf16),
            pltpu.VMEM((chunks, 2 * depth, CHUNK), bf16),
            pltpu.VMEM((chunks, 2, rows, CHUNK), bf16),
            pltpu.VMEM((chunks, 2, rows, CHUNK), bf16),
            pltpu.VMEM((chunks, 2, rows, CHUNK), bf16),
            pltpu.VMEM((chunks, 2, rows, CHUNK), bf16),
            pltpu.VMEM((chunks, rows, CHUNK), bf16),
            pltpu.VMEM((chunks, rows, CHUNK), bf16),
            pltpu.VMEM((chunks, rows, CHUNK), bf16),
            pltpu.VMEM((chunks, rows, CHUNK), bf16),
            pltpu.VMEM((chunks, 2, rows, CHUNK), f32),
            pltpu.VMEM((chunks, 2, rows, CHUNK), f32),
            pltpu.VMEM((tops, PAIRS, 2, rows, CHUNK), bf16),
            pltpu.VMEM((2, QHEADS // 2, rows, HEAD), bf16),
            pltpu.VMEM((tops, GROUP * tops, HEAD), f32),
            pltpu.VMEM((chunks - PAIRS, 2, 2 * rows, HEAD), f32),
            pltpu.VMEM((chunks - PAIRS, 2, 2 * rows, HEAD), f32),
            pltpu.VMEM((2, chunks - PAIRS, rows, CHUNK), bf16),
            pltpu.VMEM((chunks - PAIRS, rows, CHUNK), bf16),
            dma,
            dma((6,)),
            dma((3,)),
            dma((3,)),
            dma((copies,)),
            dma((copies,)),
            dma((copies,)),
            dma((3,)),
            dma((3,)),
            dma((4,)),
            dma((4,)),
            dma((tops - 1,)),
            dma((tops - 1,)),
            dma((2, 2, chunks)),
            dma((2, 2, chunks)),
            dma((2, chunks)),
            dma((2, chunks)),
            dma((PAIRS, tops)),
            dma((PAIRS, tops)),
            dma((chunks - PAIRS,)),
            dma((chunks - PAIRS,)),
        ],
        compiler_params=pltpu.CompilerParams(
            collective_id=0, has_side_effects=True, vmem_limit_bytes=56 * 1024 * 1024
        ),
    )(
        hidden,
        norm_gain,
        w_query,
        w_key,
        w_value,
        bias_query,
        bias_key,
        bias_value,
        kv_blocks,
        block_counts,
    )


def solution(mesh):
    placed = (
        P("dp", "ctx", None),
        P(),
        P("dp", None),
        P("dp", None),
        P("dp", None),
        P(),
        P(),
        P(),
        P("ctx", None, None),
        P("ctx", None),
    )
    plane = mesh.shape["dp"] == 8 and mesh.shape["ctx"] == MAXB
    return jax.shard_map(
        fused_body if plane else body, mesh=mesh, in_specs=placed, out_specs=P("dp", "ctx", None), check_vma=False
    )
```

```python
import math

import jax
import jax.numpy as jnp
from jax import lax
from jax.experimental import pallas as pl
from jax.experimental.pallas import tpu as pltpu
from jax.sharding import PartitionSpec as P

KVH = 4
HEAD = 128
QHEADS = 16
BLOCK = 128
MAXB = 4


EPSILON = 1e-06
THETA = 1000000.0


def rms_norm(tokens, norm_gain):
    floats = tokens.astype(jnp.float32)
    meansq = jnp.mean(floats * floats, axis=-1, keepdims=True)
    return (floats * lax.rsqrt(meansq + EPSILON) * norm_gain.astype(jnp.float32)).astype(
        jnp.bfloat16
    )


def rotary(heads_in, position):
    half_size = heads_in.shape[-1] // 2
    exponent = jnp.arange(half_size, dtype=jnp.float32) * (2.0 / heads_in.shape[-1])
    inverse = jnp.power(jnp.float32(THETA), -exponent)
    angles = position[:, None] * inverse[None, :]
    cosine = jnp.cos(angles)[:, None, :]
    sine = jnp.sin(angles)[:, None, :]
    first = heads_in[..., :half_size]
    second = heads_in[..., half_size:]
    return jnp.concatenate(
        [first * cosine - second * sine, second * cosine + first * sine], axis=-1
    )


def finish_heads(summed, bias, heads, position, rotate_it):
    shaped = (summed + bias.astype(jnp.float32)).reshape(summed.shape[0], heads, HEAD)
    if rotate_it:
        shaped = rotary(shaped, position)
    return shaped.astype(jnp.bfloat16)


def fold_rows(source, pieces):
    return tuple((jnp.dot(source, piece, preferred_element_type=jnp.float32) for piece in pieces))


def sparse_head(queries, key_rows, value_rows, blocks, counts):
    nblocks = queries.shape[0] // BLOCK
    query_tiles = queries.reshape(nblocks, BLOCK, HEAD)
    key_tiles = key_rows.reshape(nblocks, BLOCK, HEAD)[blocks].reshape(nblocks, MAXB * BLOCK, HEAD)
    value_tiles = value_rows.reshape(nblocks, BLOCK, HEAD)[blocks].reshape(
        nblocks, MAXB * BLOCK, HEAD
    )
    scores = jnp.einsum(
        "qih,qjh->qij", query_tiles, key_tiles, preferred_element_type=jnp.float32
    ) * HEAD ** (-0.5)
    column = jnp.arange(MAXB * BLOCK)
    slot_of = column // BLOCK
    inside = column % BLOCK
    row_pos = jnp.arange(BLOCK)
    allowed = (slot_of[None, None, :] < counts[:, None, None]) & (
        (slot_of[None, None, :] > 0) | (inside[None, None, :] <= row_pos[None, :, None])
    )
    expo = jnp.where(allowed, jnp.exp(scores), jnp.float32(0.0))
    totals = jnp.sum(expo, axis=-1)
    probs = expo.astype(jnp.bfloat16)
    mixed = (
        jnp.einsum("qij,qjh->qih", probs, value_tiles, preferred_element_type=jnp.float32)
        / totals[..., None]
    )
    return mixed.astype(jnp.bfloat16).reshape(nblocks * BLOCK, HEAD)


def one_head(packed):
    return sparse_head(packed[0], packed[1], packed[2], packed[3], packed[4])


def body(
    hidden,
    norm_gain,
    w_query,
    w_key,
    w_value,
    bias_query,
    bias_key,
    bias_value,
    kv_blocks,
    block_counts,
):
    groups = lax.axis_size("ctx")
    device = lax.axis_index("ctx")
    tokens = hidden[0]
    local_rows = tokens.shape[0]
    seq_len = local_rows * groups
    heads_here = QHEADS // groups
    kv_here = KVH // groups
    width_query = heads_here * HEAD
    width_pair = kv_here * HEAD
    normed = rms_norm(tokens, norm_gain)
    parts = lax.axis_size("dp")
    depth = w_query.shape[0]
    gathered = lax.all_to_all(
        normed.reshape(local_rows, parts, depth), "dp", split_axis=1, concat_axis=0, tiled=True
    ).reshape(parts * local_rows, depth)
    weights = jnp.concatenate([w_key, w_value, w_query], axis=1)
    partial = jnp.dot(gathered, weights, preferred_element_type=jnp.float32).astype(jnp.bfloat16)
    summed = lax.psum_scatter(partial, "dp", scatter_dimension=0, tiled=True).astype(jnp.float32)
    width = KVH * HEAD
    sum_key, sum_value, sum_query = (
        summed[:, :width],
        summed[:, width : 2 * width],
        summed[:, 2 * width :],
    )
    position = (device * local_rows + jnp.arange(local_rows, dtype=jnp.int32)).astype(jnp.float32)
    queries = finish_heads(sum_query, bias_query, QHEADS, position, True)
    key_rows = finish_heads(sum_key, bias_key, KVH, position, True)
    value_rows = finish_heads(sum_value, bias_value, KVH, position, False)
    query_send = queries.reshape(local_rows, groups, width_query)
    pair_send = jnp.concatenate([key_rows, value_rows], axis=2)
    query_got, pair_got = (
        lax.all_to_all(query_send, "ctx", split_axis=1, concat_axis=0, tiled=True),
        lax.all_to_all(pair_send, "ctx", split_axis=1, concat_axis=0, tiled=True),
    )
    queries = query_got.reshape(seq_len, heads_here, HEAD)
    key_rows = pair_got[:, 0, :width_pair].reshape(seq_len, kv_here, HEAD)
    value_rows = pair_got[:, 0, width_pair:].reshape(seq_len, kv_here, HEAD)
    group = heads_here // kv_here
    key_rows = jnp.repeat(key_rows, group, axis=1)
    value_rows = jnp.repeat(value_rows, group, axis=1)
    mixed = lax.map(
        one_head,
        (
            queries.transpose(1, 0, 2),
            key_rows.transpose(1, 0, 2),
            value_rows.transpose(1, 0, 2),
            kv_blocks,
            block_counts,
        ),
    )
    result = mixed.transpose(1, 0, 2).reshape(seq_len, 1, width_query)
    returned = lax.all_to_all(result, "ctx", split_axis=0, concat_axis=1, tiled=True)
    return returned.reshape(1, local_rows, QHEADS * HEAD)


MESH = pl.DeviceIdType.MESH
CHUNK = 2 * HEAD
GROUP = QHEADS // KVH
PAIRS = KVH // 2


def chunk_sources(half, chunk):
    if chunk < PAIRS:
        first = pl.multiple_of((PAIRS * half + chunk) * HEAD, HEAD)
        return ((1, first, HEAD, 0), (2, first, HEAD, HEAD))
    first = half * (QHEADS // 2 * HEAD) + (chunk - PAIRS) * CHUNK
    return ((0, pl.multiple_of(first, CHUNK), CHUNK, 0),)


def fused_kernel(
    hidden,
    gain_hbm,
    w_query,
    w_key,
    w_value,
    bias_query_hbm,
    bias_key_hbm,
    bias_value_hbm,
    kv_blocks_hbm,
    block_counts_hbm,
    out,
    gain,
    bias_query,
    bias_key,
    bias_value,
    kv_blocks,
    block_counts,
    raw,
    x_raw,
    scale_out,
    scale_in,
    gains,
    biases,
    cosine,
    sine,
    allowed,
    x_buf,
    w_buf,
    a1_out,
    a1_in,
    b1_out,
    b1_in,
    a2_out,
    a2_in,
    b2_out,
    b2_in,
    keep,
    own,
    kv_buf,
    q_buf,
    mask_buf,
    acc,
    tot,
    o_buf,
    o_in,
    h_sem,
    v_sem,
    c_snd,
    c_rcv,
    w_loc,
    w_snd,
    w_rcv,
    x_snd,
    x_rcv,
    f_snd,
    f_rcv,
    m_snd,
    m_rcv,
    s1_snd,
    s1_rcv,
    s2_snd,
    s2_rcv,
    kv_snd,
    kv_rcv,
    o_snd,
    o_rcv,
):
    me = lax.axis_index("dp")
    z = lax.axis_index("ctx")
    tops = lax.axis_size("ctx")
    core = lax.rem(me, 2)
    xpos = lax.rem(me // 2, 2)
    ypos = me // 4
    sibling = me + 1 - 2 * core
    xn = me + 2 - 4 * xpos
    yn = me + 4 - 8 * ypos
    dn = xn + 4 - 8 * ypos
    chunks = w_buf.shape[0]
    depth = w_query.shape[0]
    width = 2 * depth
    weights = (w_query, w_key, w_value)
    sends = []

    read = pltpu.make_async_copy(hidden.at[0], raw, h_sem)
    read.start()
    smalls = []
    for number, (source, place) in enumerate(
        (
            (gain_hbm, gain),
            (kv_blocks_hbm, kv_blocks),
            (block_counts_hbm, block_counts),
            (bias_query_hbm, bias_query),
            (bias_key_hbm, bias_key),
            (bias_value_hbm, bias_value),
        )
    ):
        smalls.append(pltpu.make_async_copy(source, place, v_sem.at[number]))
        smalls[-1].start()
    barrier = pltpu.get_barrier_semaphore()
    for peer in (sibling, xn, yn, dn):
        pl.semaphore_signal(barrier, inc=1, device_id=(peer, z), device_id_type=MESH)
    for step in range(1, tops):
        pl.semaphore_signal(barrier, inc=1, device_id=(me, lax.rem(z + step, tops)), device_id_type=MESH)

    def remote(src, dst, snd, rcv, dp, ctx):
        return pltpu.make_async_remote_copy(
            src_ref=src, dst_ref=dst, send_sem=snd, recv_sem=rcv, device_id=(dp, ctx), device_id_type=MESH
        )

    def launch(*args):
        copy = remote(*args)
        copy.start()
        sends.append(copy)

    locals_ = []
    rows = pl.ds(pl.multiple_of(core * depth, 64), depth)
    number = 0
    for chunk in range(chunks):
        for which, first, cols, place in chunk_sources(core, chunk):
            copy = pltpu.make_async_copy(
                weights[which].at[:, pl.ds(first, cols)],
                w_buf.at[chunk, rows, pl.ds(place, cols)],
                w_loc.at[number],
            )
            copy.start()
            locals_.append((chunk, copy))
            number += 1

    def columns_of(chip):
        return pl.ds(pl.multiple_of(chip * width, HEAD), width)

    relations = (dn, xn, yn)
    pl.semaphore_wait(barrier, 4 + tops - 1)

    def send_raw(index):
        peer = relations[index]
        source = hidden.at[0, :, columns_of(peer // 2)]
        launch(source, x_raw.at[index], x_snd.at[index], x_rcv.at[index], peer, z)

    send_raw(1)
    send_raw(2)

    def send_weights(wanted):
        number = 0
        for chunk in range(chunks):
            for which, first, cols, place in chunk_sources(1 - core, chunk):
                if chunk in wanted:
                    launch(
                        weights[which].at[:, pl.ds(first, cols)],
                        w_buf.at[chunk, rows, pl.ds(place, cols)],
                        w_snd.at[number],
                        w_rcv.at[number],
                        sibling,
                        z,
                    )
                number += 1

    row = lax.broadcasted_iota(jnp.int32, (BLOCK, BLOCK), 0)
    column = lax.broadcasted_iota(jnp.int32, (BLOCK, BLOCK), 1)
    read.wait()
    floats = raw[...].astype(jnp.float32)
    scale = lax.rsqrt(jnp.mean(floats * floats, axis=-1, keepdims=True) + EPSILON)
    across = jnp.sum(jnp.where(row == column, scale, 0.0), axis=0, keepdims=True)
    scale_out[...] = jnp.broadcast_to(across, scale_out.shape)
    for index in (1, 2, 0):
        launch(scale_out, scale_in.at[index], c_snd.at[index], c_rcv.at[index], relations[index], z)
    send_raw(0)
    smalls[0].wait()
    gains[...] = gain[...].astype(jnp.float32).reshape(1, -1)
    here = columns_of(me // 2)
    x_buf[me] = (raw[:, here].astype(jnp.float32) * scale * gains[:, here]).astype(jnp.bfloat16)
    launch(x_buf.at[me], x_buf.at[me], f_snd.at[3], f_rcv.at[3], sibling, z)

    send_weights((0, 1, 2))
    for copy in smalls[1:]:
        copy.wait()
    for h in range(GROUP):
        for b in range(tops):
            blocks = kv_blocks[h, b : b + 1, :]
            count = block_counts[h : h + 1, b : b + 1]
            origin = lax.broadcasted_iota(jnp.int32, (tops, HEAD), 0)
            seen = jnp.zeros((tops, HEAD), jnp.float32)
            for slot in range(1, MAXB):
                hit = (blocks[:, slot : slot + 1] == origin) & (count > slot)
                seen = jnp.where(hit, 1.0, seen)
            allowed[b, h * tops : (h + 1) * tops, :] = seen
    for step in range(1, tops):
        peer = lax.rem(z + step, tops)
        launch(allowed.at[peer], mask_buf.at[z], m_snd.at[step - 1], m_rcv.at[step - 1], me, peer)
    mask_buf[z] = allowed[z]

    lane = lax.broadcasted_iota(jnp.int32, (BLOCK, HEAD), 1)
    token = lax.broadcasted_iota(jnp.int32, (BLOCK, HEAD), 0) + z * BLOCK
    exponent = lax.rem(lane, HEAD // 2).astype(jnp.float32) * (2.0 / HEAD)
    angles = token.astype(jnp.float32) * jnp.exp(exponent * (-math.log(THETA)))
    cosine[...] = jnp.cos(angles)
    sine[...] = jnp.where(lane < HEAD // 2, -jnp.sin(angles), jnp.sin(angles))
    starts = []
    for vector in (bias_query, bias_key, bias_value):
        first = starts[-1][1] if starts else 0
        starts.append((first, first + vector.shape[0]))
        biases[:, first : first + vector.shape[0]] = vector[...].astype(jnp.float32).reshape(1, -1)

    def bias_of(chunk):
        return jnp.concatenate(
            [
                biases[:, pl.ds(pl.multiple_of(starts[which][0] + first, HEAD), cols)]
                for which, first, cols, _ in chunk_sources(core, chunk)
            ],
            axis=1,
        )

    def sibling_of(device):
        return device + 1 - 2 * core

    def docs_of(index):
        peer = relations[index]
        remote(scale_out, scale_in.at[index], c_snd.at[index], c_rcv.at[index], peer, z).wait_recv()
        across = jnp.broadcast_to(scale_in[index, 0:1], (BLOCK, BLOCK))
        scale = jnp.sum(jnp.where(row == column, across, 0.0), axis=1, keepdims=True)
        remote(x_raw.at[index], x_raw.at[index], x_snd.at[index], x_rcv.at[index], peer, z).wait_recv()
        x_buf[peer] = (
            x_raw[index].astype(jnp.float32) * scale * gains[:, columns_of(me // 2)]
        ).astype(jnp.bfloat16)
        launch(x_buf.at[peer], x_buf.at[peer], f_snd.at[index], f_rcv.at[index], sibling, z)

    def forwarded(index, device):
        there = x_buf.at[sibling_of(device)]
        remote(there, there, f_snd.at[index], f_rcv.at[index], sibling, z).wait_recv()

    def wait_weights(chunk):
        other = pl.ds(pl.multiple_of((1 - core) * depth, 64), depth)
        for number, (owner, copy) in enumerate(locals_):
            if owner == chunk:
                copy.wait()
        number = 0
        for at in range(chunks):
            for _, _, cols, place in chunk_sources(core, at):
                if at == chunk:
                    there = w_buf.at[chunk, other, pl.ds(place, cols)]
                    remote(there, there, w_snd.at[number], w_rcv.at[number], sibling, z).wait_recv()
                number += 1

    def product(chunk, device):
        pair = x_buf[pl.ds(device // 2 * 2, 2)].reshape(2 * BLOCK, width)
        return jnp.dot(pair, w_buf[chunk], preferred_element_type=jnp.float32)

    def first_x(chunk):
        to_x = product(chunk, xn)
        a1_out[chunk, 0] = to_x[:BLOCK].astype(jnp.bfloat16)
        keep[chunk, 1] = to_x[BLOCK:]

    def first_y(chunk):
        to_y = product(chunk, yn)
        b1_out[chunk, 0] = to_y[BLOCK:].astype(jnp.bfloat16)
        keep[chunk, 0] = to_y[:BLOCK]

    def first_d(chunk):
        to_d = product(chunk, dn).astype(jnp.bfloat16)
        a1_out[chunk, 1] = to_d[:BLOCK]
        b1_out[chunk, 1] = to_d[BLOCK:]

    def first_own(chunk):
        mine = product(chunk, me)
        own[chunk, 0] = mine[:BLOCK]
        own[chunk, 1] = mine[BLOCK:]

    def send_first(chunk, piece):
        first_copy(0, piece, chunk).start()
        first_copy(1, piece, chunk).start()

    def first_copy(doc, piece, chunk):
        there, back = ((a1_out, a1_in), (b1_out, b1_in))[doc]
        return remote(
            there.at[chunk, piece],
            back.at[chunk, piece],
            s1_snd.at[doc, piece, chunk],
            s1_rcv.at[doc, piece, chunk],
            (xn, yn)[doc],
            z,
        )

    def multiply(chunk):
        first_d(chunk)
        first_x(chunk)
        first_y(chunk)
        first_own(chunk)

    def second(chunk):
        first_copy(0, 1, chunk).wait_recv()
        a2_out[chunk] = (keep[chunk, 0] + a1_in[chunk, 1].astype(jnp.float32)).astype(jnp.bfloat16)
        launch(a2_out.at[chunk], a2_in.at[chunk], s2_snd.at[0, chunk], s2_rcv.at[0, chunk], yn, z)
        first_copy(1, 1, chunk).wait_recv()
        b2_out[chunk] = (keep[chunk, 1] + b1_in[chunk, 1].astype(jnp.float32)).astype(jnp.bfloat16)
        launch(b2_out.at[chunk], b2_in.at[chunk], s2_snd.at[1, chunk], s2_rcv.at[1, chunk], xn, z)

    def rotate(head):
        return (head * cosine[...] + pltpu.roll(head, HEAD // 2, 1) * sine[...]).astype(jnp.bfloat16)

    def kv_copy(pair, origin):
        place = kv_buf.at[origin, pair]
        return remote(place, place, kv_snd.at[pair, origin], kv_rcv.at[pair, origin], me, lax.rem(z + 1, tops))

    def finish(chunk):
        both = ((a1_in, a2_in, a2_out, yn), (b1_in, b2_in, b2_out, xn))
        bias = bias_of(chunk)
        for doc, (first_in, second_in, second_out, peer) in enumerate(both):
            first_copy(doc, 0, chunk).wait_recv()
            remote(
                second_out.at[chunk], second_in.at[chunk], s2_snd.at[doc, chunk], s2_rcv.at[doc, chunk], peer, z
            ).wait_recv()
            total = (
                own[chunk, doc]
                + first_in[chunk, 0].astype(jnp.float32)
                + second_in[chunk].astype(jnp.float32)
                + bias
            )
            if chunk < PAIRS:
                kv_buf[z, chunk, doc, :, :HEAD] = rotate(total[:, :HEAD])
                kv_buf[z, chunk, doc, :, HEAD:] = total[:, HEAD:].astype(jnp.bfloat16)
            else:
                head = (chunk - PAIRS) * 2
                q_buf[doc, head] = rotate(total[:, :HEAD])
                q_buf[doc, head + 1] = rotate(total[:, HEAD:])
        if chunk < PAIRS:

            @pl.when(z < tops - 1)
            def _():
                kv_copy(chunk, z).start()

    def pass_on(pair, step):
        @pl.when(z >= step)
        def _():
            kv_copy(pair, z - step).wait_recv()

            @pl.when(z < tops - 1)
            def _():
                kv_copy(pair, z - step).start()

    def scores_of(queries, keys):
        return lax.dot_general(
            queries, keys, (((1,), (1,)), ((), ())), preferred_element_type=jnp.float32
        ) * HEAD ** (-0.5)

    causal = jnp.concatenate([column <= row] * 2, axis=0)

    def attend_own(chunk):
        at = chunk - PAIRS
        for doc in range(2):
            queries = q_buf[doc, 2 * at : 2 * at + 2].reshape(2 * BLOCK, HEAD)
            block = kv_buf[z, at // 2, doc]
            expo = jnp.where(causal, jnp.exp(scores_of(queries, block[:, :HEAD])), 0.0)
            tot[at, doc] = expo
            acc[at, doc] = jnp.dot(
                expo.astype(jnp.bfloat16), block[:, HEAD:], preferred_element_type=jnp.float32
            )

    def attend_below(chunk, step):
        at = chunk - PAIRS

        @pl.when(z >= step)
        def _():
            origin = z - step
            rows_of = [
                mask_buf[PAIRS * core + at // 2, pl.ds((at % 2 * 2 + h) * tops + origin, 1)]
                for h in range(2)
            ]
            seen = jnp.concatenate([jnp.broadcast_to(r, (BLOCK, BLOCK)) for r in rows_of], axis=0)
            for doc in range(2):
                queries = q_buf[doc, 2 * at : 2 * at + 2].reshape(2 * BLOCK, HEAD)
                block = kv_buf[origin, at // 2, doc]
                expo = jnp.where(seen > 0.5, jnp.exp(scores_of(queries, block[:, :HEAD])), 0.0)
                tot[at, doc] += expo
                acc[at, doc] += jnp.dot(
                    expo.astype(jnp.bfloat16), block[:, HEAD:], preferred_element_type=jnp.float32
                )

    def attend_end(chunk):
        at = chunk - PAIRS
        for doc in range(2):
            mixed = (acc[at, doc] / jnp.sum(tot[at, doc], axis=-1, keepdims=True)).astype(jnp.bfloat16)
            o_buf[doc, at, :, :HEAD] = mixed[:BLOCK]
            o_buf[doc, at, :, HEAD:] = mixed[BLOCK:]
        launch(o_buf.at[1 - core, at], o_in.at[at], o_snd.at[at], o_rcv.at[at], sibling, z)

    for chunk in range(3):
        wait_weights(chunk)
    forwarded(3, me)
    docs_of(1)
    docs_of(2)
    forwarded(1, xn)
    for chunk in range(3):
        first_x(chunk)
        first_copy(0, 0, chunk).start()
    forwarded(2, yn)
    for chunk in range(3):
        first_y(chunk)
        first_copy(1, 0, chunk).start()
    first_own(0)
    docs_of(0)
    send_weights(range(3, chunks))
    first_own(1)
    forwarded(0, dn)
    for chunk in range(2):
        first_d(chunk)
        send_first(chunk, 1)
    first_d(2)
    first_own(2)
    second(0)
    for chunk in range(3, chunks):
        wait_weights(chunk)
    second(1)
    send_first(2, 1)
    finish(0)
    multiply(3)
    send_first(3, 1)
    send_first(3, 0)
    finish(1)
    multiply(4)
    second(2)
    send_first(4, 1)
    send_first(4, 0)
    pass_on(0, 1)
    multiply(5)
    for step in range(1, tops):
        here = mask_buf.at[lax.rem(z - step + tops, tops)]
        remote(here, here, m_snd.at[step - 1], m_rcv.at[step - 1], me, z).wait_recv()
    pass_on(1, 1)
    second(3)
    send_first(5, 1)
    send_first(5, 0)
    pass_on(0, 2)
    finish(2)
    attend_own(2)
    attend_below(2, 1)
    attend_below(2, 2)
    pass_on(1, 2)
    second(4)
    finish(3)
    attend_own(3)
    attend_below(3, 1)
    attend_below(3, 2)
    pass_on(0, 3)
    attend_below(2, 3)
    attend_end(2)
    second(5)
    attend_below(3, 3)
    attend_end(3)
    finish(4)
    attend_own(4)
    attend_below(4, 1)
    attend_below(4, 2)
    pass_on(1, 3)
    attend_below(4, 3)
    attend_end(4)
    finish(5)
    attend_own(5)
    attend_below(5, 1)
    attend_below(5, 2)
    attend_below(5, 3)
    attend_end(5)

    half = QHEADS // 2 * HEAD
    for at in range(chunks - PAIRS):
        first = pl.multiple_of(core * half + at * CHUNK, CHUNK)
        out[0, :, pl.ds(first, CHUNK)] = o_buf[core, at]
    for at in range(chunks - PAIRS):
        first = pl.multiple_of((1 - core) * half + at * CHUNK, CHUNK)
        remote(o_buf.at[core, at], o_in.at[at], o_snd.at[at], o_rcv.at[at], sibling, z).wait_recv()
        out[0, :, pl.ds(first, CHUNK)] = o_in[at]
    for doc in range(2):
        for piece in range(2):
            for chunk in range(chunks):
                first_copy(doc, piece, chunk).wait_send()
    for copy in sends:
        copy.wait_send()
    for pair in range(PAIRS):
        for step in range(tops):

            @pl.when((z >= step) & (z < tops - 1))
            def _():
                kv_copy(pair, z - step).wait_send()


def fused_body(
    hidden,
    norm_gain,
    w_query,
    w_key,
    w_value,
    bias_query,
    bias_key,
    bias_value,
    kv_blocks,
    block_counts,
):
    tops = lax.axis_size("ctx")
    rows = hidden.shape[1]
    depth = w_query.shape[0]
    chunks = PAIRS + QHEADS // 4
    bf16, f32 = jnp.bfloat16, jnp.float32
    vmem = pl.BlockSpec(memory_space=pltpu.VMEM)
    hbm = pl.BlockSpec(memory_space=pl.ANY)
    dma = pltpu.SemaphoreType.DMA
    copies = 2 * PAIRS + chunks - PAIRS
    return pl.pallas_call(
        fused_kernel,
        out_shape=pltpu.VMEM((1, rows, QHEADS * HEAD), bf16),
        in_specs=[hbm] * 10,
        out_specs=vmem,
        scratch_shapes=[
            pltpu.VMEM(norm_gain.shape, bf16),
            pltpu.VMEM(bias_query.shape, bf16),
            pltpu.VMEM(bias_key.shape, bf16),
            pltpu.VMEM(bias_value.shape, bf16),
            pltpu.VMEM(kv_blocks.shape, jnp.int32),
            pltpu.VMEM(block_counts.shape, jnp.int32),
            pltpu.VMEM((rows, hidden.shape[2]), bf16),
            pltpu.VMEM((3, rows, 2 * depth), bf16),
            pltpu.VMEM((8, rows), f32),
            pltpu.VMEM((3, 8, rows), f32),
            pltpu.VMEM((1, hidden.shape[2]), f32),
            pltpu.VMEM((1, (QHEADS + 2 * KVH) * HEAD), f32),
            pltpu.VMEM((rows, HEAD), f32),
            pltpu.VMEM((rows, HEAD), f32),
            pltpu.VMEM((tops, GROUP * tops, HEAD), f32),
            pltpu.VMEM((8, rows, 2 * depth), bf16),
            pltpu.VMEM((chunks, 2 * depth, CHUNK), bf16),
            pltpu.VMEM((chunks, 2, rows, CHUNK), bf16),
            pltpu.VMEM((chunks, 2, rows, CHUNK), bf16),
            pltpu.VMEM((chunks, 2, rows, CHUNK), bf16),
            pltpu.VMEM((chunks, 2, rows, CHUNK), bf16),
            pltpu.VMEM((chunks, rows, CHUNK), bf16),
            pltpu.VMEM((chunks, rows, CHUNK), bf16),
            pltpu.VMEM((chunks, rows, CHUNK), bf16),
            pltpu.VMEM((chunks, rows, CHUNK), bf16),
            pltpu.VMEM((chunks, 2, rows, CHUNK), f32),
            pltpu.VMEM((chunks, 2, rows, CHUNK), f32),
            pltpu.VMEM((tops, PAIRS, 2, rows, CHUNK), bf16),
            pltpu.VMEM((2, QHEADS // 2, rows, HEAD), bf16),
            pltpu.VMEM((tops, GROUP * tops, HEAD), f32),
            pltpu.VMEM((chunks - PAIRS, 2, 2 * rows, HEAD), f32),
            pltpu.VMEM((chunks - PAIRS, 2, 2 * rows, HEAD), f32),
            pltpu.VMEM((2, chunks - PAIRS, rows, CHUNK), bf16),
            pltpu.VMEM((chunks - PAIRS, rows, CHUNK), bf16),
            dma,
            dma((6,)),
            dma((3,)),
            dma((3,)),
            dma((copies,)),
            dma((copies,)),
            dma((copies,)),
            dma((3,)),
            dma((3,)),
            dma((4,)),
            dma((4,)),
            dma((tops - 1,)),
            dma((tops - 1,)),
            dma((2, 2, chunks)),
            dma((2, 2, chunks)),
            dma((2, chunks)),
            dma((2, chunks)),
            dma((PAIRS, tops)),
            dma((PAIRS, tops)),
            dma((chunks - PAIRS,)),
            dma((chunks - PAIRS,)),
        ],
        compiler_params=pltpu.CompilerParams(
            collective_id=0, has_side_effects=True, vmem_limit_bytes=56 * 1024 * 1024
        ),
    )(
        hidden,
        norm_gain,
        w_query,
        w_key,
        w_value,
        bias_query,
        bias_key,
        bias_value,
        kv_blocks,
        block_counts,
    )


def solution(mesh):
    placed = (
        P("dp", "ctx", None),
        P(),
        P("dp", None),
        P("dp", None),
        P("dp", None),
        P(),
        P(),
        P(),
        P("ctx", None, None),
        P("ctx", None),
    )
    plane = mesh.shape["dp"] == 8 and mesh.shape["ctx"] == MAXB
    return jax.shard_map(
        fused_body if plane else body, mesh=mesh, in_specs=placed, out_specs=P("dp", "ctx", None), check_vma=False
    )
```

```python
import math

import jax
import jax.numpy as jnp
from jax import lax
from jax.experimental import pallas as pl
from jax.experimental.pallas import tpu as pltpu
from jax.sharding import PartitionSpec as P

KVH = 4
HEAD = 128
QHEADS = 16
BLOCK = 128
MAXB = 4


EPSILON = 1e-06
THETA = 1000000.0


def rms_norm(tokens, norm_gain):
    floats = tokens.astype(jnp.float32)
    meansq = jnp.mean(floats * floats, axis=-1, keepdims=True)
    return (floats * lax.rsqrt(meansq + EPSILON) * norm_gain.astype(jnp.float32)).astype(
        jnp.bfloat16
    )


def rotary(heads_in, position):
    half_size = heads_in.shape[-1] // 2
    exponent = jnp.arange(half_size, dtype=jnp.float32) * (2.0 / heads_in.shape[-1])
    inverse = jnp.power(jnp.float32(THETA), -exponent)
    angles = position[:, None] * inverse[None, :]
    cosine = jnp.cos(angles)[:, None, :]
    sine = jnp.sin(angles)[:, None, :]
    first = heads_in[..., :half_size]
    second = heads_in[..., half_size:]
    return jnp.concatenate(
        [first * cosine - second * sine, second * cosine + first * sine], axis=-1
    )


def finish_heads(summed, bias, heads, position, rotate_it):
    shaped = (summed + bias.astype(jnp.float32)).reshape(summed.shape[0], heads, HEAD)
    if rotate_it:
        shaped = rotary(shaped, position)
    return shaped.astype(jnp.bfloat16)


def fold_rows(source, pieces):
    return tuple((jnp.dot(source, piece, preferred_element_type=jnp.float32) for piece in pieces))


def sparse_head(queries, key_rows, value_rows, blocks, counts):
    nblocks = queries.shape[0] // BLOCK
    query_tiles = queries.reshape(nblocks, BLOCK, HEAD)
    key_tiles = key_rows.reshape(nblocks, BLOCK, HEAD)[blocks].reshape(nblocks, MAXB * BLOCK, HEAD)
    value_tiles = value_rows.reshape(nblocks, BLOCK, HEAD)[blocks].reshape(
        nblocks, MAXB * BLOCK, HEAD
    )
    scores = jnp.einsum(
        "qih,qjh->qij", query_tiles, key_tiles, preferred_element_type=jnp.float32
    ) * HEAD ** (-0.5)
    column = jnp.arange(MAXB * BLOCK)
    slot_of = column // BLOCK
    inside = column % BLOCK
    row_pos = jnp.arange(BLOCK)
    allowed = (slot_of[None, None, :] < counts[:, None, None]) & (
        (slot_of[None, None, :] > 0) | (inside[None, None, :] <= row_pos[None, :, None])
    )
    expo = jnp.where(allowed, jnp.exp(scores), jnp.float32(0.0))
    totals = jnp.sum(expo, axis=-1)
    probs = expo.astype(jnp.bfloat16)
    mixed = (
        jnp.einsum("qij,qjh->qih", probs, value_tiles, preferred_element_type=jnp.float32)
        / totals[..., None]
    )
    return mixed.astype(jnp.bfloat16).reshape(nblocks * BLOCK, HEAD)


def one_head(packed):
    return sparse_head(packed[0], packed[1], packed[2], packed[3], packed[4])


def body(
    hidden,
    norm_gain,
    w_query,
    w_key,
    w_value,
    bias_query,
    bias_key,
    bias_value,
    kv_blocks,
    block_counts,
):
    groups = lax.axis_size("ctx")
    device = lax.axis_index("ctx")
    tokens = hidden[0]
    local_rows = tokens.shape[0]
    seq_len = local_rows * groups
    heads_here = QHEADS // groups
    kv_here = KVH // groups
    width_query = heads_here * HEAD
    width_pair = kv_here * HEAD
    normed = rms_norm(tokens, norm_gain)
    parts = lax.axis_size("dp")
    depth = w_query.shape[0]
    gathered = lax.all_to_all(
        normed.reshape(local_rows, parts, depth), "dp", split_axis=1, concat_axis=0, tiled=True
    ).reshape(parts * local_rows, depth)
    weights = jnp.concatenate([w_key, w_value, w_query], axis=1)
    partial = jnp.dot(gathered, weights, preferred_element_type=jnp.float32).astype(jnp.bfloat16)
    summed = lax.psum_scatter(partial, "dp", scatter_dimension=0, tiled=True).astype(jnp.float32)
    width = KVH * HEAD
    sum_key, sum_value, sum_query = (
        summed[:, :width],
        summed[:, width : 2 * width],
        summed[:, 2 * width :],
    )
    position = (device * local_rows + jnp.arange(local_rows, dtype=jnp.int32)).astype(jnp.float32)
    queries = finish_heads(sum_query, bias_query, QHEADS, position, True)
    key_rows = finish_heads(sum_key, bias_key, KVH, position, True)
    value_rows = finish_heads(sum_value, bias_value, KVH, position, False)
    query_send = queries.reshape(local_rows, groups, width_query)
    pair_send = jnp.concatenate([key_rows, value_rows], axis=2)
    query_got, pair_got = (
        lax.all_to_all(query_send, "ctx", split_axis=1, concat_axis=0, tiled=True),
        lax.all_to_all(pair_send, "ctx", split_axis=1, concat_axis=0, tiled=True),
    )
    queries = query_got.reshape(seq_len, heads_here, HEAD)
    key_rows = pair_got[:, 0, :width_pair].reshape(seq_len, kv_here, HEAD)
    value_rows = pair_got[:, 0, width_pair:].reshape(seq_len, kv_here, HEAD)
    group = heads_here // kv_here
    key_rows = jnp.repeat(key_rows, group, axis=1)
    value_rows = jnp.repeat(value_rows, group, axis=1)
    mixed = lax.map(
        one_head,
        (
            queries.transpose(1, 0, 2),
            key_rows.transpose(1, 0, 2),
            value_rows.transpose(1, 0, 2),
            kv_blocks,
            block_counts,
        ),
    )
    result = mixed.transpose(1, 0, 2).reshape(seq_len, 1, width_query)
    returned = lax.all_to_all(result, "ctx", split_axis=0, concat_axis=1, tiled=True)
    return returned.reshape(1, local_rows, QHEADS * HEAD)


MESH = pl.DeviceIdType.MESH
CHUNK = 2 * HEAD
GROUP = QHEADS // KVH
PAIRS = KVH // 2


def chunk_sources(half, chunk):
    if chunk < PAIRS:
        first = pl.multiple_of((PAIRS * half + chunk) * HEAD, HEAD)
        return ((1, first, HEAD, 0), (2, first, HEAD, HEAD))
    first = half * (QHEADS // 2 * HEAD) + (chunk - PAIRS) * CHUNK
    return ((0, pl.multiple_of(first, CHUNK), CHUNK, 0),)


def fused_kernel(
    hidden,
    gain_hbm,
    w_query,
    w_key,
    w_value,
    bias_query_hbm,
    bias_key_hbm,
    bias_value_hbm,
    kv_blocks_hbm,
    block_counts_hbm,
    out,
    gain,
    bias_query,
    bias_key,
    bias_value,
    kv_blocks,
    block_counts,
    raw,
    x_raw,
    scale_out,
    scale_in,
    gains,
    biases,
    cosine,
    sine,
    allowed,
    x_buf,
    w_buf,
    a1_out,
    a1_in,
    b1_out,
    b1_in,
    a2_out,
    a2_in,
    b2_out,
    b2_in,
    keep,
    own,
    kv_buf,
    q_buf,
    mask_buf,
    acc,
    tot,
    o_buf,
    o_in,
    h_sem,
    v_sem,
    c_snd,
    c_rcv,
    w_loc,
    w_snd,
    w_rcv,
    x_snd,
    x_rcv,
    f_snd,
    f_rcv,
    m_snd,
    m_rcv,
    s1_snd,
    s1_rcv,
    s2_snd,
    s2_rcv,
    kv_snd,
    kv_rcv,
    o_snd,
    o_rcv,
):
    me = lax.axis_index("dp")
    z = lax.axis_index("ctx")
    tops = lax.axis_size("ctx")
    core = lax.rem(me, 2)
    xpos = lax.rem(me // 2, 2)
    ypos = me // 4
    sibling = me + 1 - 2 * core
    xn = me + 2 - 4 * xpos
    yn = me + 4 - 8 * ypos
    dn = xn + 4 - 8 * ypos
    chunks = w_buf.shape[0]
    depth = w_query.shape[0]
    width = 2 * depth
    weights = (w_query, w_key, w_value)
    sends = []

    read = pltpu.make_async_copy(hidden.at[0], raw, h_sem)
    read.start()
    smalls = []
    for number, (source, place) in enumerate(
        (
            (gain_hbm, gain),
            (kv_blocks_hbm, kv_blocks),
            (block_counts_hbm, block_counts),
            (bias_query_hbm, bias_query),
            (bias_key_hbm, bias_key),
            (bias_value_hbm, bias_value),
        )
    ):
        smalls.append(pltpu.make_async_copy(source, place, v_sem.at[number]))
        smalls[-1].start()
    barrier = pltpu.get_barrier_semaphore()
    for peer in (sibling, xn, yn, dn):
        pl.semaphore_signal(barrier, inc=1, device_id=(peer, z), device_id_type=MESH)
    for step in range(1, tops):
        pl.semaphore_signal(barrier, inc=1, device_id=(me, lax.rem(z + step, tops)), device_id_type=MESH)

    def remote(src, dst, snd, rcv, dp, ctx):
        return pltpu.make_async_remote_copy(
            src_ref=src, dst_ref=dst, send_sem=snd, recv_sem=rcv, device_id=(dp, ctx), device_id_type=MESH
        )

    def launch(*args):
        copy = remote(*args)
        copy.start()
        sends.append(copy)

    locals_ = []
    rows = pl.ds(pl.multiple_of(core * depth, 64), depth)
    number = 0
    for chunk in range(chunks):
        for which, first, cols, place in chunk_sources(core, chunk):
            copy = pltpu.make_async_copy(
                weights[which].at[:, pl.ds(first, cols)],
                w_buf.at[chunk, rows, pl.ds(place, cols)],
                w_loc.at[number],
            )
            copy.start()
            locals_.append((chunk, copy))
            number += 1

    def columns_of(chip):
        return pl.ds(pl.multiple_of(chip * width, HEAD), width)

    relations = (dn, xn, yn)
    pl.semaphore_wait(barrier, 4 + tops - 1)

    def send_raw(index):
        peer = relations[index]
        source = hidden.at[0, :, columns_of(peer // 2)]
        launch(source, x_raw.at[index], x_snd.at[index], x_rcv.at[index], peer, z)

    send_raw(1)
    send_raw(2)

    def send_weights(wanted):
        number = 0
        for chunk in range(chunks):
            for which, first, cols, place in chunk_sources(1 - core, chunk):
                if chunk in wanted:
                    launch(
                        weights[which].at[:, pl.ds(first, cols)],
                        w_buf.at[chunk, rows, pl.ds(place, cols)],
                        w_snd.at[number],
                        w_rcv.at[number],
                        sibling,
                        z,
                    )
                number += 1

    row = lax.broadcasted_iota(jnp.int32, (BLOCK, BLOCK), 0)
    column = lax.broadcasted_iota(jnp.int32, (BLOCK, BLOCK), 1)
    read.wait()
    floats = raw[...].astype(jnp.float32)
    scale = lax.rsqrt(jnp.mean(floats * floats, axis=-1, keepdims=True) + EPSILON)
    across = jnp.sum(jnp.where(row == column, scale, 0.0), axis=0, keepdims=True)
    scale_out[...] = jnp.broadcast_to(across, scale_out.shape)
    for index in (1, 2, 0):
        launch(scale_out, scale_in.at[index], c_snd.at[index], c_rcv.at[index], relations[index], z)
    send_raw(0)
    smalls[0].wait()
    gains[...] = gain[...].astype(jnp.float32).reshape(1, -1)
    here = columns_of(me // 2)
    x_buf[me] = (raw[:, here].astype(jnp.float32) * scale * gains[:, here]).astype(jnp.bfloat16)
    launch(x_buf.at[me], x_buf.at[me], f_snd.at[3], f_rcv.at[3], sibling, z)

    send_weights((0, 1, 2))
    for copy in smalls[1:]:
        copy.wait()
    for h in range(GROUP):
        for b in range(tops):
            blocks = kv_blocks[h, b : b + 1, :]
            count = block_counts[h : h + 1, b : b + 1]
            origin = lax.broadcasted_iota(jnp.int32, (tops, HEAD), 0)
            seen = jnp.zeros((tops, HEAD), jnp.float32)
            for slot in range(1, MAXB):
                hit = (blocks[:, slot : slot + 1] == origin) & (count > slot)
                seen = jnp.where(hit, 1.0, seen)
            allowed[b, h * tops : (h + 1) * tops, :] = seen
    for step in range(1, tops):
        peer = lax.rem(z + step, tops)
        launch(allowed.at[peer], mask_buf.at[z], m_snd.at[step - 1], m_rcv.at[step - 1], me, peer)
    mask_buf[z] = allowed[z]

    lane = lax.broadcasted_iota(jnp.int32, (BLOCK, HEAD), 1)
    token = lax.broadcasted_iota(jnp.int32, (BLOCK, HEAD), 0) + z * BLOCK
    exponent = lax.rem(lane, HEAD // 2).astype(jnp.float32) * (2.0 / HEAD)
    angles = token.astype(jnp.float32) * jnp.exp(exponent * (-math.log(THETA)))
    cosine[...] = jnp.cos(angles)
    sine[...] = jnp.where(lane < HEAD // 2, -jnp.sin(angles), jnp.sin(angles))
    starts = []
    for vector in (bias_query, bias_key, bias_value):
        first = starts[-1][1] if starts else 0
        starts.append((first, first + vector.shape[0]))
        biases[:, first : first + vector.shape[0]] = vector[...].astype(jnp.float32).reshape(1, -1)

    def bias_of(chunk):
        return jnp.concatenate(
            [
                biases[:, pl.ds(pl.multiple_of(starts[which][0] + first, HEAD), cols)]
                for which, first, cols, _ in chunk_sources(core, chunk)
            ],
            axis=1,
        )

    def sibling_of(device):
        return device + 1 - 2 * core

    def docs_of(index):
        peer = relations[index]
        remote(scale_out, scale_in.at[index], c_snd.at[index], c_rcv.at[index], peer, z).wait_recv()
        across = jnp.broadcast_to(scale_in[index, 0:1], (BLOCK, BLOCK))
        scale = jnp.sum(jnp.where(row == column, across, 0.0), axis=1, keepdims=True)
        remote(x_raw.at[index], x_raw.at[index], x_snd.at[index], x_rcv.at[index], peer, z).wait_recv()
        x_buf[peer] = (
            x_raw[index].astype(jnp.float32) * scale * gains[:, columns_of(me // 2)]
        ).astype(jnp.bfloat16)
        launch(x_buf.at[peer], x_buf.at[peer], f_snd.at[index], f_rcv.at[index], sibling, z)

    def forwarded(index, device):
        there = x_buf.at[sibling_of(device)]
        remote(there, there, f_snd.at[index], f_rcv.at[index], sibling, z).wait_recv()

    def wait_weights(chunk):
        other = pl.ds(pl.multiple_of((1 - core) * depth, 64), depth)
        for number, (owner, copy) in enumerate(locals_):
            if owner == chunk:
                copy.wait()
        number = 0
        for at in range(chunks):
            for _, _, cols, place in chunk_sources(core, at):
                if at == chunk:
                    there = w_buf.at[chunk, other, pl.ds(place, cols)]
                    remote(there, there, w_snd.at[number], w_rcv.at[number], sibling, z).wait_recv()
                number += 1

    def product(chunk, device):
        pair = x_buf[pl.ds(device // 2 * 2, 2)].reshape(2 * BLOCK, width)
        return jnp.dot(pair, w_buf[chunk], preferred_element_type=jnp.float32)

    def first_x(chunk):
        to_x = product(chunk, xn)
        a1_out[chunk, 0] = to_x[:BLOCK].astype(jnp.bfloat16)
        keep[chunk, 1] = to_x[BLOCK:]

    def first_y(chunk):
        to_y = product(chunk, yn)
        b1_out[chunk, 0] = to_y[BLOCK:].astype(jnp.bfloat16)
        keep[chunk, 0] = to_y[:BLOCK]

    def first_d(chunk):
        to_d = product(chunk, dn).astype(jnp.bfloat16)
        a1_out[chunk, 1] = to_d[:BLOCK]
        b1_out[chunk, 1] = to_d[BLOCK:]

    def first_own(chunk):
        mine = product(chunk, me)
        own[chunk, 0] = mine[:BLOCK]
        own[chunk, 1] = mine[BLOCK:]

    def send_first(chunk, piece):
        first_copy(0, piece, chunk).start()
        first_copy(1, piece, chunk).start()

    def first_copy(doc, piece, chunk):
        there, back = ((a1_out, a1_in), (b1_out, b1_in))[doc]
        return remote(
            there.at[chunk, piece],
            back.at[chunk, piece],
            s1_snd.at[doc, piece, chunk],
            s1_rcv.at[doc, piece, chunk],
            (xn, yn)[doc],
            z,
        )

    def multiply(chunk):
        first_d(chunk)
        first_x(chunk)
        first_y(chunk)
        first_own(chunk)

    def second(chunk):
        first_copy(0, 1, chunk).wait_recv()
        a2_out[chunk] = (keep[chunk, 0] + a1_in[chunk, 1].astype(jnp.float32)).astype(jnp.bfloat16)
        launch(a2_out.at[chunk], a2_in.at[chunk], s2_snd.at[0, chunk], s2_rcv.at[0, chunk], yn, z)
        first_copy(1, 1, chunk).wait_recv()
        b2_out[chunk] = (keep[chunk, 1] + b1_in[chunk, 1].astype(jnp.float32)).astype(jnp.bfloat16)
        launch(b2_out.at[chunk], b2_in.at[chunk], s2_snd.at[1, chunk], s2_rcv.at[1, chunk], xn, z)

    def rotate(head):
        return (head * cosine[...] + pltpu.roll(head, HEAD // 2, 1) * sine[...]).astype(jnp.bfloat16)

    def kv_copy(pair, origin):
        place = kv_buf.at[origin, pair]
        return remote(place, place, kv_snd.at[pair, origin], kv_rcv.at[pair, origin], me, lax.rem(z + 1, tops))

    def finish(chunk):
        both = ((a1_in, a2_in, a2_out, yn), (b1_in, b2_in, b2_out, xn))
        bias = bias_of(chunk)
        for doc, (first_in, second_in, second_out, peer) in enumerate(both):
            first_copy(doc, 0, chunk).wait_recv()
            remote(
                second_out.at[chunk], second_in.at[chunk], s2_snd.at[doc, chunk], s2_rcv.at[doc, chunk], peer, z
            ).wait_recv()
            total = (
                own[chunk, doc]
                + first_in[chunk, 0].astype(jnp.float32)
                + second_in[chunk].astype(jnp.float32)
                + bias
            )
            if chunk < PAIRS:
                kv_buf[z, chunk, doc, :, :HEAD] = rotate(total[:, :HEAD])
                kv_buf[z, chunk, doc, :, HEAD:] = total[:, HEAD:].astype(jnp.bfloat16)
            else:
                head = (chunk - PAIRS) * 2
                q_buf[doc, head] = rotate(total[:, :HEAD])
                q_buf[doc, head + 1] = rotate(total[:, HEAD:])
        if chunk < PAIRS:

            @pl.when(z < tops - 1)
            def _():
                kv_copy(chunk, z).start()

    def pass_on(pair, step):
        @pl.when(z >= step)
        def _():
            kv_copy(pair, z - step).wait_recv()

            @pl.when(z < tops - 1)
            def _():
                kv_copy(pair, z - step).start()

    def scores_of(queries, keys):
        return lax.dot_general(
            queries, keys, (((1,), (1,)), ((), ())), preferred_element_type=jnp.float32
        ) * HEAD ** (-0.5)

    causal = jnp.concatenate([column <= row] * 2, axis=0)

    def attend_own(chunk):
        at = chunk - PAIRS
        for doc in range(2):
            queries = q_buf[doc, 2 * at : 2 * at + 2].reshape(2 * BLOCK, HEAD)
            block = kv_buf[z, at // 2, doc]
            expo = jnp.where(causal, jnp.exp(scores_of(queries, block[:, :HEAD])), 0.0)
            tot[at, doc] = expo
            acc[at, doc] = jnp.dot(
                expo.astype(jnp.bfloat16), block[:, HEAD:], preferred_element_type=jnp.float32
            )

    def attend_below(chunk, step):
        at = chunk - PAIRS

        @pl.when(z >= step)
        def _():
            origin = z - step
            rows_of = [
                mask_buf[PAIRS * core + at // 2, pl.ds((at % 2 * 2 + h) * tops + origin, 1)]
                for h in range(2)
            ]
            seen = jnp.concatenate([jnp.broadcast_to(r, (BLOCK, BLOCK)) for r in rows_of], axis=0)
            for doc in range(2):
                queries = q_buf[doc, 2 * at : 2 * at + 2].reshape(2 * BLOCK, HEAD)
                block = kv_buf[origin, at // 2, doc]
                expo = jnp.where(seen > 0.5, jnp.exp(scores_of(queries, block[:, :HEAD])), 0.0)
                tot[at, doc] += expo
                acc[at, doc] += jnp.dot(
                    expo.astype(jnp.bfloat16), block[:, HEAD:], preferred_element_type=jnp.float32
                )

    def attend_end(chunk):
        at = chunk - PAIRS
        for doc in range(2):
            mixed = (acc[at, doc] / jnp.sum(tot[at, doc], axis=-1, keepdims=True)).astype(jnp.bfloat16)
            o_buf[doc, at, :, :HEAD] = mixed[:BLOCK]
            o_buf[doc, at, :, HEAD:] = mixed[BLOCK:]
        launch(o_buf.at[1 - core, at], o_in.at[at], o_snd.at[at], o_rcv.at[at], sibling, z)

    for chunk in range(3):
        wait_weights(chunk)
    forwarded(3, me)
    docs_of(1)
    docs_of(2)
    forwarded(1, xn)
    for chunk in range(2):
        first_x(chunk)
        first_copy(0, 0, chunk).start()
    forwarded(2, yn)
    for chunk in range(2):
        first_y(chunk)
        first_copy(1, 0, chunk).start()
    first_x(2)
    first_y(2)
    docs_of(0)
    send_weights(range(3, chunks))
    first_own(0)
    forwarded(0, dn)
    for chunk in range(2):
        first_d(chunk)
        send_first(chunk, 1)
    first_own(1)
    second(0)
    send_first(2, 0)
    first_d(2)
    for chunk in range(3, chunks):
        wait_weights(chunk)
    second(1)
    send_first(2, 1)
    first_own(2)
    finish(0)
    multiply(3)
    send_first(3, 1)
    send_first(3, 0)
    finish(1)
    multiply(4)
    second(2)
    send_first(4, 1)
    send_first(4, 0)
    pass_on(0, 1)
    multiply(5)
    for step in range(1, tops):
        here = mask_buf.at[lax.rem(z - step + tops, tops)]
        remote(here, here, m_snd.at[step - 1], m_rcv.at[step - 1], me, z).wait_recv()
    second(3)
    send_first(5, 1)
    send_first(5, 0)
    pass_on(1, 1)
    finish(2)
    attend_own(2)
    attend_below(2, 1)
    pass_on(0, 2)
    attend_below(2, 2)
    second(4)
    finish(3)
    attend_own(3)
    attend_below(3, 1)
    pass_on(1, 2)
    attend_below(3, 2)
    second(5)
    pass_on(0, 3)
    attend_below(2, 3)
    attend_end(2)
    attend_below(3, 3)
    attend_end(3)
    finish(4)
    attend_own(4)
    attend_below(4, 1)
    attend_below(4, 2)
    pass_on(1, 3)
    attend_below(4, 3)
    attend_end(4)
    finish(5)
    attend_own(5)
    attend_below(5, 1)
    attend_below(5, 2)
    attend_below(5, 3)
    attend_end(5)

    half = QHEADS // 2 * HEAD
    for at in range(chunks - PAIRS):
        first = pl.multiple_of(core * half + at * CHUNK, CHUNK)
        out[0, :, pl.ds(first, CHUNK)] = o_buf[core, at]
    for at in range(chunks - PAIRS):
        first = pl.multiple_of((1 - core) * half + at * CHUNK, CHUNK)
        remote(o_buf.at[core, at], o_in.at[at], o_snd.at[at], o_rcv.at[at], sibling, z).wait_recv()
        out[0, :, pl.ds(first, CHUNK)] = o_in[at]
    for doc in range(2):
        for piece in range(2):
            for chunk in range(chunks):
                first_copy(doc, piece, chunk).wait_send()
    for copy in sends:
        copy.wait_send()
    for pair in range(PAIRS):
        for step in range(tops):

            @pl.when((z >= step) & (z < tops - 1))
            def _():
                kv_copy(pair, z - step).wait_send()


def fused_body(
    hidden,
    norm_gain,
    w_query,
    w_key,
    w_value,
    bias_query,
    bias_key,
    bias_value,
    kv_blocks,
    block_counts,
):
    tops = lax.axis_size("ctx")
    rows = hidden.shape[1]
    depth = w_query.shape[0]
    chunks = PAIRS + QHEADS // 4
    bf16, f32 = jnp.bfloat16, jnp.float32
    vmem = pl.BlockSpec(memory_space=pltpu.VMEM)
    hbm = pl.BlockSpec(memory_space=pl.ANY)
    dma = pltpu.SemaphoreType.DMA
    copies = 2 * PAIRS + chunks - PAIRS
    return pl.pallas_call(
        fused_kernel,
        out_shape=pltpu.VMEM((1, rows, QHEADS * HEAD), bf16),
        in_specs=[hbm] * 10,
        out_specs=vmem,
        scratch_shapes=[
            pltpu.VMEM(norm_gain.shape, bf16),
            pltpu.VMEM(bias_query.shape, bf16),
            pltpu.VMEM(bias_key.shape, bf16),
            pltpu.VMEM(bias_value.shape, bf16),
            pltpu.VMEM(kv_blocks.shape, jnp.int32),
            pltpu.VMEM(block_counts.shape, jnp.int32),
            pltpu.VMEM((rows, hidden.shape[2]), bf16),
            pltpu.VMEM((3, rows, 2 * depth), bf16),
            pltpu.VMEM((8, rows), f32),
            pltpu.VMEM((3, 8, rows), f32),
            pltpu.VMEM((1, hidden.shape[2]), f32),
            pltpu.VMEM((1, (QHEADS + 2 * KVH) * HEAD), f32),
            pltpu.VMEM((rows, HEAD), f32),
            pltpu.VMEM((rows, HEAD), f32),
            pltpu.VMEM((tops, GROUP * tops, HEAD), f32),
            pltpu.VMEM((8, rows, 2 * depth), bf16),
            pltpu.VMEM((chunks, 2 * depth, CHUNK), bf16),
            pltpu.VMEM((chunks, 2, rows, CHUNK), bf16),
            pltpu.VMEM((chunks, 2, rows, CHUNK), bf16),
            pltpu.VMEM((chunks, 2, rows, CHUNK), bf16),
            pltpu.VMEM((chunks, 2, rows, CHUNK), bf16),
            pltpu.VMEM((chunks, rows, CHUNK), bf16),
            pltpu.VMEM((chunks, rows, CHUNK), bf16),
            pltpu.VMEM((chunks, rows, CHUNK), bf16),
            pltpu.VMEM((chunks, rows, CHUNK), bf16),
            pltpu.VMEM((chunks, 2, rows, CHUNK), f32),
            pltpu.VMEM((chunks, 2, rows, CHUNK), f32),
            pltpu.VMEM((tops, PAIRS, 2, rows, CHUNK), bf16),
            pltpu.VMEM((2, QHEADS // 2, rows, HEAD), bf16),
            pltpu.VMEM((tops, GROUP * tops, HEAD), f32),
            pltpu.VMEM((chunks - PAIRS, 2, 2 * rows, HEAD), f32),
            pltpu.VMEM((chunks - PAIRS, 2, 2 * rows, HEAD), f32),
            pltpu.VMEM((2, chunks - PAIRS, rows, CHUNK), bf16),
            pltpu.VMEM((chunks - PAIRS, rows, CHUNK), bf16),
            dma,
            dma((6,)),
            dma((3,)),
            dma((3,)),
            dma((copies,)),
            dma((copies,)),
            dma((copies,)),
            dma((3,)),
            dma((3,)),
            dma((4,)),
            dma((4,)),
            dma((tops - 1,)),
            dma((tops - 1,)),
            dma((2, 2, chunks)),
            dma((2, 2, chunks)),
            dma((2, chunks)),
            dma((2, chunks)),
            dma((PAIRS, tops)),
            dma((PAIRS, tops)),
            dma((chunks - PAIRS,)),
            dma((chunks - PAIRS,)),
        ],
        compiler_params=pltpu.CompilerParams(
            collective_id=0, has_side_effects=True, vmem_limit_bytes=56 * 1024 * 1024
        ),
    )(
        hidden,
        norm_gain,
        w_query,
        w_key,
        w_value,
        bias_query,
        bias_key,
        bias_value,
        kv_blocks,
        block_counts,
    )


def solution(mesh):
    placed = (
        P("dp", "ctx", None),
        P(),
        P("dp", None),
        P("dp", None),
        P("dp", None),
        P(),
        P(),
        P(),
        P("ctx", None, None),
        P("ctx", None),
    )
    plane = mesh.shape["dp"] == 8 and mesh.shape["ctx"] == MAXB
    return jax.shard_map(
        fused_body if plane else body, mesh=mesh, in_specs=placed, out_specs=P("dp", "ctx", None), check_vma=False
    )
```

```python
import math

import jax
import jax.numpy as jnp
from jax import lax
from jax.experimental import pallas as pl
from jax.experimental.pallas import tpu as pltpu
from jax.sharding import PartitionSpec as P

KVH = 4
HEAD = 128
QHEADS = 16
BLOCK = 128
MAXB = 4


EPSILON = 1e-06
THETA = 1000000.0


def rms_norm(tokens, norm_gain):
    floats = tokens.astype(jnp.float32)
    meansq = jnp.mean(floats * floats, axis=-1, keepdims=True)
    return (floats * lax.rsqrt(meansq + EPSILON) * norm_gain.astype(jnp.float32)).astype(
        jnp.bfloat16
    )


def rotary(heads_in, position):
    half_size = heads_in.shape[-1] // 2
    exponent = jnp.arange(half_size, dtype=jnp.float32) * (2.0 / heads_in.shape[-1])
    inverse = jnp.power(jnp.float32(THETA), -exponent)
    angles = position[:, None] * inverse[None, :]
    cosine = jnp.cos(angles)[:, None, :]
    sine = jnp.sin(angles)[:, None, :]
    first = heads_in[..., :half_size]
    second = heads_in[..., half_size:]
    return jnp.concatenate(
        [first * cosine - second * sine, second * cosine + first * sine], axis=-1
    )


def finish_heads(summed, bias, heads, position, rotate_it):
    shaped = (summed + bias.astype(jnp.float32)).reshape(summed.shape[0], heads, HEAD)
    if rotate_it:
        shaped = rotary(shaped, position)
    return shaped.astype(jnp.bfloat16)


def fold_rows(source, pieces):
    return tuple((jnp.dot(source, piece, preferred_element_type=jnp.float32) for piece in pieces))


def sparse_head(queries, key_rows, value_rows, blocks, counts):
    nblocks = queries.shape[0] // BLOCK
    query_tiles = queries.reshape(nblocks, BLOCK, HEAD)
    key_tiles = key_rows.reshape(nblocks, BLOCK, HEAD)[blocks].reshape(nblocks, MAXB * BLOCK, HEAD)
    value_tiles = value_rows.reshape(nblocks, BLOCK, HEAD)[blocks].reshape(
        nblocks, MAXB * BLOCK, HEAD
    )
    scores = jnp.einsum(
        "qih,qjh->qij", query_tiles, key_tiles, preferred_element_type=jnp.float32
    ) * HEAD ** (-0.5)
    column = jnp.arange(MAXB * BLOCK)
    slot_of = column // BLOCK
    inside = column % BLOCK
    row_pos = jnp.arange(BLOCK)
    allowed = (slot_of[None, None, :] < counts[:, None, None]) & (
        (slot_of[None, None, :] > 0) | (inside[None, None, :] <= row_pos[None, :, None])
    )
    expo = jnp.where(allowed, jnp.exp(scores), jnp.float32(0.0))
    totals = jnp.sum(expo, axis=-1)
    probs = expo.astype(jnp.bfloat16)
    mixed = (
        jnp.einsum("qij,qjh->qih", probs, value_tiles, preferred_element_type=jnp.float32)
        / totals[..., None]
    )
    return mixed.astype(jnp.bfloat16).reshape(nblocks * BLOCK, HEAD)


def one_head(packed):
    return sparse_head(packed[0], packed[1], packed[2], packed[3], packed[4])


def body(
    hidden,
    norm_gain,
    w_query,
    w_key,
    w_value,
    bias_query,
    bias_key,
    bias_value,
    kv_blocks,
    block_counts,
):
    groups = lax.axis_size("ctx")
    device = lax.axis_index("ctx")
    tokens = hidden[0]
    local_rows = tokens.shape[0]
    seq_len = local_rows * groups
    heads_here = QHEADS // groups
    kv_here = KVH // groups
    width_query = heads_here * HEAD
    width_pair = kv_here * HEAD
    normed = rms_norm(tokens, norm_gain)
    parts = lax.axis_size("dp")
    depth = w_query.shape[0]
    gathered = lax.all_to_all(
        normed.reshape(local_rows, parts, depth), "dp", split_axis=1, concat_axis=0, tiled=True
    ).reshape(parts * local_rows, depth)
    weights = jnp.concatenate([w_key, w_value, w_query], axis=1)
    partial = jnp.dot(gathered, weights, preferred_element_type=jnp.float32).astype(jnp.bfloat16)
    summed = lax.psum_scatter(partial, "dp", scatter_dimension=0, tiled=True).astype(jnp.float32)
    width = KVH * HEAD
    sum_key, sum_value, sum_query = (
        summed[:, :width],
        summed[:, width : 2 * width],
        summed[:, 2 * width :],
    )
    position = (device * local_rows + jnp.arange(local_rows, dtype=jnp.int32)).astype(jnp.float32)
    queries = finish_heads(sum_query, bias_query, QHEADS, position, True)
    key_rows = finish_heads(sum_key, bias_key, KVH, position, True)
    value_rows = finish_heads(sum_value, bias_value, KVH, position, False)
    query_send = queries.reshape(local_rows, groups, width_query)
    pair_send = jnp.concatenate([key_rows, value_rows], axis=2)
    query_got, pair_got = (
        lax.all_to_all(query_send, "ctx", split_axis=1, concat_axis=0, tiled=True),
        lax.all_to_all(pair_send, "ctx", split_axis=1, concat_axis=0, tiled=True),
    )
    queries = query_got.reshape(seq_len, heads_here, HEAD)
    key_rows = pair_got[:, 0, :width_pair].reshape(seq_len, kv_here, HEAD)
    value_rows = pair_got[:, 0, width_pair:].reshape(seq_len, kv_here, HEAD)
    group = heads_here // kv_here
    key_rows = jnp.repeat(key_rows, group, axis=1)
    value_rows = jnp.repeat(value_rows, group, axis=1)
    mixed = lax.map(
        one_head,
        (
            queries.transpose(1, 0, 2),
            key_rows.transpose(1, 0, 2),
            value_rows.transpose(1, 0, 2),
            kv_blocks,
            block_counts,
        ),
    )
    result = mixed.transpose(1, 0, 2).reshape(seq_len, 1, width_query)
    returned = lax.all_to_all(result, "ctx", split_axis=0, concat_axis=1, tiled=True)
    return returned.reshape(1, local_rows, QHEADS * HEAD)


MESH = pl.DeviceIdType.MESH
CHUNK = 2 * HEAD
GROUP = QHEADS // KVH
PAIRS = KVH // 2


def chunk_sources(half, chunk):
    if chunk < PAIRS:
        first = pl.multiple_of((PAIRS * half + chunk) * HEAD, HEAD)
        return ((1, first, HEAD, 0), (2, first, HEAD, HEAD))
    first = half * (QHEADS // 2 * HEAD) + (chunk - PAIRS) * CHUNK
    return ((0, pl.multiple_of(first, CHUNK), CHUNK, 0),)


def fused_kernel(
    hidden,
    gain_hbm,
    w_query,
    w_key,
    w_value,
    bias_query_hbm,
    bias_key_hbm,
    bias_value_hbm,
    kv_blocks_hbm,
    block_counts_hbm,
    out,
    gain,
    bias_query,
    bias_key,
    bias_value,
    kv_blocks,
    block_counts,
    raw,
    x_raw,
    scale_out,
    scale_in,
    gains,
    biases,
    cosine,
    sine,
    allowed,
    x_buf,
    w_buf,
    a1_out,
    a1_in,
    b1_out,
    b1_in,
    a2_out,
    a2_in,
    b2_out,
    b2_in,
    keep,
    own,
    kv_buf,
    q_buf,
    mask_buf,
    acc,
    tot,
    o_buf,
    o_in,
    h_sem,
    v_sem,
    c_snd,
    c_rcv,
    w_loc,
    w_snd,
    w_rcv,
    x_snd,
    x_rcv,
    f_snd,
    f_rcv,
    m_snd,
    m_rcv,
    s1_snd,
    s1_rcv,
    s2_snd,
    s2_rcv,
    kv_snd,
    kv_rcv,
    o_snd,
    o_rcv,
):
    me = lax.axis_index("dp")
    z = lax.axis_index("ctx")
    tops = lax.axis_size("ctx")
    core = lax.rem(me, 2)
    xpos = lax.rem(me // 2, 2)
    ypos = me // 4
    sibling = me + 1 - 2 * core
    xn = me + 2 - 4 * xpos
    yn = me + 4 - 8 * ypos
    dn = xn + 4 - 8 * ypos
    chunks = w_buf.shape[0]
    depth = w_query.shape[0]
    width = 2 * depth
    weights = (w_query, w_key, w_value)
    sends = []

    read = pltpu.make_async_copy(hidden.at[0], raw, h_sem)
    read.start()
    smalls = []
    for number, (source, place) in enumerate(
        (
            (gain_hbm, gain),
            (kv_blocks_hbm, kv_blocks),
            (block_counts_hbm, block_counts),
            (bias_query_hbm, bias_query),
            (bias_key_hbm, bias_key),
            (bias_value_hbm, bias_value),
        )
    ):
        smalls.append(pltpu.make_async_copy(source, place, v_sem.at[number]))
        smalls[-1].start()
    barrier = pltpu.get_barrier_semaphore()
    for peer in (sibling, xn, yn, dn):
        pl.semaphore_signal(barrier, inc=1, device_id=(peer, z), device_id_type=MESH)
    for step in range(1, tops):
        pl.semaphore_signal(barrier, inc=1, device_id=(me, lax.rem(z + step, tops)), device_id_type=MESH)

    def remote(src, dst, snd, rcv, dp, ctx):
        return pltpu.make_async_remote_copy(
            src_ref=src, dst_ref=dst, send_sem=snd, recv_sem=rcv, device_id=(dp, ctx), device_id_type=MESH
        )

    def launch(*args):
        copy = remote(*args)
        copy.start()
        sends.append(copy)

    locals_ = []
    rows = pl.ds(pl.multiple_of(core * depth, 64), depth)
    number = 0
    for chunk in range(chunks):
        for which, first, cols, place in chunk_sources(core, chunk):
            copy = pltpu.make_async_copy(
                weights[which].at[:, pl.ds(first, cols)],
                w_buf.at[chunk, rows, pl.ds(place, cols)],
                w_loc.at[number],
            )
            copy.start()
            locals_.append((chunk, copy))
            number += 1

    def columns_of(chip):
        return pl.ds(pl.multiple_of(chip * width, HEAD), width)

    relations = (dn, xn, yn)
    pl.semaphore_wait(barrier, 4 + tops - 1)

    def send_raw(index):
        peer = relations[index]
        source = hidden.at[0, :, columns_of(peer // 2)]
        launch(source, x_raw.at[index], x_snd.at[index], x_rcv.at[index], peer, z)

    send_raw(1)
    send_raw(2)

    def send_weights(wanted):
        number = 0
        for chunk in range(chunks):
            for which, first, cols, place in chunk_sources(1 - core, chunk):
                if chunk in wanted:
                    launch(
                        weights[which].at[:, pl.ds(first, cols)],
                        w_buf.at[chunk, rows, pl.ds(place, cols)],
                        w_snd.at[number],
                        w_rcv.at[number],
                        sibling,
                        z,
                    )
                number += 1

    row = lax.broadcasted_iota(jnp.int32, (BLOCK, BLOCK), 0)
    column = lax.broadcasted_iota(jnp.int32, (BLOCK, BLOCK), 1)
    read.wait()
    floats = raw[...].astype(jnp.float32)
    scale = lax.rsqrt(jnp.mean(floats * floats, axis=-1, keepdims=True) + EPSILON)
    across = jnp.sum(jnp.where(row == column, scale, 0.0), axis=0, keepdims=True)
    scale_out[...] = jnp.broadcast_to(across, scale_out.shape)
    for index in (1, 2, 0):
        launch(scale_out, scale_in.at[index], c_snd.at[index], c_rcv.at[index], relations[index], z)
    send_raw(0)
    smalls[0].wait()
    gains[...] = gain[...].astype(jnp.float32).reshape(1, -1)
    here = columns_of(me // 2)
    x_buf[me] = (raw[:, here].astype(jnp.float32) * scale * gains[:, here]).astype(jnp.bfloat16)
    launch(x_buf.at[me], x_buf.at[me], f_snd.at[3], f_rcv.at[3], sibling, z)

    send_weights((0, 1, 2))
    for copy in smalls[1:]:
        copy.wait()
    for h in range(GROUP):
        for b in range(tops):
            blocks = kv_blocks[h, b : b + 1, :]
            count = block_counts[h : h + 1, b : b + 1]
            origin = lax.broadcasted_iota(jnp.int32, (tops, HEAD), 0)
            seen = jnp.zeros((tops, HEAD), jnp.float32)
            for slot in range(1, MAXB):
                hit = (blocks[:, slot : slot + 1] == origin) & (count > slot)
                seen = jnp.where(hit, 1.0, seen)
            allowed[b, h * tops : (h + 1) * tops, :] = seen
    for step in range(1, tops):
        peer = lax.rem(z + step, tops)
        launch(allowed.at[peer], mask_buf.at[z], m_snd.at[step - 1], m_rcv.at[step - 1], me, peer)
    mask_buf[z] = allowed[z]

    lane = lax.broadcasted_iota(jnp.int32, (BLOCK, HEAD), 1)
    token = lax.broadcasted_iota(jnp.int32, (BLOCK, HEAD), 0) + z * BLOCK
    exponent = lax.rem(lane, HEAD // 2).astype(jnp.float32) * (2.0 / HEAD)
    angles = token.astype(jnp.float32) * jnp.exp(exponent * (-math.log(THETA)))
    cosine[...] = jnp.cos(angles)
    sine[...] = jnp.where(lane < HEAD // 2, -jnp.sin(angles), jnp.sin(angles))
    starts = []
    for vector in (bias_query, bias_key, bias_value):
        first = starts[-1][1] if starts else 0
        starts.append((first, first + vector.shape[0]))
        biases[:, first : first + vector.shape[0]] = vector[...].astype(jnp.float32).reshape(1, -1)

    def bias_of(chunk):
        return jnp.concatenate(
            [
                biases[:, pl.ds(pl.multiple_of(starts[which][0] + first, HEAD), cols)]
                for which, first, cols, _ in chunk_sources(core, chunk)
            ],
            axis=1,
        )

    def sibling_of(device):
        return device + 1 - 2 * core

    def docs_of(index):
        peer = relations[index]
        remote(scale_out, scale_in.at[index], c_snd.at[index], c_rcv.at[index], peer, z).wait_recv()
        across = jnp.broadcast_to(scale_in[index, 0:1], (BLOCK, BLOCK))
        scale = jnp.sum(jnp.where(row == column, across, 0.0), axis=1, keepdims=True)
        remote(x_raw.at[index], x_raw.at[index], x_snd.at[index], x_rcv.at[index], peer, z).wait_recv()
        x_buf[peer] = (
            x_raw[index].astype(jnp.float32) * scale * gains[:, columns_of(me // 2)]
        ).astype(jnp.bfloat16)
        launch(x_buf.at[peer], x_buf.at[peer], f_snd.at[index], f_rcv.at[index], sibling, z)

    def forwarded(index, device):
        there = x_buf.at[sibling_of(device)]
        remote(there, there, f_snd.at[index], f_rcv.at[index], sibling, z).wait_recv()

    def wait_weights(chunk):
        other = pl.ds(pl.multiple_of((1 - core) * depth, 64), depth)
        for number, (owner, copy) in enumerate(locals_):
            if owner == chunk:
                copy.wait()
        number = 0
        for at in range(chunks):
            for _, _, cols, place in chunk_sources(core, at):
                if at == chunk:
                    there = w_buf.at[chunk, other, pl.ds(place, cols)]
                    remote(there, there, w_snd.at[number], w_rcv.at[number], sibling, z).wait_recv()
                number += 1

    def product(chunk, device):
        pair = x_buf[pl.ds(device // 2 * 2, 2)].reshape(2 * BLOCK, width)
        return jnp.dot(pair, w_buf[chunk], preferred_element_type=jnp.float32)

    def first_x(chunk):
        to_x = product(chunk, xn)
        a1_out[chunk, 0] = to_x[:BLOCK].astype(jnp.bfloat16)
        keep[chunk, 1] = to_x[BLOCK:]

    def first_y(chunk):
        to_y = product(chunk, yn)
        b1_out[chunk, 0] = to_y[BLOCK:].astype(jnp.bfloat16)
        keep[chunk, 0] = to_y[:BLOCK]

    def first_d(chunk):
        to_d = product(chunk, dn).astype(jnp.bfloat16)
        a1_out[chunk, 1] = to_d[:BLOCK]
        b1_out[chunk, 1] = to_d[BLOCK:]

    def first_own(chunk):
        mine = product(chunk, me)
        own[chunk, 0] = mine[:BLOCK]
        own[chunk, 1] = mine[BLOCK:]

    def send_first(chunk, piece):
        first_copy(0, piece, chunk).start()
        first_copy(1, piece, chunk).start()

    def first_copy(doc, piece, chunk):
        there, back = ((a1_out, a1_in), (b1_out, b1_in))[doc]
        return remote(
            there.at[chunk, piece],
            back.at[chunk, piece],
            s1_snd.at[doc, piece, chunk],
            s1_rcv.at[doc, piece, chunk],
            (xn, yn)[doc],
            z,
        )

    def multiply(chunk):
        first_d(chunk)
        first_x(chunk)
        first_y(chunk)
        first_own(chunk)

    def second(chunk):
        first_copy(0, 1, chunk).wait_recv()
        a2_out[chunk] = (keep[chunk, 0] + a1_in[chunk, 1].astype(jnp.float32)).astype(jnp.bfloat16)
        launch(a2_out.at[chunk], a2_in.at[chunk], s2_snd.at[0, chunk], s2_rcv.at[0, chunk], yn, z)
        first_copy(1, 1, chunk).wait_recv()
        b2_out[chunk] = (keep[chunk, 1] + b1_in[chunk, 1].astype(jnp.float32)).astype(jnp.bfloat16)
        launch(b2_out.at[chunk], b2_in.at[chunk], s2_snd.at[1, chunk], s2_rcv.at[1, chunk], xn, z)

    def rotate(head):
        return (head * cosine[...] + pltpu.roll(head, HEAD // 2, 1) * sine[...]).astype(jnp.bfloat16)

    def kv_copy(pair, origin):
        place = kv_buf.at[origin, pair]
        return remote(place, place, kv_snd.at[pair, origin], kv_rcv.at[pair, origin], me, lax.rem(z + 1, tops))

    def finish(chunk):
        both = ((a1_in, a2_in, a2_out, yn), (b1_in, b2_in, b2_out, xn))
        bias = bias_of(chunk)
        for doc, (first_in, second_in, second_out, peer) in enumerate(both):
            first_copy(doc, 0, chunk).wait_recv()
            remote(
                second_out.at[chunk], second_in.at[chunk], s2_snd.at[doc, chunk], s2_rcv.at[doc, chunk], peer, z
            ).wait_recv()
            total = (
                own[chunk, doc]
                + first_in[chunk, 0].astype(jnp.float32)
                + second_in[chunk].astype(jnp.float32)
                + bias
            )
            if chunk < PAIRS:
                kv_buf[z, chunk, doc, :, :HEAD] = rotate(total[:, :HEAD])
                kv_buf[z, chunk, doc, :, HEAD:] = total[:, HEAD:].astype(jnp.bfloat16)
            else:
                head = (chunk - PAIRS) * 2
                q_buf[doc, head] = rotate(total[:, :HEAD])
                q_buf[doc, head + 1] = rotate(total[:, HEAD:])
        if chunk < PAIRS:

            @pl.when(z < tops - 1)
            def _():
                kv_copy(chunk, z).start()

    def pass_on(pair, step):
        @pl.when(z >= step)
        def _():
            kv_copy(pair, z - step).wait_recv()

            @pl.when(z < tops - 1)
            def _():
                kv_copy(pair, z - step).start()

    def scores_of(queries, keys):
        return lax.dot_general(
            queries, keys, (((1,), (1,)), ((), ())), preferred_element_type=jnp.float32
        ) * HEAD ** (-0.5)

    causal = jnp.concatenate([column <= row] * 2, axis=0)

    def attend_own(chunk):
        at = chunk - PAIRS
        for doc in range(2):
            queries = q_buf[doc, 2 * at : 2 * at + 2].reshape(2 * BLOCK, HEAD)
            block = kv_buf[z, at // 2, doc]
            expo = jnp.where(causal, jnp.exp(scores_of(queries, block[:, :HEAD])), 0.0)
            tot[at, doc] = expo
            acc[at, doc] = jnp.dot(
                expo.astype(jnp.bfloat16), block[:, HEAD:], preferred_element_type=jnp.float32
            )

    def attend_below(chunk, step):
        at = chunk - PAIRS

        @pl.when(z >= step)
        def _():
            origin = z - step
            rows_of = [
                mask_buf[PAIRS * core + at // 2, pl.ds((at % 2 * 2 + h) * tops + origin, 1)]
                for h in range(2)
            ]
            seen = jnp.concatenate([jnp.broadcast_to(r, (BLOCK, BLOCK)) for r in rows_of], axis=0)
            for doc in range(2):
                queries = q_buf[doc, 2 * at : 2 * at + 2].reshape(2 * BLOCK, HEAD)
                block = kv_buf[origin, at // 2, doc]
                expo = jnp.where(seen > 0.5, jnp.exp(scores_of(queries, block[:, :HEAD])), 0.0)
                tot[at, doc] += expo
                acc[at, doc] += jnp.dot(
                    expo.astype(jnp.bfloat16), block[:, HEAD:], preferred_element_type=jnp.float32
                )

    def attend_end(chunk):
        at = chunk - PAIRS
        for doc in range(2):
            mixed = (acc[at, doc] / jnp.sum(tot[at, doc], axis=-1, keepdims=True)).astype(jnp.bfloat16)
            o_buf[doc, at, :, :HEAD] = mixed[:BLOCK]
            o_buf[doc, at, :, HEAD:] = mixed[BLOCK:]
        launch(o_buf.at[1 - core, at], o_in.at[at], o_snd.at[at], o_rcv.at[at], sibling, z)

    for chunk in range(3):
        wait_weights(chunk)
    forwarded(3, me)
    docs_of(1)
    docs_of(2)
    forwarded(1, xn)
    for chunk in range(2):
        first_x(chunk)
        first_copy(0, 0, chunk).start()
    forwarded(2, yn)
    for chunk in range(2):
        first_y(chunk)
        first_copy(1, 0, chunk).start()
    first_x(2)
    first_y(2)
    docs_of(0)
    send_weights(range(3, chunks))
    first_own(0)
    forwarded(0, dn)
    for chunk in range(2):
        first_d(chunk)
        send_first(chunk, 1)
    first_own(1)
    second(0)
    send_first(2, 0)
    first_d(2)
    for chunk in range(3, chunks):
        wait_weights(chunk)
    second(1)
    send_first(2, 1)
    finish(0)
    first_d(3)
    first_x(3)
    first_y(3)
    send_first(3, 1)
    send_first(3, 0)
    finish(1)
    first_own(2)
    first_own(3)
    multiply(4)
    second(2)
    send_first(4, 1)
    send_first(4, 0)
    pass_on(0, 1)
    multiply(5)
    for step in range(1, tops):
        here = mask_buf.at[lax.rem(z - step + tops, tops)]
        remote(here, here, m_snd.at[step - 1], m_rcv.at[step - 1], me, z).wait_recv()
    second(3)
    send_first(5, 1)
    send_first(5, 0)
    pass_on(1, 1)
    finish(2)
    attend_own(2)
    attend_below(2, 1)
    pass_on(0, 2)
    attend_below(2, 2)
    second(4)
    finish(3)
    attend_own(3)
    attend_below(3, 1)
    pass_on(1, 2)
    attend_below(3, 2)
    second(5)
    pass_on(0, 3)
    attend_below(2, 3)
    attend_end(2)
    attend_below(3, 3)
    attend_end(3)
    finish(4)
    attend_own(4)
    attend_below(4, 1)
    attend_below(4, 2)
    pass_on(1, 3)
    attend_below(4, 3)
    attend_end(4)
    finish(5)
    attend_own(5)
    attend_below(5, 1)
    attend_below(5, 2)
    attend_below(5, 3)
    attend_end(5)

    half = QHEADS // 2 * HEAD
    for at in range(chunks - PAIRS):
        first = pl.multiple_of(core * half + at * CHUNK, CHUNK)
        out[0, :, pl.ds(first, CHUNK)] = o_buf[core, at]
    for at in range(chunks - PAIRS):
        first = pl.multiple_of((1 - core) * half + at * CHUNK, CHUNK)
        remote(o_buf.at[core, at], o_in.at[at], o_snd.at[at], o_rcv.at[at], sibling, z).wait_recv()
        out[0, :, pl.ds(first, CHUNK)] = o_in[at]
    for doc in range(2):
        for piece in range(2):
            for chunk in range(chunks):
                first_copy(doc, piece, chunk).wait_send()
    for copy in sends:
        copy.wait_send()
    for pair in range(PAIRS):
        for step in range(tops):

            @pl.when((z >= step) & (z < tops - 1))
            def _():
                kv_copy(pair, z - step).wait_send()


def fused_body(
    hidden,
    norm_gain,
    w_query,
    w_key,
    w_value,
    bias_query,
    bias_key,
    bias_value,
    kv_blocks,
    block_counts,
):
    tops = lax.axis_size("ctx")
    rows = hidden.shape[1]
    depth = w_query.shape[0]
    chunks = PAIRS + QHEADS // 4
    bf16, f32 = jnp.bfloat16, jnp.float32
    vmem = pl.BlockSpec(memory_space=pltpu.VMEM)
    hbm = pl.BlockSpec(memory_space=pl.ANY)
    dma = pltpu.SemaphoreType.DMA
    copies = 2 * PAIRS + chunks - PAIRS
    return pl.pallas_call(
        fused_kernel,
        out_shape=pltpu.VMEM((1, rows, QHEADS * HEAD), bf16),
        in_specs=[hbm] * 10,
        out_specs=vmem,
        scratch_shapes=[
            pltpu.VMEM(norm_gain.shape, bf16),
            pltpu.VMEM(bias_query.shape, bf16),
            pltpu.VMEM(bias_key.shape, bf16),
            pltpu.VMEM(bias_value.shape, bf16),
            pltpu.VMEM(kv_blocks.shape, jnp.int32),
            pltpu.VMEM(block_counts.shape, jnp.int32),
            pltpu.VMEM((rows, hidden.shape[2]), bf16),
            pltpu.VMEM((3, rows, 2 * depth), bf16),
            pltpu.VMEM((8, rows), f32),
            pltpu.VMEM((3, 8, rows), f32),
            pltpu.VMEM((1, hidden.shape[2]), f32),
            pltpu.VMEM((1, (QHEADS + 2 * KVH) * HEAD), f32),
            pltpu.VMEM((rows, HEAD), f32),
            pltpu.VMEM((rows, HEAD), f32),
            pltpu.VMEM((tops, GROUP * tops, HEAD), f32),
            pltpu.VMEM((8, rows, 2 * depth), bf16),
            pltpu.VMEM((chunks, 2 * depth, CHUNK), bf16),
            pltpu.VMEM((chunks, 2, rows, CHUNK), bf16),
            pltpu.VMEM((chunks, 2, rows, CHUNK), bf16),
            pltpu.VMEM((chunks, 2, rows, CHUNK), bf16),
            pltpu.VMEM((chunks, 2, rows, CHUNK), bf16),
            pltpu.VMEM((chunks, rows, CHUNK), bf16),
            pltpu.VMEM((chunks, rows, CHUNK), bf16),
            pltpu.VMEM((chunks, rows, CHUNK), bf16),
            pltpu.VMEM((chunks, rows, CHUNK), bf16),
            pltpu.VMEM((chunks, 2, rows, CHUNK), f32),
            pltpu.VMEM((chunks, 2, rows, CHUNK), f32),
            pltpu.VMEM((tops, PAIRS, 2, rows, CHUNK), bf16),
            pltpu.VMEM((2, QHEADS // 2, rows, HEAD), bf16),
            pltpu.VMEM((tops, GROUP * tops, HEAD), f32),
            pltpu.VMEM((chunks - PAIRS, 2, 2 * rows, HEAD), f32),
            pltpu.VMEM((chunks - PAIRS, 2, 2 * rows, HEAD), f32),
            pltpu.VMEM((2, chunks - PAIRS, rows, CHUNK), bf16),
            pltpu.VMEM((chunks - PAIRS, rows, CHUNK), bf16),
            dma,
            dma((6,)),
            dma((3,)),
            dma((3,)),
            dma((copies,)),
            dma((copies,)),
            dma((copies,)),
            dma((3,)),
            dma((3,)),
            dma((4,)),
            dma((4,)),
            dma((tops - 1,)),
            dma((tops - 1,)),
            dma((2, 2, chunks)),
            dma((2, 2, chunks)),
            dma((2, chunks)),
            dma((2, chunks)),
            dma((PAIRS, tops)),
            dma((PAIRS, tops)),
            dma((chunks - PAIRS,)),
            dma((chunks - PAIRS,)),
        ],
        compiler_params=pltpu.CompilerParams(
            collective_id=0, has_side_effects=True, vmem_limit_bytes=56 * 1024 * 1024
        ),
    )(
        hidden,
        norm_gain,
        w_query,
        w_key,
        w_value,
        bias_query,
        bias_key,
        bias_value,
        kv_blocks,
        block_counts,
    )


def solution(mesh):
    placed = (
        P("dp", "ctx", None),
        P(),
        P("dp", None),
        P("dp", None),
        P("dp", None),
        P(),
        P(),
        P(),
        P("ctx", None, None),
        P("ctx", None),
    )
    plane = mesh.shape["dp"] == 8 and mesh.shape["ctx"] == MAXB
    return jax.shard_map(
        fused_body if plane else body, mesh=mesh, in_specs=placed, out_specs=P("dp", "ctx", None), check_vma=False
    )
```
